256 devices in a mesh: dom: 256 (over z, y, x, core).
Axes of the slice: x: 4, y: 4, z: 8, core: 2. Of those that a mesh axis runs over, the one named last changes fastest.
Arguments:
- modal_state: float32 [56, 9, 32768], P(None, None, 'dom'), may hold values from -6 to 6
- inv_size: float32 [32768], P('dom'), may hold values from 0.5 to 2
- time_step: float32 [], replicated, may hold values from 0.24 to 0.3
- stiffness: float32 [3, 56, 56], replicated, may hold values from -3.5 to 3.5
- star_matrices: float32 [3, 9, 9], replicated, may hold values from -1.25 to 1.25
- projection: float32 [4, 21, 56], replicated, may hold values from -0.75 to 0.75
- lifting: float32 [4, 56, 21], replicated, may hold values from -1.25 to 1.25
- upwind: float32 [9, 9], replicated, may hold values from -2 to 2
- nb_index: int32 [4, 32768], P(None, 'dom'), may hold values from 0 to 255, as said below
- nb_face: int32 [4, 32768], P(None, 'dom'), may hold values from 0 to 3
- iface_elem: int32 [8192], P('dom'), may hold values from 0 to 127
- iface_face: int32 [8192], P('dom'), may hold values from 0 to 3
- iface_counts: int32 [256], replicated, may hold values from 0 to 32
Outputs:
- updated_state: float32 [56, 9, 32768], P(None, None, 'dom')
The draws below stay inside these ranges and needn't reach their ends.
Inputs may be any that keep to these rules, and one draw needn't show every extreme that they name: nb_index - 64 is the neighbour's offset from the partition's first element; neighbours lie in the same partition or in the adjacent one of the same cluster, never beyond the first or last partition.
All inputs are finite; a program needn't handle non-finite values.
Results may differ from the reference program's by a relative error of at most 0.0001.
Values sent between devices are 32-bit elements; how exact they have to be, the bound alone decides.
No kernel may reach another device: no remote copies, remote signals or barrier semaphores. Data moves between devices by JAX's collectives and lax.ppermute only.
A program may use at most 128 MiB of HBM per device.

```python
import math
import jax
import jax.numpy as jnp
from jax import lax

MODES = 56
QTY = 9
FACE_MODES = 21
TAYLOR = 6
SUBSTEPS = 4
E_DEV = 128
BND = 64
CAP = 32
ELEMS = 32768
SLOTS = 8192
N_DOM = 256


def draw_nb_index(key, part):
    key = jax.random.fold_in(key, 11)
    key_own, key_remote, key_coin = jax.random.split(key, 3)
    total = E_DEV * N_DOM
    border = E_DEV // 2
    fine_devs = N_DOM // 3
    column = jnp.arange(total, dtype=jnp.int32)
    device = column // E_DEV
    local = column % E_DEV
    cluster = (device >= fine_devs).astype(jnp.int32)
    left_same = (device - 1 >= fine_devs).astype(jnp.int32) == cluster
    right_same = (device + 1 >= fine_devs).astype(jnp.int32) == cluster
    left_ok = (device > 0) & left_same
    right_ok = (device < N_DOM - 1) & right_same
    own_pick = border + jax.random.randint(key_own, (4, total), 0, E_DEV)
    remote_pick = jax.random.randint(key_remote, (4, total), 0, border)
    coin = jax.random.randint(key_coin, (4, total), 0, 2)
    go_left = (local < border)[None, :] & left_ok[None, :] & (coin == 1)
    go_right = (local >= E_DEV - border)[None, :] & right_ok[None, :] & (coin == 1)
    result = jnp.where(go_left, remote_pick, own_pick)
    result = jnp.where(go_right, border + E_DEV + remote_pick, result)
    face_zero = (jnp.arange(4, dtype=jnp.int32) == 0)[:, None]
    result = jnp.where(face_zero & (column == 2 * E_DEV - 1)[None, :], E_DEV + 2 * border - 1, result)
    result = jnp.where(face_zero & (column == E_DEV)[None, :], 0, result)
    return result.astype(jnp.int32)


def draw_iface_counts(key, part):
    key = jax.random.fold_in(key, 23)
    fine_devs = N_DOM // 3
    lowest = max(1, CAP // 3)
    counts = jax.random.randint(key, (N_DOM,), lowest, CAP + 1)
    rows = jnp.arange(N_DOM, dtype=jnp.int32)
    counts = jnp.where(rows < fine_devs, counts, 0)
    return counts.at[0].set(CAP).astype(jnp.int32)


def place_ends(array, stream_key, least, largest):
    longest = array.shape.index(max(array.shape))
    spots = []
    for shift in (0, 1):
        where = [jax.random.randint(jax.random.fold_in(stream_key, axis), (), 0, length) for axis, length in enumerate(array.shape)]
        where[longest] = (where[longest] + shift) % array.shape[longest]
        spots.append(tuple(where))
    return array.at[spots[0]].set(least).at[spots[1]].set(largest)


def shard_levels(key, dims, pieces, least, high):
    loudness, own = 1.0, jax.random.fold_in(key, 6)
    for axis_at, blocks in pieces:
        steps = jnp.exp(jax.random.uniform(jax.random.fold_in(own, axis_at), (blocks,), jnp.float32, least / len(pieces), high / len(pieces)))
        loudness = loudness * jnp.repeat(steps, dims[axis_at] // blocks).reshape([-1 if axis == axis_at else 1 for axis in range(len(dims))])
    return loudness


def scatter_about(own_key, dims, deviation, most, shards=(), kind=jnp.bfloat16):
    loudness = shard_levels(own_key, dims, shards, -0.22, 0.18) if shards else 1.0
    values = jax.random.normal(own_key, dims, jnp.float32) * deviation * loudness
    return jnp.minimum(jnp.maximum(values, -most), most).astype(kind)


def setup_inputs(seed: int = 0) -> dict:
    key_list = jax.random.split(jax.random.key(seed), 14)
    modal_state = scatter_about(key_list[0], (MODES, QTY, ELEMS), 1.0, 6.0, ((2, 256),), jnp.float32)
    inv_size = jnp.clip(jnp.exp(math.log(2.0) - 1.3862944 * jax.random.uniform(key_list[1], (ELEMS,), jnp.float32) ** shard_levels(key_list[1], (ELEMS,), ((0, 256),), -0.2, 0.2)), 0.5, 2.0)
    time_step = jnp.clip(jnp.exp(jax.random.uniform(key_list[2], (), jnp.float32, math.log(0.24), math.log(0.3))), 0.24, 0.3)
    stiffness = scatter_about(key_list[3], (3, MODES, MODES), (MODES // 16) ** -0.5, 3.5, (), jnp.float32)
    star_matrices = scatter_about(key_list[4], (3, QTY, QTY), (3 * QTY) ** -0.5, 1.25, (), jnp.float32)
    projection = scatter_about(key_list[5], (4, FACE_MODES, MODES), MODES ** -0.5, 0.75, (), jnp.float32)
    lifting = scatter_about(key_list[6], (4, MODES, FACE_MODES), FACE_MODES ** -0.5, 1.25, (), jnp.float32)
    upwind = scatter_about(key_list[7], (QTY, QTY), QTY ** -0.5, 2.0, (), jnp.float32)
    nb_index = draw_nb_index(jax.random.fold_in(key_list[13], 71), 0)
    nb_face = place_ends(jax.random.randint(key_list[9], (4, ELEMS), 0, 4), jax.random.fold_in(key_list[9], 1), 0, 3).astype(jnp.int32)
    iface_elem = place_ends(jax.random.randint(key_list[10], (SLOTS,), 0, E_DEV), jax.random.fold_in(key_list[10], 1), 0, E_DEV - 1).astype(jnp.int32)
    iface_face = place_ends(jax.random.randint(key_list[11], (SLOTS,), 0, 4), jax.random.fold_in(key_list[11], 1), 0, 3).astype(jnp.int32)
    iface_counts = draw_iface_counts(jax.random.fold_in(key_list[13], 71), 0)
    return dict(modal_state=modal_state, inv_size=inv_size, time_step=time_step, stiffness=stiffness, star_matrices=star_matrices, projection=projection, lifting=lifting, upwind=upwind, nb_index=nb_index, nb_face=nb_face, iface_elem=iface_elem, iface_face=iface_face, iface_counts=iface_counts)


PRECISE = lax.Precision.HIGHEST


def derivative(values, inv_scale, stiffness, star_matrices):
    mode_count = values.shape[0]
    mixed_terms = jnp.einsum("dqp,npe->dnqe", star_matrices, values, precision=PRECISE)
    stacked = stiffness.transpose(1, 0, 2).reshape(mode_count, -1)
    result = jnp.dot(stacked, mixed_terms.reshape(stacked.shape[1], -1), precision=PRECISE)
    return -inv_scale * result.reshape(values.shape)


def volume(integral, inv_scale, stiffness, star_matrices):
    mode_count = integral.shape[0]
    mixed_terms = jnp.einsum("dqp,npe->dnqe", star_matrices, integral, precision=PRECISE)
    stacked = stiffness.transpose(2, 0, 1).reshape(mode_count, -1)
    result = jnp.dot(stacked, mixed_terms.reshape(stacked.shape[1], -1), precision=PRECISE)
    return inv_scale * result.reshape(integral.shape)


def taylor(values, inv_scale, stiffness, star_matrices):
    series = [values]
    for order in range(TAYLOR - 1):
        series.append(derivative(series[-1], inv_scale, stiffness, star_matrices))
    return series


def integrate(series, begin_time, end_time):
    running = jnp.zeros_like(series[0])
    for order in range(len(series)):
        weight = (end_time ** (order + 1) - begin_time ** (order + 1)) / math.factorial(order + 1)
        running = running + weight * series[order]
    return running


def project_all(projection, values):
    matrix_rows = projection.reshape(-1, projection.shape[2])
    result = jnp.dot(matrix_rows, values.reshape(values.shape[0], -1), precision=PRECISE)
    return result.reshape(matrix_rows.shape[0], values.shape[1], values.shape[2])


def face_flux(own_traces, extended, face_ids, elem_ids, inv_scale, upwind, lifting):
    by_face = extended.reshape(4, -1, extended.shape[1], extended.shape[2])
    remote = by_face[face_ids, :, :, elem_ids].transpose(0, 2, 3, 1)
    jump = own_traces.reshape(remote.shape) - remote
    mixed_terms = jnp.einsum("qp,frpe->frqe", upwind, jump, precision=PRECISE)
    stacked = lifting.transpose(1, 0, 2).reshape(lifting.shape[1], -1)
    result = jnp.dot(stacked, mixed_terms.reshape(stacked.shape[1], -1), precision=PRECISE)
    return inv_scale * result.reshape(lifting.shape[1], own_traces.shape[1], own_traces.shape[2])


def slot_pick(traces, face_ids, elem_ids):
    by_face = traces.reshape(4, -1, traces.shape[1], traces.shape[2])
    return by_face[face_ids, :, :, elem_ids].transpose(1, 2, 0)


def slot_terms(series, projection, face_ids, elem_ids):
    chosen = projection[face_ids]
    return jnp.stack([jnp.einsum("srm,mqs->rqs", chosen, member[:, :, elem_ids], precision=PRECISE) for member in series])


def slot_lift(jump, face_ids, weights, upwind, lifting):
    mixed_terms = jnp.einsum("qp,rps->rqs", upwind, jump, precision=PRECISE)
    chosen = lifting[face_ids]
    return jnp.einsum("smr,rqs->mqs", chosen, mixed_terms, precision=PRECISE) * weights


def reference(modal_state, inv_size, time_step, stiffness, star_matrices, projection, lifting, upwind, nb_index, nb_face, iface_elem, iface_face, iface_counts):
    elem_count = modal_state.shape[2]
    fine_devs = N_DOM // 3
    device = jnp.arange(elem_count, dtype=jnp.int32) // E_DEV
    global_index = (device[None, :] * E_DEV + nb_index - BND).astype(jnp.int32)
    fine_rows = jnp.arange(fine_devs, dtype=jnp.int32)[:, None]
    slots = jnp.arange(CAP, dtype=jnp.int32)[None, :]
    fine_column = fine_rows * CAP + slots
    coarse_rows = fine_rows + (N_DOM - fine_devs)
    coarse_column = coarse_rows * CAP + slots
    fine_elem = (fine_rows * E_DEV + iface_elem[fine_column]).reshape(-1).astype(jnp.int32)
    fine_face = iface_face[fine_column].reshape(-1)
    coarse_elem = (coarse_rows * E_DEV + iface_elem[coarse_column]).reshape(-1).astype(jnp.int32)
    coarse_face = iface_face[coarse_column].reshape(-1)
    live = (slots < iface_counts[:fine_devs][:, None]).astype(jnp.float32).reshape(-1)

    start_time = time_step * 0.0
    coarse_series = taylor(modal_state, inv_size, stiffness, star_matrices)
    coarse_integral = integrate(coarse_series, start_time, time_step)
    coarse_traces = project_all(projection, coarse_integral)
    down_terms = slot_terms(coarse_series, projection, coarse_face, coarse_elem)

    substep = time_step / SUBSTEPS
    fine_state = modal_state
    fine_weight = inv_size[fine_elem] * live
    for section in range(SUBSTEPS):
        series = taylor(fine_state, inv_size, stiffness, star_matrices)
        integral = integrate(series, start_time, substep)
        traces = project_all(projection, integral)
        flux = face_flux(traces, traces, nb_face, global_index, inv_size, upwind, lifting)
        own_trace = slot_pick(traces, fine_face, fine_elem)
        remote_trace = integrate(down_terms, section * substep, (section + 1) * substep)
        lifted = slot_lift(own_trace - remote_trace, fine_face, fine_weight, upwind, lifting)
        spread = jnp.zeros_like(modal_state).at[:, :, fine_elem].add(lifted)
        fine_state = fine_state + volume(integral, inv_size, stiffness, star_matrices) - flux - spread
        summed = own_trace if section == 0 else summed + own_trace

    coarse_flux = face_flux(coarse_traces, coarse_traces, nb_face, global_index, inv_size, upwind, lifting)
    coarse_own = slot_pick(coarse_traces, coarse_face, coarse_elem)
    lifted = slot_lift(coarse_own - summed, coarse_face, inv_size[coarse_elem] * live, upwind, lifting)
    spread = jnp.zeros_like(modal_state).at[:, :, coarse_elem].add(lifted)
    coarse_state = modal_state + volume(coarse_integral, inv_size, stiffness, star_matrices) - coarse_flux - spread
    return jnp.where(device[None, None, :] < fine_devs, fine_state, coarse_state)
```

```python
import functools

import jax
import jax.numpy as jnp
from jax import lax
from jax.experimental import pallas as pl
from jax.experimental.pallas import tpu as pltpu
from jax.sharding import PartitionSpec as P

TAYLOR = 6
SUBSTEPS = 4
MODES = 56
QTY = 9
FACE_MODES = 21
FACE_PAD = 24
FACES = 4
CELLS = 128
HALF = 64
SLOTS = 32
WIDTH = QTY * CELLS
FINE = 85
FIRST_PARTNER = 256 - FINE
PAIRS = (QTY + 1) // 2

F32 = jnp.float32
BF16 = jnp.bfloat16


def lanes(q, count=1):
    return slice(q * CELLS, (q + count) * CELLS)


def lane_ids(rows):
    return lax.broadcasted_iota(jnp.int32, (rows, CELLS), 1)


def swap_halves(x):
    return pltpu.roll(x, HALF, 1)


def coarse_part(x):
    return x.astype(BF16).astype(F32)


def weights_k(w):
    hi = coarse_part(w)
    lane = lax.broadcasted_iota(jnp.int32, w.shape, 1)
    return jnp.where(lane < 128, hi, w - hi).astype(BF16)


def weights_m(w):
    hi = coarse_part(w)
    row = lax.broadcasted_iota(jnp.int32, w.shape, 0)
    return jnp.where(row < MODES, hi, w - hi).astype(BF16)


def field_k(x):
    padded = jnp.concatenate([x, jnp.zeros((8, x.shape[1]), F32)], axis=0)
    hi = padded.astype(BF16)
    lo = (padded - hi.astype(F32)).astype(BF16)
    return jnp.concatenate([hi, lo, hi], axis=0)


def dot(a, b):
    return jnp.dot(a, b, preferred_element_type=F32)


def apply_k(weights, field_ref, out_ref, rows):
    for start in range(0, QTY, 2):
        part = lanes(start, min(2, QTY - start))
        out_ref[:rows, part] = dot(weights, field_k(field_ref[:, part]))


def mix_star(star_ref, y_ref, emit):
    for base in range(0, QTY, 3):
        sums = [None] * 3
        for p in range(QTY):
            for d in range(3):
                y = y_ref[d * MODES : (d + 1) * MODES, lanes(p)]
                for j in range(3):
                    term = star_ref[d, base + j, p] * y
                    sums[j] = term if sums[j] is None else sums[j] + term
        for j in range(3):
            emit(base + j, sums[j])


def mix_upwind(upwind_ref, w_ref, emit):
    for base in range(0, QTY, 3):
        sums = [None] * 3
        for p in range(QTY):
            w = w_ref[:, lanes(p)]
            for j in range(3):
                term = upwind_ref[base + j, p] * w
                sums[j] = term if sums[j] is None else sums[j] + term
        for j in range(3):
            emit(base + j, sums[j])


def predict(v_ref, w_ref, y_ref, coef_ref, stiff, inv, star_ref):
    for q in range(QTY):
        w_ref[:, lanes(q)] = coef_ref[0:1, :] * v_ref[:, lanes(q)]

    def order(k, carry):
        apply_k(stiff, v_ref, y_ref, 3 * MODES)
        weight = coef_ref[pl.ds(k, 1), :]

        def emit(q, value):
            term = -inv * value
            v_ref[:, lanes(q)] = term
            w_ref[:, lanes(q)] = w_ref[:, lanes(q)] + weight * term

        mix_star(star_ref, y_ref, emit)
        return carry

    lax.fori_loop(1, TAYLOR, order, 0)


def fill_coefs(coef_ref, begin, end):
    b, e, fact = begin, end, 1.0
    for k in range(TAYLOR):
        fact = fact * (k + 1)
        coef_ref[k : k + 1, :] = (e - b) * (1.0 / fact)
        b, e = b * begin, e * end


def put_messages(even, u_of, odd_ref, even_ref):
    low = lane_ids(MODES) < HALF
    for j in range(PAIRS):
        first, second = u_of(2 * j), u_of(min(2 * j + 1, QTY - 1))
        left = jnp.where(low, first, swap_halves(second))
        right = jnp.where(low, swap_halves(first), second)
        odd_ref[:, lanes(j)] = jnp.where(even, left, right)
        even_ref[:, lanes(j)] = jnp.where(even, right, left)


def take_messages(even, odd_ref, even_ref, halo_ref):
    low = lane_ids(MODES) < HALF
    for j in range(PAIRS):
        a, b = odd_ref[:, lanes(j)], even_ref[:, lanes(j)]
        left = jnp.where(even, a, b)
        right = jnp.where(even, b, a)
        halo_ref[:, lanes(2 * j)] = jnp.where(low, left, swap_halves(right))
        if 2 * j + 1 < QTY:
            halo_ref[:, lanes(2 * j + 1)] = jnp.where(low, swap_halves(left), right)


def pick_matrix(target, rows):
    row = lax.broadcasted_iota(jnp.int32, (rows, CELLS), 0)
    return jnp.concatenate(
        [
            jnp.where(row == target[f : f + 1, :], 1.0, 0.0).astype(BF16)
            for f in range(FACES)
        ],
        axis=1,
    )


def slot_matrix(slot_target, live, section):
    shape = (CELLS, FACES * CELLS)
    row = lax.broadcasted_iota(jnp.int32, shape, 0)
    column = lax.broadcasted_iota(jnp.int32, shape, 1)
    keep = (column == slot_target) & (row % SLOTS < live)
    if section is not None:
        keep = keep & (row // SLOTS == section)
    return jnp.where(keep, 1.0, 0.0)


def by_quantity(t_ref):
    return jnp.concatenate(
        [
            jnp.concatenate(
                [
                    t_ref[f * FACE_PAD : (f + 1) * FACE_PAD, lanes(q)]
                    for q in range(QTY)
                ],
                axis=0,
            )
            for f in range(FACES)
        ],
        axis=1,
    )


def by_face(g):
    return jnp.concatenate(
        [
            jnp.concatenate(
                [
                    g[q * FACE_PAD : (q + 1) * FACE_PAD, lanes(f)]
                    for f in range(FACES)
                ],
                axis=0,
            )
            for q in range(QTY)
        ],
        axis=1,
    )


def two_parts(x):
    hi = coarse_part(x)
    return jnp.concatenate([hi, x - hi], axis=0).astype(BF16)


def lift(lift_w, stacked):
    both = dot(lift_w, stacked)
    return both[:MODES] + both[MODES:]


def pick_parts(source, matrix):
    return dot(two_parts(source), matrix)


def lift_picked(lift_w, picked):
    rows = QTY * FACE_PAD
    stacked = jnp.concatenate([by_face(picked[:rows]), by_face(picked[rows:])], axis=0)
    return lift(lift_w, stacked.astype(BF16))


def slot_traces(u_of, elems, faces, proj, u_ref, t_ref):
    index = jnp.broadcast_to(elems, (MODES, CELLS))
    for q in range(QTY):
        u_ref[:, lanes(q)] = jnp.take_along_axis(u_of(q), index, axis=1)
    return slot_faces(faces, proj, u_ref, t_ref)


def slot_faces(faces, proj, u_ref, t_ref):
    apply_k(proj, u_ref, t_ref, FACES * FACE_PAD)
    tiles = []
    for q in range(QTY):
        total = jnp.zeros((FACE_PAD, CELLS), F32)
        for f in range(FACES):
            total = jnp.where(
                faces == f, t_ref[f * FACE_PAD : (f + 1) * FACE_PAD, lanes(q)], total
            )
        tiles.append(total)
    return tiles


def live_slots(own, counts_ref):
    fine = own < FINE
    partner = own >= FIRST_PARTNER
    at = jnp.where(fine, own, jnp.where(partner, own - FIRST_PARTNER, 0))
    return jnp.where(fine | partner, counts_ref[at], 0)


def remote_kernel(
    own_ref, dt_ref, star_ref, upwind_ref, state_ref, inv_ref, elem_ref, face_ref,
    stiff_ref, proj_ref, out_ref, v_ref, w_ref, y_ref, t_ref, coef_ref,
):
    @pl.when(own_ref[0] >= FIRST_PARTNER)
    def _():
        index = jnp.broadcast_to(elem_ref[...], (MODES, CELLS))
        for q in range(QTY):
            v_ref[:, lanes(q)] = jnp.take_along_axis(state_ref[:, q, :], index, axis=1)
        spread = jnp.broadcast_to(inv_ref[...], (8, CELLS))
        inv = jnp.take_along_axis(spread, index[:8], axis=1)[0:1, :]
        section = (lane_ids(1) // SLOTS).astype(F32)
        substep = dt_ref[0] * (1.0 / SUBSTEPS)
        fill_coefs(coef_ref, section * substep, (section + 1.0) * substep)
        predict(v_ref, w_ref, y_ref, coef_ref, weights_k(stiff_ref[...]), inv, star_ref)

        def emit(q, value):
            v_ref[:, lanes(q)] = value

        mix_upwind(upwind_ref, w_ref, emit)
        tiles = slot_faces(face_ref[...], weights_k(proj_ref[...]), v_ref, t_ref)
        for q in range(QTY):
            out_ref[q * FACE_PAD : (q + 1) * FACE_PAD, :] = tiles[q]


def uniform_coefs(coef_ref, end):
    fill_coefs(coef_ref, jnp.zeros((1, CELLS), F32), jnp.full((1, CELLS), end, F32))


def first_kernel(
    own_ref, dt_ref, star_ref, upwind_ref, state_ref, inv_ref, stiff_ref,
    flat_ref, w_ref, u_ref, odd_ref, even_ref, v_ref, y_ref, coef_ref,
):
    own = own_ref[0]
    for q in range(QTY):
        value = state_ref[:, q, :]
        v_ref[:, lanes(q)] = value
        flat_ref[:, lanes(q)] = value
    step = jnp.where(own < FINE, dt_ref[0] * (1.0 / SUBSTEPS), dt_ref[0])
    uniform_coefs(coef_ref, step)
    predict(v_ref, w_ref, y_ref, coef_ref, weights_k(stiff_ref[...]), inv_ref[...], star_ref)

    def emit(q, value):
        u_ref[:, lanes(q)] = value

    mix_upwind(upwind_ref, w_ref, emit)
    put_messages(own % 2 == 0, lambda q: u_ref[:, lanes(q)], odd_ref, even_ref)


def inner_kernel(
    section, own_ref, counts_ref, star_ref, state_ref, w_ref, u_ref, inv_ref, index_ref,
    face_ref, target_ref, remote_ref, stiff_t_ref, proj_ref, lift_ref, out_ref, t_ref, y_ref,
):
    own = own_ref[0]

    def work():
        apply_k(weights_k(proj_ref[...]), u_ref, t_ref, FACES * FACE_PAD)
        nb = index_ref[...]
        inside = (nb >= HALF) & (nb < HALF + CELLS)
        target = jnp.where(inside, face_ref[...] * CELLS + nb - HALF, -1)
        slots = slot_matrix(target_ref[...], live_slots(own, counts_ref), section)
        matrix = jnp.concatenate(
            [pick_matrix(target, FACES * CELLS), slots.astype(BF16)], axis=0
        )
        own_traces = by_quantity(t_ref)
        source = jnp.concatenate([own_traces, remote_ref[...]], axis=1)
        picked = pick_parts(source, matrix)
        rows = QTY * FACE_PAD
        factor = 1.0 + jnp.sum(slots, axis=0, keepdims=True)
        jump = factor * own_traces - (picked[:rows] + picked[rows:])
        flux = lift(weights_m(lift_ref[...]), two_parts(by_face(jump)))
        apply_k(weights_k(stiff_t_ref[...]), w_ref, y_ref, 3 * MODES)
        inv = inv_ref[...]

        def emit(q, value):
            out_ref[:, lanes(q)] = state_ref[:, lanes(q)] + inv * (value - flux[:, lanes(q)])

        mix_star(star_ref, y_ref, emit)

    if section == 0:
        work()
    else:
        pl.when(own < FINE)(work)


def halo_lift(own, odd_in, even_in, index_ref, face_ref, proj_ref, lift_w, halo_ref, t_ref):
    take_messages(own % 2 == 0, odd_in, even_in, halo_ref)
    apply_k(weights_k(proj_ref[...]), halo_ref, t_ref, FACES * FACE_PAD)
    nb = index_ref[...]
    lane = jnp.where(nb < HALF, nb, nb - CELLS)
    outside = (nb < HALF) | (nb >= HALF + CELLS)
    target = jnp.where(outside, face_ref[...] * CELLS + lane, -1)
    picked = pick_parts(by_quantity(t_ref), pick_matrix(target, FACES * CELLS))
    return lift_picked(lift_w, picked)


def outer_kernel(
    section, own_ref, dt_ref, star_ref, upwind_ref, state_ref, odd_in, even_in, inv_ref, index_ref,
    face_ref, proj_ref, lift_ref, stiff_ref, sum_in, elem_ref, slot_face_ref,
    flat_ref, w_ref, u_ref, odd_ref, even_ref, sum_ref, halo_ref, t_ref, v_ref, y_ref, coef_ref,
):
    own = own_ref[0]

    def update():
        lift_w = weights_m(lift_ref[...])
        gain = halo_lift(
            own, odd_in, even_in, index_ref, face_ref, proj_ref, lift_w, halo_ref, t_ref
        )
        inv = inv_ref[...]
        for q in range(QTY):
            value = state_ref[:, lanes(q)] + inv * gain[:, lanes(q)]
            flat_ref[:, lanes(q)] = value
            v_ref[:, lanes(q)] = value

    if section == 0:
        update()

    @pl.when(own < FINE)
    def _():
        if section > 0:
            update()
        uniform_coefs(coef_ref, dt_ref[0] * (1.0 / SUBSTEPS))
        predict(
            v_ref, w_ref, y_ref, coef_ref, weights_k(stiff_ref[...]), inv_ref[...], star_ref
        )

        def emit(q, value):
            u_ref[:, lanes(q)] = value

        mix_upwind(upwind_ref, w_ref, emit)
        put_messages(own % 2 == 0, lambda q: u_ref[:, lanes(q)], odd_ref, even_ref)
        if section < SUBSTEPS - 2:
            sum_ref[...] = sum_in[...] + u_ref[...]
        else:
            tiles = slot_traces(
                lambda q: sum_in[:, lanes(q)] + u_ref[:, lanes(q)],
                elem_ref[...],
                slot_face_ref[...],
                weights_k(proj_ref[...]),
                halo_ref,
                t_ref,
            )
            whole = jnp.concatenate(tiles + [jnp.zeros((8, CELLS), F32)], axis=0)
            group = lane_ids(8) // SLOTS
            for j in range(whole.shape[0] // 32):
                total = whole[32 * j : 32 * j + 8]
                for g in range(1, 4):
                    rows = 32 * j + 8 * g
                    total = jnp.where(group == g, whole[rows : rows + 8], total)
                sum_ref[8 * j : 8 * j + 8, :] = total


def last_kernel(
    own_ref, counts_ref, fine_ref, coarse_ref, odd_in, even_in, inv_ref, index_ref, face_ref, proj_ref,
    lift_ref, up_ref, target_ref, out_ref, halo_ref, t_ref,
):
    own = own_ref[0]
    inv = inv_ref[...]

    @pl.when(own < FINE)
    def _():
        gain = halo_lift(
            own, odd_in, even_in, index_ref, face_ref, proj_ref,
            weights_m(lift_ref[...]), halo_ref, t_ref,
        )
        for q in range(QTY):
            out_ref[:, q, :] = fine_ref[:, lanes(q)] + inv * gain[:, lanes(q)]

    @pl.when(own >= FINE)
    def _():
        group = lane_ids(8) // SLOTS
        tiles = []
        for j in range(QTY * FACE_PAD // 8):
            row = 8 * (j // 4)
            tiles.append(jnp.where(group == j % 4, up_ref[row : row + 8, :], 0.0))
        source = jnp.concatenate(tiles, axis=0)
        slots = slot_matrix(target_ref[...], live_slots(own, counts_ref), None)
        picked = pick_parts(source, slots.astype(BF16))
        gain = lift_picked(weights_m(lift_ref[...]), picked)
        for q in range(QTY):
            out_ref[:, q, :] = coarse_ref[:, lanes(q)] + inv * gain[:, lanes(q)]


S = pl.BlockSpec(memory_space=pltpu.SMEM)
V = pl.BlockSpec(memory_space=pltpu.VMEM)
FIELD = (MODES, WIDTH)
MESSAGE = (MODES, PAIRS * CELLS)
SLOT_ROWS = QTY * FACE_PAD
UP_ROWS = 56


def call(kernel, specs, outs, scratch, operands, flops, name):
    shapes = [jax.ShapeDtypeStruct(o, F32) for o in outs]
    result = pl.pallas_call(
        kernel,
        in_specs=specs,
        out_specs=[V] * len(outs),
        out_shape=shapes,
        scratch_shapes=[pltpu.VMEM(s, F32) for s in scratch],
        compiler_params=pltpu.CompilerParams(vmem_limit_bytes=32 * 1024 * 1024),
        cost_estimate=pl.CostEstimate(
            flops=flops, bytes_accessed=2_000_000, transcendentals=0
        ),
        name=name,
    )(*operands)
    return result


def shards(
    modal_state, inv_size, time_step, stiffness, star_matrices, projection, lifting, upwind,
    nb_index, nb_face, iface_elem, iface_face, iface_counts,
):
    own = lax.axis_index("dom").astype(jnp.int32).reshape(1)
    dt = time_step.reshape(1)
    inv = inv_size.reshape(1, CELLS)
    elems = jnp.tile(iface_elem, 4).reshape(1, CELLS)
    faces = jnp.tile(iface_face, 4).reshape(1, CELLS)
    target = (faces * CELLS + elems).reshape(CELLS, 1)

    wide = ((0, 0), (0, 0), (0, 64 - MODES))

    def thrice(x):
        return jnp.concatenate([x, x, x], axis=1)

    stiff = thrice(jnp.pad(stiffness, wide).reshape(3 * MODES, 64))
    stiff_t = thrice(jnp.pad(stiffness.transpose(0, 2, 1), wide).reshape(3 * MODES, 64))
    tall = ((0, 0), (0, FACE_PAD - FACE_MODES), (0, 64 - MODES))
    proj = thrice(jnp.pad(projection, tall).reshape(FACES * FACE_PAD, 64))
    lift_w = jnp.pad(lifting, ((0, 0), (0, 0), (0, FACE_PAD - FACE_MODES)))
    lift_w = lift_w.transpose(1, 0, 2).reshape(MODES, FACES * FACE_PAD)
    lift_w = jnp.tile(lift_w, (2, 2))

    count = lax.axis_size("dom")
    down = [(i + FIRST_PARTNER, i) for i in range(FINE)]
    up = [(i, i + FIRST_PARTNER) for i in range(FINE)]

    def swaps(first, last):
        pairs = [(i, i + 1) for i in range(first, last, 2)]
        pairs = [p for p in pairs if p[1] < last]
        return pairs + [(b, a) for a, b in pairs]

    odd_fine, even_fine = swaps(1, FINE), swaps(0, FINE)
    odd_all = odd_fine + swaps(FINE, count)
    even_all = even_fine + swaps(FINE + 1, count)

    coef = (8, CELLS)
    y_shape = (3 * MODES, WIDTH)
    t_shape = (FACES * FACE_PAD, WIDTH)

    (remote,) = call(
        remote_kernel,
        [S] * 4 + [V] * 6,
        [(SLOT_ROWS, CELLS)],
        [FIELD, FIELD, y_shape, t_shape, coef],
        (own, dt, star_matrices, upwind, modal_state, inv, elems, faces, stiff, proj),
        20_000_000,
        "remote",
    )
    remote = lax.ppermute(remote, "dom", down)

    flat, w, u, odd, even = call(
        first_kernel,
        [S] * 4 + [V] * 3,
        [FIELD, FIELD, FIELD, MESSAGE, MESSAGE],
        [FIELD, y_shape, coef],
        (own, dt, star_matrices, upwind, modal_state, inv, stiff),
        2_000_000_000,
        "first",
    )
    total = u
    coarse = None
    for section in range(SUBSTEPS):
        odd_in = lax.ppermute(odd, "dom", odd_all if section == 0 else odd_fine)
        even_in = lax.ppermute(even, "dom", even_all if section == 0 else even_fine)
        (inner,) = call(
            functools.partial(inner_kernel, section),
            [S] * 3 + [V] * 11,
            [FIELD],
            [t_shape, y_shape],
            (own, iface_counts, star_matrices, flat, w, u, inv, nb_index, nb_face, target,
             remote, stiff_t, proj, lift_w),
            2_000_000_000,
            f"inner{section}",
        )
        if section == SUBSTEPS - 1:
            break
        last = section == SUBSTEPS - 2
        flat, w, u, odd, even, total = call(
            functools.partial(outer_kernel, section),
            [S] * 4 + [V] * 12,
            [FIELD, FIELD, FIELD, MESSAGE, MESSAGE, (UP_ROWS, CELLS) if last else FIELD],
            [FIELD, t_shape, FIELD, y_shape, coef],
            (own, dt, star_matrices, upwind, inner, odd_in, even_in, inv, nb_index, nb_face,
             proj, lift_w, stiff, total, elems, faces),
            2_000_000_000,
            f"outer{section}",
        )
        if section == 0:
            coarse = flat
    arrived = lax.ppermute(total, "dom", up)
    (out,) = call(
        last_kernel,
        [S] * 2 + [V] * 11,
        [(MODES, QTY, CELLS)],
        [FIELD, t_shape],
        (own, iface_counts, inner, coarse, odd_in, even_in, inv, nb_index, nb_face, proj, lift_w,
         arrived, target),
        1_000_000_000,
        "last",
    )
    return out


def solution(mesh):
    return jax.shard_map(
        shards,
        mesh=mesh,
        in_specs=(
            P(None, None, "dom"),
            P("dom"),
            P(),
            P(),
            P(),
            P(),
            P(),
            P(),
            P(None, "dom"),
            P(None, "dom"),
            P("dom"),
            P("dom"),
            P(),
        ),
        out_specs=P(None, None, "dom"),
        check_vma=False,
    )
```

```python
import functools

import jax
import jax.numpy as jnp
from jax import lax
from jax.experimental import pallas as pl
from jax.experimental.pallas import tpu as pltpu
from jax.sharding import PartitionSpec as P

TAYLOR = 6
SUBSTEPS = 4
MODES = 56
QTY = 9
FACE_MODES = 21
FACE_PAD = 24
FACES = 4
CELLS = 128
HALF = 64
SLOTS = 32
WIDTH = QTY * CELLS
FINE = 85
FIRST_PARTNER = 256 - FINE
DENSE = 512
PACKED = (56, CELLS)
LOADED = 8
SETUP_VMEM = 16

F32 = jnp.float32
BF16 = jnp.bfloat16


def lanes(q, count=1):
    return slice(q * CELLS, (q + count) * CELLS)


def lane_ids(rows):
    return lax.broadcasted_iota(jnp.int32, (rows, CELLS), 1)


def swap_halves(x):
    return pltpu.roll(x, HALF, 1)


def coarse_part(x):
    return x.astype(BF16).astype(F32)


def field_k(x):
    padded = jnp.concatenate([x, jnp.zeros((8, x.shape[1]), F32)], axis=0)
    hi = padded.astype(BF16)
    lo = (padded - hi.astype(F32)).astype(BF16)
    return jnp.concatenate([hi, lo, hi], axis=0)


def dot(a, b):
    return jnp.dot(a, b, preferred_element_type=F32)


def apply_k(weights, field_ref, out_ref, rows):
    for start in range(0, QTY, 2):
        part = lanes(start, min(2, QTY - start))
        out_ref[:rows, part] = dot(weights, field_k(field_ref[:, part]))


def spread_star(star_ref, table_ref):
    for d in range(3):
        entries = star_ref[:, d, :]
        for p in range(QTY):
            row = (d * QTY + p) * 16
            table_ref[row : row + QTY, :] = jnp.broadcast_to(
                entries[:, p : p + 1], (QTY, CELLS)
            )


def spread_upwind(upwind_ref, table_ref):
    entries = upwind_ref[...]
    for p in range(QTY):
        table_ref[p * 16 : p * 16 + QTY, :] = jnp.broadcast_to(
            entries[:, p : p + 1], (QTY, CELLS)
        )


def mix_star(table_ref, y_ref, emit):
    for base in range(0, QTY, 3):
        sums = [None] * 3
        for p in range(QTY):
            for d in range(3):
                y = y_ref[d * MODES : (d + 1) * MODES, lanes(p)]
                for j in range(3):
                    row = (d * QTY + p) * 16 + base + j
                    term = table_ref[row : row + 1, :] * y
                    sums[j] = term if sums[j] is None else sums[j] + term
        for j in range(3):
            emit(base + j, sums[j])


def mix_upwind(table_ref, w_of, emit):
    for base in range(0, QTY, 3):
        sums = [None] * 3
        for p in range(QTY):
            w = w_of(p)
            for j in range(3):
                row = p * 16 + base + j
                term = table_ref[row : row + 1, :] * w
                sums[j] = term if sums[j] is None else sums[j] + term
        for j in range(3):
            emit(base + j, sums[j])


def put_dense(value, base, out_ref):
    hi = coarse_part(value)
    out_ref[base : base + MODES, :] = hi
    out_ref[DENSE + base : DENSE + base + MODES, :] = value - hi


def build_dense(star_ref, stiff_ref, out_ref):
    tiled, scales = [], []
    wide = lax.broadcasted_iota(jnp.int32, (QTY, DENSE), 1)
    for d in range(3):
        block = jnp.concatenate(
            [stiff_ref[d], jnp.zeros((MODES, CELLS - MODES), F32)], axis=1
        )
        columns = []
        for c in range(DENSE // CELLS):
            column = lane_ids(MODES) + c * CELLS
            index = column % MODES
            columns.append(jnp.take_along_axis(block, index, axis=1))
        tiled.append(jnp.concatenate(columns, axis=1))
        entries = star_ref[:, d, :]
        scale = jnp.zeros((QTY, DENSE), F32)
        for p in range(QTY):
            here = (wide >= p * MODES) & (wide < (p + 1) * MODES)
            scale = jnp.where(here, entries[:, p : p + 1], scale)
        scales.append(scale)
    for q in range(QTY):
        value = sum(scales[d][q : q + 1, :] * tiled[d] for d in range(3))
        put_dense(value, q * MODES, out_ref)
    out_ref[QTY * MODES : DENSE, :] = jnp.zeros((8, DENSE), F32)
    out_ref[DENSE + QTY * MODES :, :] = jnp.zeros((8, DENSE), F32)


def dense(weights, rows):
    padded = jnp.concatenate([rows, jnp.zeros((8, CELLS), F32)], axis=0)
    hi = padded.astype(BF16)
    lo = (padded - hi.astype(F32)).astype(BF16)
    both = dot(weights, jnp.concatenate([hi, lo], axis=1))
    top = both[: QTY * MODES]
    return top[:, :CELLS] + (top[:, CELLS:] + both[DENSE : DENSE + QTY * MODES, :CELLS])


def block(rows, q):
    return rows[q * MODES : (q + 1) * MODES]


def predict_five(dense_ref, v_ref, u_ref, coef_ref, inv):
    u_ref[...] = coef_ref[TAYLOR - 1 : TAYLOR, :] * v_ref[...]

    def order(k, carry):
        weight = coef_ref[pl.ds(TAYLOR - 1 - k, 1), :]
        u_ref[...] = weight * v_ref[...] - inv * dense(dense_ref[...], u_ref[...])
        return carry

    lax.fori_loop(1, TAYLOR, order, 0)


def predict_three(dense_ref, square_ref, v, coef_ref, inv):
    c = [coef_ref[k : k + 1, :] for k in range(TAYLOR)]
    two = inv * inv
    u = -inv * dense(dense_ref[...], v)
    top = c[4] * v + c[5] * u
    mid = c[2] * v + c[3] * u + two * dense(square_ref[...], top)
    return c[0] * v + c[1] * u + two * dense(square_ref[...], mid)


def fill_coefs(coef_ref, begin, end):
    b, e, fact = begin, end, 1.0
    for k in range(TAYLOR):
        fact = fact * (k + 1)
        coef_ref[k : k + 1, :] = (e - b) * (1.0 / fact)
        b, e = b * begin, e * end


def put_messages(even, u_of, odd_ref, even_ref):
    def put(row, first, second):
        rows = first.shape[0]
        low = lane_ids(rows) < HALF
        left = jnp.where(low, first, swap_halves(second))
        right = jnp.where(low, swap_halves(first), second)
        odd_ref[row : row + rows, :] = jnp.where(even, left, right)
        even_ref[row : row + rows, :] = jnp.where(even, right, left)

    for j in range(QTY // 2):
        put(j * MODES, u_of(2 * j), u_of(2 * j + 1))
    tail = u_of(QTY - 1)
    put(QTY // 2 * MODES, tail[:32], tail[24:])


def take_messages(even, odd_ref, even_ref, halo_ref):
    def take(row, rows):
        low = lane_ids(rows) < HALF
        a, b = odd_ref[row : row + rows, :], even_ref[row : row + rows, :]
        left = jnp.where(even, a, b)
        right = jnp.where(even, b, a)
        first = jnp.where(low, left, swap_halves(right))
        second = jnp.where(low, swap_halves(left), right)
        return first, second

    for j in range(QTY // 2):
        first, second = take(j * MODES, MODES)
        halo_ref[:, lanes(2 * j)] = first
        halo_ref[:, lanes(2 * j + 1)] = second
    first, second = take(QTY // 2 * MODES, 32)
    halo_ref[:32, lanes(QTY - 1)] = first
    halo_ref[32:, lanes(QTY - 1)] = second[8:]


def pick_matrix(target, rows):
    row = lax.broadcasted_iota(jnp.int32, (rows, CELLS), 0)
    return jnp.concatenate(
        [
            jnp.where(row == target[f : f + 1, :], 1.0, 0.0).astype(BF16)
            for f in range(FACES)
        ],
        axis=1,
    )


def slot_matrix(slot_target, live):
    shape = (CELLS, FACES * CELLS)
    row = lax.broadcasted_iota(jnp.int32, shape, 0) % SLOTS
    column = lax.broadcasted_iota(jnp.int32, shape, 1)
    keep = (column == slot_target) & (row.astype(F32) < live)
    return jnp.where(keep, 1.0, 0.0)


def as_column(row):
    shape = (CELLS, CELLS)
    same = lax.broadcasted_iota(jnp.int32, shape, 0) == lax.broadcasted_iota(
        jnp.int32, shape, 1
    )
    kept = jnp.where(same, row.astype(F32), 0.0)
    return jnp.sum(kept, axis=1, keepdims=True).astype(jnp.int32)


def transposed(x):
    tall = jnp.concatenate([x, jnp.zeros((CELLS - x.shape[0], x.shape[1]), F32)], axis=0)
    full = jnp.concatenate([tall, jnp.zeros((CELLS, CELLS - x.shape[1]), F32)], axis=1)
    return full.T[: x.shape[1]]


def by_quantity(t_ref):
    return jnp.concatenate(
        [
            jnp.concatenate(
                [
                    t_ref[f * FACE_PAD : (f + 1) * FACE_PAD, lanes(q)]
                    for q in range(QTY)
                ],
                axis=0,
            )
            for f in range(FACES)
        ],
        axis=1,
    )


def by_face(g):
    return jnp.concatenate(
        [
            jnp.concatenate(
                [
                    g[q * FACE_PAD : (q + 1) * FACE_PAD, lanes(f)]
                    for f in range(FACES)
                ],
                axis=0,
            )
            for q in range(QTY)
        ],
        axis=1,
    )


def two_parts(x):
    hi = coarse_part(x)
    return jnp.concatenate([hi, x - hi], axis=0).astype(BF16)


def lift(lift_w, stacked):
    both = dot(lift_w, stacked)
    return both[:MODES] + both[MODES:]


def pick_parts(source, matrix):
    return dot(two_parts(source), matrix)


def lift_picked(lift_w, picked):
    rows = QTY * FACE_PAD
    stacked = jnp.concatenate([by_face(picked[:rows]), by_face(picked[rows:])], axis=0)
    return lift(lift_w, stacked.astype(BF16))


def slot_traces(u_of, elems, faces, proj, u_ref, t_ref):
    index = jnp.broadcast_to(elems, (MODES, CELLS))
    for q in range(QTY):
        u_ref[:, lanes(q)] = jnp.take_along_axis(u_of(q), index, axis=1)
    return slot_faces(faces, proj, u_ref, t_ref)


def pack_slots(tiles, section, out_ref, base):
    whole = jnp.concatenate(tiles + [jnp.zeros((8, CELLS), F32)], axis=0)
    group = lane_ids(8) // SLOTS
    for j in range(whole.shape[0] // 32):
        total = None
        for g in range(4):
            row = 32 * j + 8 * g
            part = whole[row : row + 8]
            if section is not None and g != section:
                part = pltpu.roll(part, SLOTS * ((g - section) % 4), 1)
            total = part if total is None else jnp.where(group == g, part, total)
        out_ref[base + 8 * j : base + 8 * j + 8, :] = total


def unpack_slots(in_ref, base=0):
    group = lane_ids(8) // SLOTS
    tiles = []
    for j in range(QTY * FACE_PAD // 8):
        row = base + 8 * (j // 4)
        tiles.append(jnp.where(group == j % 4, in_ref[row : row + 8, :], 0.0))
    return jnp.concatenate(tiles, axis=0)


def four_times(row):
    return jnp.concatenate([row] * 4, axis=1)


def slot_faces(faces, proj, u_ref, t_ref):
    apply_k(proj, u_ref, t_ref, FACES * FACE_PAD)
    tiles = []
    for q in range(QTY):
        total = jnp.zeros((FACE_PAD, CELLS), F32)
        for f in range(FACES):
            total = jnp.where(
                faces == f, t_ref[f * FACE_PAD : (f + 1) * FACE_PAD, lanes(q)], total
            )
        tiles.append(total)
    return tiles


def live_slots(own, counts_ref):
    fine = own < FINE
    partner = own >= FIRST_PARTNER
    at = jnp.where(fine, own, jnp.where(partner, own - FIRST_PARTNER, -1))
    place = lax.broadcasted_iota(jnp.int32, (2, CELLS), 0) * CELLS + lane_ids(2)
    mine = jnp.where(place == at, counts_ref[...].astype(F32), 0.0)
    return jnp.sum(jnp.sum(mine, axis=1, keepdims=True), axis=0, keepdims=True)


def put_weights_k(value, row, out_ref):
    hi = coarse_part(value)
    rows = slice(row, row + value.shape[0])
    out_ref[rows, 0:MODES] = hi
    out_ref[rows, 64 : 64 + MODES] = hi
    out_ref[rows, 128 : 128 + MODES] = value - hi


def setup_kernel(*refs):
    own_ref, dt_ref, sources, refs = *refs[:2], refs[2 : 2 + LOADED], refs[2 + LOADED :]
    copies, refs = refs[:LOADED], refs[LOADED:]
    (
        dense_ref, table_ref, early_ref, second_ref, late_ref,
        flat_ref, v_ref, u_ref, t_ref, coef_ref, wide_ref, proj_k_ref, done,
    ) = refs
    moves = [
        pltpu.make_async_copy(source, copy, done.at[i])
        for i, (source, copy) in enumerate(zip(sources, copies))
    ]
    for move in moves:
        move.start()
    (star_ref, stiff_ref, upwind_ref, state_ref, inv_ref, elem_ref, face_ref, proj_ref) = copies
    for move in moves:
        move.wait()
    build_dense(star_ref, stiff_ref, wide_ref)
    dense_ref[...] = wide_ref[...].astype(BF16)
    spread_upwind(upwind_ref, table_ref)

    @pl.when(own_ref[0] >= FIRST_PARTNER)
    def _():
        proj_k_ref[...] = jnp.zeros_like(proj_k_ref)
        for f in range(FACES):
            put_weights_k(proj_ref[:, f, :], f * FACE_PAD, proj_k_ref)
        elems = four_times(elem_ref[...])
        faces = four_times(face_ref[...])
        index = jnp.broadcast_to(elems, (MODES, CELLS))
        for q in range(QTY):
            v_ref[q * MODES : (q + 1) * MODES, :] = jnp.take_along_axis(
                state_ref[q], index, axis=1
            )
        spread = jnp.broadcast_to(inv_ref[...], (8, CELLS))
        inv = jnp.take_along_axis(spread, index[:8], axis=1)[0:1, :]
        section = (lane_ids(1) // SLOTS).astype(F32)
        substep = jnp.full((1, CELLS), dt_ref[0], F32) * (1.0 / SUBSTEPS)
        fill_coefs(coef_ref, section * substep, (section + 1.0) * substep)
        predict_five(dense_ref, v_ref, u_ref, coef_ref, inv)

        def emit(q, value):
            flat_ref[:, lanes(q)] = value

        mix_upwind(table_ref, lambda q: u_ref[q * MODES : (q + 1) * MODES, :], emit)
        tiles = slot_faces(faces, proj_k_ref[...].astype(BF16), flat_ref, t_ref)
        pack_slots(tiles, 0, early_ref, 0)
        pack_slots(tiles, 1, second_ref, 0)
        pack_slots(tiles, 2, late_ref, 0)
        pack_slots(tiles, 3, late_ref, PACKED[0])


def uniform_coefs(coef_ref, end):
    fill_coefs(coef_ref, jnp.zeros((1, CELLS), F32), jnp.full((1, CELLS), end, F32))


def first_kernel(
    own_ref, dt_ref, table_ref, state_ref, inv_ref, dense_ref,
    flat_ref, w_ref, u_ref, odd_ref, even_ref, v_ref, sum_ref, coef_ref,
):
    own = own_ref[0]
    for q in range(QTY):
        value = state_ref[q]
        v_ref[q * MODES : (q + 1) * MODES, :] = value
        flat_ref[:, lanes(q)] = value
    dt = dt_ref[0]
    uniform_coefs(coef_ref, jnp.where(own < FINE, dt * (1.0 / SUBSTEPS), dt))
    predict_five(dense_ref, v_ref, sum_ref, coef_ref, inv_ref[...])

    def rows(q):
        return sum_ref[q * MODES : (q + 1) * MODES, :]

    def emit(q, value):
        u_ref[:, lanes(q)] = value

    mix_upwind(table_ref, rows, emit)
    put_messages(own % 2 == 0, lambda q: u_ref[:, lanes(q)], odd_ref, even_ref)
    for q in range(QTY):
        w_ref[:, lanes(q)] = rows(q)


def prep_kernel(
    own_ref, counts_ref, dense_ref, star_ref, stiff_ref, proj_ref, lift_ref, index_ref, face_ref,
    elem_ref, slot_face_ref, late_in, square_ref, star_table_ref, stiff_t_ref, proj_k_ref, lift_m_ref,
    inside_ref, outside_ref, slots_ref, factor_ref, late_ref, wide_ref, k_ref, m_ref,
):
    own = own_ref[0]

    @pl.when(own < FINE)
    def _():
        whole = dense_ref[...]
        top, low = whole[:DENSE], whole[DENSE:]
        both = dot(whole, top)
        square = both[:DENSE] + (both[DENSE:] + dot(top, low))
        hi = coarse_part(square)
        wide_ref[:DENSE, :] = hi
        wide_ref[DENSE:, :] = square - hi
        square_ref[...] = wide_ref[...].astype(BF16)

    spread_star(star_ref, star_table_ref)
    k_ref[...] = jnp.zeros_like(k_ref)
    for f in range(FACES):
        put_weights_k(proj_ref[:, f, :], f * FACE_PAD, k_ref)
    proj_k_ref[...] = k_ref[: FACES * FACE_PAD, :].astype(BF16)
    k_ref[...] = jnp.zeros_like(k_ref)
    for d in range(3):
        put_weights_k(transposed(stiff_ref[d])[:, :MODES], d * MODES, k_ref)
    stiff_t_ref[...] = k_ref[...].astype(BF16)
    m_ref[...] = jnp.zeros_like(m_ref)
    for f in range(FACES):
        value = transposed(lift_ref[:, f, :])[:, :FACE_PAD]
        hi = coarse_part(value)
        for base in (f * FACE_PAD, (FACES + f) * FACE_PAD):
            m_ref[:MODES, base : base + FACE_PAD] = hi
            m_ref[MODES:, base : base + FACE_PAD] = value - hi
    lift_m_ref[...] = m_ref[...].astype(BF16)
    nb, face = index_ref[...], face_ref[...] * CELLS
    inside = (nb >= HALF) & (nb < HALF + CELLS)
    lane = jnp.where(nb < HALF, nb, nb - CELLS)
    inside_ref[...] = pick_matrix(jnp.where(inside, face + nb - HALF, -1), FACES * CELLS)
    outside_ref[...] = pick_matrix(jnp.where(inside, -1, face + lane), FACES * CELLS)
    target = four_times(slot_face_ref[...] * CELLS + elem_ref[...])
    slots = slot_matrix(as_column(target), live_slots(own, counts_ref))
    slots_ref[...] = slots.astype(BF16)
    count = jnp.sum(slots, axis=0, keepdims=True) * 0.25
    factor_ref[...] = jnp.broadcast_to(1.0 + count, factor_ref.shape)


def inner_kernel(
    section, own_ref, state_ref, w_ref, u_ref, inv_ref, inside_ref, slots_ref, factor_ref,
    remote_ref, star_table_ref, stiff_t_ref, proj_ref, lift_ref, *rest,
):
    out_ref, t_ref, y_ref = rest[section == 1], rest[-2], rest[-1]
    own = own_ref[0]

    def work():
        apply_k(proj_ref[...], u_ref, t_ref, FACES * FACE_PAD)
        remote = unpack_slots(remote_ref, PACKED[0] if section == 3 else 0)
        matrix = jnp.concatenate([inside_ref[...], slots_ref[...]], axis=0)
        own_traces = by_quantity(t_ref)
        source = jnp.concatenate([own_traces, remote], axis=1)
        picked = pick_parts(source, matrix)
        rows = QTY * FACE_PAD
        jump = factor_ref[0:1, :] * own_traces - (picked[:rows] + picked[rows:])
        flux = lift(lift_ref[...], two_parts(by_face(jump)))
        apply_k(stiff_t_ref[...], w_ref, y_ref, 3 * MODES + 8)
        inv = inv_ref[...]

        def emit(q, value):
            out_ref[:, lanes(q)] = state_ref[:, lanes(q)] + inv * (value - flux[:, lanes(q)])

        mix_star(star_table_ref, y_ref, emit)

    if section == 0:
        work()
    else:
        pl.when(own < FINE)(work)


def halo_lift(own, odd_in, even_in, outside_ref, proj_ref, lift_w, halo_ref, t_ref):
    take_messages(own % 2 == 0, odd_in, even_in, halo_ref)
    apply_k(proj_ref[...], halo_ref, t_ref, FACES * FACE_PAD)
    picked = pick_parts(by_quantity(t_ref), outside_ref[...])
    return lift_picked(lift_w, picked)


def outer_kernel(
    section, own_ref, dt_ref, table_ref, state_ref, odd_in, even_in, inv_ref, outside_ref,
    proj_ref, lift_ref, dense_ref, square_ref, sum_in, elem_ref, slot_face_ref,
    flat_ref, w_ref, u_ref, odd_ref, even_ref, sum_ref, halo_ref, t_ref, coef_ref,
):
    own = own_ref[0]

    def update():
        lift_w = lift_ref[...]
        gain = halo_lift(own, odd_in, even_in, outside_ref, proj_ref, lift_w, halo_ref, t_ref)
        inv = inv_ref[...]
        for q in range(QTY):
            flat_ref[:, lanes(q)] = state_ref[:, lanes(q)] + inv * gain[:, lanes(q)]

    if section == 0:
        update()

    @pl.when(own < FINE)
    def _():
        if section > 0:
            update()
        uniform_coefs(coef_ref, dt_ref[0] * (1.0 / SUBSTEPS))
        rows = jnp.concatenate([flat_ref[:, lanes(q)] for q in range(QTY)], axis=0)
        w = predict_three(dense_ref, square_ref, rows, coef_ref, inv_ref[...])
        for q in range(QTY):
            w_ref[:, lanes(q)] = block(w, q)

        def emit(q, value):
            u_ref[:, lanes(q)] = value

        mix_upwind(table_ref, lambda q: w_ref[:, lanes(q)], emit)
        put_messages(own % 2 == 0, lambda q: u_ref[:, lanes(q)], odd_ref, even_ref)
        if section < SUBSTEPS - 2:
            sum_ref[...] = sum_in[...] + u_ref[...]
        else:
            tiles = slot_traces(
                lambda q: sum_in[:, lanes(q)] + u_ref[:, lanes(q)],
                four_times(elem_ref[...]),
                four_times(slot_face_ref[...]),
                proj_ref[...],
                halo_ref,
                t_ref,
            )
            pack_slots(tiles, None, sum_ref, 0)


def last_kernel(
    own_ref, fine_ref, coarse_ref, odd_in, even_in, inv_ref, outside_ref, proj_ref,
    lift_ref, up_ref, slots_ref, out_ref, halo_ref, t_ref,
):
    own = own_ref[0]
    inv = inv_ref[...]

    @pl.when(own < FINE)
    def _():
        gain = halo_lift(
            own, odd_in, even_in, outside_ref, proj_ref, lift_ref[...], halo_ref, t_ref
        )
        for q in range(QTY):
            out_ref[q] = fine_ref[:, lanes(q)] + inv * gain[:, lanes(q)]

    @pl.when(own >= FINE)
    def _():
        picked = pick_parts(unpack_slots(up_ref), slots_ref[...])
        gain = lift_picked(lift_ref[...], picked)
        for q in range(QTY):
            out_ref[q] = coarse_ref[:, lanes(q)] + inv * gain[:, lanes(q)]


S = pl.BlockSpec(memory_space=pltpu.SMEM)
V = pl.BlockSpec(memory_space=pltpu.VMEM)
H = pl.BlockSpec(memory_space=pltpu.HBM)
FIELD = (MODES, WIDTH)
ROWS = (QTY * MODES, CELLS)
MESSAGE = (256, CELLS)


def call(kernel, inputs, outs, scratch, operands, flops, name, aliases=None, place=None, vmem=16, scalars=2):
    shapes = [
        jax.ShapeDtypeStruct(o, F32) if isinstance(o, tuple) else o for o in outs
    ]
    return pl.pallas_call(
        kernel,
        in_specs=[S] * scalars + [place or V] * (inputs - scalars),
        out_specs=[V] * len(outs),
        out_shape=shapes,
        scratch_shapes=[
            pltpu.VMEM(s, F32) if isinstance(s, tuple) else s for s in scratch
        ],
        input_output_aliases=aliases or {},
        compiler_params=pltpu.CompilerParams(vmem_limit_bytes=vmem * 1024 * 1024),
        cost_estimate=pl.CostEstimate(
            flops=flops, bytes_accessed=2_000_000, transcendentals=0
        ),
        name=name,
    )(*operands)


def half(*shape):
    return jax.ShapeDtypeStruct(shape, BF16)


def shards(
    modal_state, inv_size, time_step, stiffness, star_matrices, projection, lifting, upwind,
    nb_index, nb_face, iface_elem, iface_face, iface_counts,
):
    own = lax.axis_index("dom").astype(jnp.int32).reshape(1)
    state = modal_state.transpose(1, 0, 2)
    star = star_matrices.transpose(1, 0, 2)
    proj = projection.transpose(1, 0, 2)
    lift_w = lifting.transpose(2, 0, 1)
    dt = time_step.reshape(1)
    inv = inv_size.reshape(1, CELLS)
    elems = iface_elem.reshape(1, SLOTS)
    faces = iface_face.reshape(1, SLOTS)
    counts = iface_counts.reshape(2, CELLS)

    count = lax.axis_size("dom")
    down = [(i + FIRST_PARTNER, i) for i in range(FINE)]
    up = [(i, i + FIRST_PARTNER) for i in range(FINE)]

    def swaps(first, last):
        pairs = [(i, i + 1) for i in range(first, last, 2)]
        pairs = [p for p in pairs if p[1] < last]
        return pairs + [(b, a) for a, b in pairs]

    odd_fine, even_fine = swaps(1, FINE), swaps(0, FINE)
    odd_all = odd_fine + swaps(FINE, count)
    even_all = even_fine + swaps(FINE + 1, count)

    coef = (8, CELLS)
    t_rows = FACES * FACE_PAD
    t_shape = (t_rows, WIDTH)
    y_rows = 3 * MODES + 8
    wide_operator = (2 * DENSE, DENSE)
    columns = FACES * CELLS

    loaded = (star, stiffness, upwind, state, inv, elems, faces, proj)
    results = call(
        setup_kernel,
        2 + LOADED,
        [jax.ShapeDtypeStruct(x.shape, x.dtype) for x in loaded]
        + [half(*wide_operator), (QTY * 16, CELLS), PACKED, PACKED, (2 * PACKED[0], CELLS)],
        [FIELD, ROWS, ROWS, t_shape, coef, wide_operator, (t_rows, 192),
         pltpu.SemaphoreType.DMA((LOADED,))],
        (own, dt, *(pltpu.with_memory_space_constraint(x, pltpu.HBM) for x in loaded)),
        20_000_000,
        "setup",
        place=H,
        vmem=SETUP_VMEM,
    )
    (star, stiffness, _, state, inv, elems, faces, proj, dense_op, table, early, second,
     late) = results
    early = lax.ppermute(early, "dom", down)

    flat, w, u, odd, even = call(
        first_kernel,
        6,
        [FIELD, FIELD, FIELD, MESSAGE, MESSAGE],
        [ROWS, ROWS, coef],
        (own, dt, table, state, inv, dense_op),
        2_000_000_000,
        "first",
    )
    total = u
    coarse = None
    for section in range(SUBSTEPS):
        odd_in = lax.ppermute(odd, "dom", odd_all if section == 0 else odd_fine)
        even_in = lax.ppermute(even, "dom", even_all if section == 0 else even_fine)
        if section == 0:
            (
                square_op, star_table, stiff_t, proj_k, lift_m, inside, outside, slots, factor,
                second,
            ) = call(
                prep_kernel,
                12,
                [
                    half(*wide_operator), (3 * QTY * 16, CELLS), half(y_rows, 192),
                    half(t_rows, 192), half(2 * MODES, 2 * t_rows), half(columns, columns),
                    half(columns, columns), half(CELLS, columns), (8, columns),
                    PACKED,
                ],
                [wide_operator, (y_rows, 192), (2 * MODES, 2 * t_rows)],
                (own, counts, dense_op, star, stiffness, proj, lift_w, nb_index, nb_face,
                 elems, faces, second),
                2_000_000_000,
                "prep",
                {11: 9},
                scalars=1,
            )
            second = lax.ppermute(second, "dom", down)
        passed = section == 1
        remote = (early, second, late, late)[section]
        results = call(
            functools.partial(inner_kernel, section),
            13 + passed,
            [FIELD] + [(2 * PACKED[0], CELLS)] * passed,
            [t_shape, (y_rows, WIDTH)],
            (own, flat, w, u, inv, inside, slots, factor, remote, star_table, stiff_t,
             proj_k, lift_m) + (late,) * passed,
            2_000_000_000,
            f"inner{section}",
            {13: 1} if passed else None,
            scalars=1,
        )
        inner = results[0]
        if passed:
            late = lax.ppermute(results[1], "dom", down)
        if section == SUBSTEPS - 1:
            break
        last = section == SUBSTEPS - 2
        flat, w, u, odd, even, total = call(
            functools.partial(outer_kernel, section),
            15,
            [FIELD, FIELD, FIELD, MESSAGE, MESSAGE, PACKED if last else FIELD],
            [FIELD, t_shape, coef],
            (own, dt, table, inner, odd_in, even_in, inv, outside,
             proj_k, lift_m, dense_op, square_op, total, elems, faces),
            2_000_000_000,
            f"outer{section}",
        )
        if section == 0:
            coarse = flat
    arrived = lax.ppermute(total, "dom", up)
    (out,) = call(
        last_kernel,
        11,
        [(QTY, MODES, CELLS)],
        [FIELD, t_shape],
        (own, inner, coarse, odd_in, even_in, inv, outside, proj_k, lift_m, arrived, slots),
        1_000_000_000,
        "last",
        scalars=1,
    )
    return out.transpose(1, 0, 2)


def solution(mesh):
    return jax.shard_map(
        shards,
        mesh=mesh,
        in_specs=(
            P(None, None, "dom"),
            P("dom"),
            P(),
            P(),
            P(),
            P(),
            P(),
            P(),
            P(None, "dom"),
            P(None, "dom"),
            P("dom"),
            P("dom"),
            P(),
        ),
        out_specs=P(None, None, "dom"),
        check_vma=False,
    )
```

```python
import functools

import jax
import jax.numpy as jnp
from jax import lax
from jax.experimental import pallas as pl
from jax.experimental.pallas import tpu as pltpu
from jax.sharding import PartitionSpec as P

TAYLOR = 6
SUBSTEPS = 4
MODES = 56
QTY = 9
FACE_MODES = 21
FACE_PAD = 24
FACES = 4
CELLS = 128
HALF = 64
SLOTS = 32
WIDTH = QTY * CELLS
FINE = 85
FIRST_PARTNER = 256 - FINE
DENSE = 512
PACKED = (56, CELLS)
LOADED = 12

F32 = jnp.float32
BF16 = jnp.bfloat16


def lanes(q, count=1):
    return slice(q * CELLS, (q + count) * CELLS)


def lane_ids(rows):
    return lax.broadcasted_iota(jnp.int32, (rows, CELLS), 1)


def swap_halves(x):
    return pltpu.roll(x, HALF, 1)


def coarse_part(x):
    return x.astype(BF16).astype(F32)


def field_k(x):
    padded = jnp.concatenate([x, jnp.zeros((8, x.shape[1]), F32)], axis=0)
    hi = padded.astype(BF16)
    lo = (padded - hi.astype(F32)).astype(BF16)
    return jnp.concatenate([hi, lo, hi], axis=0)


def dot(a, b):
    return jnp.dot(a, b, preferred_element_type=F32)


def apply_k(weights, field_ref, out_ref, rows):
    for start in range(0, QTY, 2):
        part = lanes(start, min(2, QTY - start))
        out_ref[:rows, part] = dot(weights, field_k(field_ref[:, part]))


def spread_star(star_ref, table_ref):
    for d in range(3):
        entries = star_ref[:, d, :]
        for p in range(QTY):
            row = (d * QTY + p) * 16
            table_ref[row : row + QTY, :] = jnp.broadcast_to(
                entries[:, p : p + 1], (QTY, CELLS)
            )


def spread_upwind(upwind_ref, table_ref):
    entries = upwind_ref[...]
    for p in range(QTY):
        table_ref[p * 16 : p * 16 + QTY, :] = jnp.broadcast_to(
            entries[:, p : p + 1], (QTY, CELLS)
        )


def mix_star(table_ref, y_ref, emit):
    for base in range(0, QTY, 3):
        sums = [None] * 3
        for p in range(QTY):
            for d in range(3):
                y = y_ref[d * MODES : (d + 1) * MODES, lanes(p)]
                for j in range(3):
                    row = (d * QTY + p) * 16 + base + j
                    term = table_ref[row : row + 1, :] * y
                    sums[j] = term if sums[j] is None else sums[j] + term
        for j in range(3):
            emit(base + j, sums[j])


def mix_upwind(table_ref, w_of, emit):
    for base in range(0, QTY, 3):
        sums = [None] * 3
        for p in range(QTY):
            w = w_of(p)
            for j in range(3):
                row = p * 16 + base + j
                term = table_ref[row : row + 1, :] * w
                sums[j] = term if sums[j] is None else sums[j] + term
        for j in range(3):
            emit(base + j, sums[j])


def put_dense(value, base, out_ref):
    hi = coarse_part(value)
    out_ref[base : base + MODES, :] = hi
    out_ref[DENSE + base : DENSE + base + MODES, :] = value - hi


def build_dense(star_ref, stiff_ref, out_ref):
    tiled, scales = [], []
    wide = lax.broadcasted_iota(jnp.int32, (QTY, DENSE), 1)
    for d in range(3):
        block = jnp.concatenate(
            [stiff_ref[d], jnp.zeros((MODES, CELLS - MODES), F32)], axis=1
        )
        columns = []
        for c in range(DENSE // CELLS):
            column = lane_ids(MODES) + c * CELLS
            index = column % MODES
            columns.append(jnp.take_along_axis(block, index, axis=1))
        tiled.append(jnp.concatenate(columns, axis=1))
        entries = star_ref[:, d, :]
        scale = jnp.zeros((QTY, DENSE), F32)
        for p in range(QTY):
            here = (wide >= p * MODES) & (wide < (p + 1) * MODES)
            scale = jnp.where(here, entries[:, p : p + 1], scale)
        scales.append(scale)
    for q in range(QTY):
        value = sum(scales[d][q : q + 1, :] * tiled[d] for d in range(3))
        put_dense(value, q * MODES, out_ref)
    out_ref[QTY * MODES : DENSE, :] = jnp.zeros((8, DENSE), F32)
    out_ref[DENSE + QTY * MODES :, :] = jnp.zeros((8, DENSE), F32)


def dense(weights, rows):
    padded = jnp.concatenate([rows, jnp.zeros((8, CELLS), F32)], axis=0)
    hi = padded.astype(BF16)
    lo = (padded - hi.astype(F32)).astype(BF16)
    both = dot(weights, jnp.concatenate([hi, lo], axis=1))
    top = both[: QTY * MODES]
    return top[:, :CELLS] + (top[:, CELLS:] + both[DENSE : DENSE + QTY * MODES, :CELLS])


def block(rows, q):
    return rows[q * MODES : (q + 1) * MODES]


def predict_five(dense_ref, v_ref, u_ref, coef_ref, inv):
    u_ref[...] = coef_ref[TAYLOR - 1 : TAYLOR, :] * v_ref[...]

    def order(k, carry):
        weight = coef_ref[pl.ds(TAYLOR - 1 - k, 1), :]
        u_ref[...] = weight * v_ref[...] - inv * dense(dense_ref[...], u_ref[...])
        return carry

    lax.fori_loop(1, TAYLOR, order, 0)


def predict_three(dense_ref, square_ref, v, coef_ref, inv):
    c = [coef_ref[k : k + 1, :] for k in range(TAYLOR)]
    two = inv * inv
    u = -inv * dense(dense_ref[...], v)
    top = c[4] * v + c[5] * u
    mid = c[2] * v + c[3] * u + two * dense(square_ref[...], top)
    return c[0] * v + c[1] * u + two * dense(square_ref[...], mid)


def fill_coefs(coef_ref, begin, end):
    b, e, fact = begin, end, 1.0
    for k in range(TAYLOR):
        fact = fact * (k + 1)
        coef_ref[k : k + 1, :] = (e - b) * (1.0 / fact)
        b, e = b * begin, e * end


def put_messages(even, u_of, odd_ref, even_ref):
    def put(row, first, second):
        rows = first.shape[0]
        low = lane_ids(rows) < HALF
        left = jnp.where(low, first, swap_halves(second))
        right = jnp.where(low, swap_halves(first), second)
        odd_ref[row : row + rows, :] = jnp.where(even, left, right)
        even_ref[row : row + rows, :] = jnp.where(even, right, left)

    for j in range(QTY // 2):
        put(j * MODES, u_of(2 * j), u_of(2 * j + 1))
    tail = u_of(QTY - 1)
    put(QTY // 2 * MODES, tail[:32], tail[24:])


def take_messages(even, odd_ref, even_ref, halo_ref):
    def take(row, rows):
        low = lane_ids(rows) < HALF
        a, b = odd_ref[row : row + rows, :], even_ref[row : row + rows, :]
        left = jnp.where(even, a, b)
        right = jnp.where(even, b, a)
        first = jnp.where(low, left, swap_halves(right))
        second = jnp.where(low, swap_halves(left), right)
        return first, second

    for j in range(QTY // 2):
        first, second = take(j * MODES, MODES)
        halo_ref[:, lanes(2 * j)] = first
        halo_ref[:, lanes(2 * j + 1)] = second
    first, second = take(QTY // 2 * MODES, 32)
    halo_ref[:32, lanes(QTY - 1)] = first
    halo_ref[32:, lanes(QTY - 1)] = second[8:]


def pick_matrix(target, rows):
    row = lax.broadcasted_iota(jnp.int32, (rows, CELLS), 0)
    return jnp.concatenate(
        [
            jnp.where(row == target[f : f + 1, :], 1.0, 0.0).astype(BF16)
            for f in range(FACES)
        ],
        axis=1,
    )


def slot_matrix(slot_target, live):
    shape = (CELLS, FACES * CELLS)
    row = lax.broadcasted_iota(jnp.int32, shape, 0) % SLOTS
    column = lax.broadcasted_iota(jnp.int32, shape, 1)
    keep = (column == slot_target) & (row.astype(F32) < live)
    return jnp.where(keep, 1.0, 0.0)


def as_column(row):
    shape = (CELLS, CELLS)
    same = lax.broadcasted_iota(jnp.int32, shape, 0) == lax.broadcasted_iota(
        jnp.int32, shape, 1
    )
    kept = jnp.where(same, row.astype(F32), 0.0)
    return jnp.sum(kept, axis=1, keepdims=True).astype(jnp.int32)


def transposed(x):
    tall = jnp.concatenate([x, jnp.zeros((CELLS - x.shape[0], x.shape[1]), F32)], axis=0)
    full = jnp.concatenate([tall, jnp.zeros((CELLS, CELLS - x.shape[1]), F32)], axis=1)
    return full.T[: x.shape[1]]


def by_quantity(t_ref):
    return jnp.concatenate(
        [
            jnp.concatenate(
                [
                    t_ref[f * FACE_PAD : (f + 1) * FACE_PAD, lanes(q)]
                    for q in range(QTY)
                ],
                axis=0,
            )
            for f in range(FACES)
        ],
        axis=1,
    )


def by_face(g):
    return jnp.concatenate(
        [
            jnp.concatenate(
                [
                    g[q * FACE_PAD : (q + 1) * FACE_PAD, lanes(f)]
                    for f in range(FACES)
                ],
                axis=0,
            )
            for q in range(QTY)
        ],
        axis=1,
    )


def two_parts(x):
    hi = coarse_part(x)
    return jnp.concatenate([hi, x - hi], axis=0).astype(BF16)


def lift(lift_w, stacked):
    both = dot(lift_w, stacked)
    return both[:MODES] + both[MODES:]


def pick_parts(source, matrix):
    return dot(two_parts(source), matrix)


def lift_summed(lift_w, picked):
    rows = QTY * FACE_PAD
    return lift(lift_w, two_parts(by_face(picked[:rows] + picked[rows:])))


def lift_picked(lift_w, picked):
    rows = QTY * FACE_PAD
    stacked = jnp.concatenate([by_face(picked[:rows]), by_face(picked[rows:])], axis=0)
    return lift(lift_w, stacked.astype(BF16))


def slot_traces(u_of, elems, faces, proj, u_ref, t_ref):
    index = jnp.broadcast_to(elems, (MODES, CELLS))
    for q in range(QTY):
        u_ref[:, lanes(q)] = jnp.take_along_axis(u_of(q), index, axis=1)
    return slot_faces(faces, proj, u_ref, t_ref)


def pack_slots(tiles, section, out_ref, base):
    whole = jnp.concatenate(tiles + [jnp.zeros((8, CELLS), F32)], axis=0)
    group = lane_ids(8) // SLOTS
    for j in range(whole.shape[0] // 32):
        total = None
        for g in range(4):
            row = 32 * j + 8 * g
            part = whole[row : row + 8]
            if section is not None and g != section:
                part = pltpu.roll(part, SLOTS * ((g - section) % 4), 1)
            total = part if total is None else jnp.where(group == g, part, total)
        out_ref[base + 8 * j : base + 8 * j + 8, :] = total


def unpack_slots(in_ref, base=0):
    group = lane_ids(8) // SLOTS
    tiles = []
    for j in range(QTY * FACE_PAD // 8):
        row = base + 8 * (j // 4)
        tiles.append(jnp.where(group == j % 4, in_ref[row : row + 8, :], 0.0))
    return jnp.concatenate(tiles, axis=0)


def four_times(row):
    return jnp.concatenate([row] * 4, axis=1)


def slot_faces(faces, proj, u_ref, t_ref):
    apply_k(proj, u_ref, t_ref, FACES * FACE_PAD)
    tiles = []
    for q in range(QTY):
        total = jnp.zeros((FACE_PAD, CELLS), F32)
        for f in range(FACES):
            total = jnp.where(
                faces == f, t_ref[f * FACE_PAD : (f + 1) * FACE_PAD, lanes(q)], total
            )
        tiles.append(total)
    return tiles


def live_slots(own, counts_ref):
    fine = own < FINE
    partner = own >= FIRST_PARTNER
    at = jnp.where(fine, own, jnp.where(partner, own - FIRST_PARTNER, -1))
    place = lax.broadcasted_iota(jnp.int32, (2, CELLS), 0) * CELLS + lane_ids(2)
    mine = jnp.where(place == at, counts_ref[...].astype(F32), 0.0)
    return jnp.sum(jnp.sum(mine, axis=1, keepdims=True), axis=0, keepdims=True)


def put_weights_k(value, row, out_ref):
    hi = coarse_part(value)
    rows = slice(row, row + value.shape[0])
    out_ref[rows, 0:MODES] = hi
    out_ref[rows, 64 : 64 + MODES] = hi
    out_ref[rows, 128 : 128 + MODES] = value - hi


def setup_kernel(*refs):
    own_ref, dt_ref, sources, refs = *refs[:2], refs[2 : 2 + LOADED], refs[2 + LOADED :]
    copies, refs = refs[: LOADED - 1], refs[LOADED - 1 :]
    (
        dense_ref, table_ref, early_ref, late_ref,
        flat_ref, v_ref, u_ref, t_ref, coef_ref, wide_ref, proj_k_ref, upwind_ref, done,
    ) = refs
    moves = [
        pltpu.make_async_copy(source, copy, done.at[i])
        for i, (source, copy) in enumerate(zip(sources, (*copies, upwind_ref)))
    ]
    for move in moves:
        move.start()
    star_ref, stiff_ref, state_ref, inv_ref, elem_ref, face_ref, proj_ref = copies[:7]
    for move in moves[:2]:
        move.wait()
    build_dense(star_ref, stiff_ref, wide_ref)
    dense_ref[...] = wide_ref[...].astype(BF16)
    for move in moves[2:]:
        move.wait()
    spread_upwind(upwind_ref, table_ref)

    @pl.when(own_ref[0] >= FIRST_PARTNER)
    def _():
        proj_k_ref[...] = jnp.zeros_like(proj_k_ref)
        for f in range(FACES):
            put_weights_k(proj_ref[:, f, :], f * FACE_PAD, proj_k_ref)
        elems = four_times(elem_ref[...])
        faces = four_times(face_ref[...])
        index = jnp.broadcast_to(elems, (MODES, CELLS))
        for q in range(QTY):
            v_ref[q * MODES : (q + 1) * MODES, :] = jnp.take_along_axis(
                state_ref[q], index, axis=1
            )
        spread = jnp.broadcast_to(inv_ref[...], (8, CELLS))
        inv = jnp.take_along_axis(spread, index[:8], axis=1)[0:1, :]
        section = (lane_ids(1) // SLOTS).astype(F32)
        substep = jnp.full((1, CELLS), dt_ref[0], F32) * (1.0 / SUBSTEPS)
        fill_coefs(coef_ref, section * substep, (section + 1.0) * substep)
        predict_five(dense_ref, v_ref, u_ref, coef_ref, inv)

        def emit(q, value):
            flat_ref[:, lanes(q)] = value

        mix_upwind(table_ref, lambda q: u_ref[q * MODES : (q + 1) * MODES, :], emit)
        tiles = slot_faces(faces, proj_k_ref[...].astype(BF16), flat_ref, t_ref)
        pack_slots(tiles, 0, early_ref, 0)
        pack_slots(tiles, 1, early_ref, PACKED[0])
        pack_slots(tiles, 2, late_ref, 0)
        pack_slots(tiles, 3, late_ref, PACKED[0])


def uniform_coefs(coef_ref, end):
    fill_coefs(coef_ref, jnp.zeros((1, CELLS), F32), jnp.full((1, CELLS), end, F32))


def first_kernel(
    own_ref, dt_ref, table_ref, state_ref, inv_ref, dense_ref,
    flat_ref, w_ref, u_ref, odd_ref, even_ref, v_ref, sum_ref, coef_ref,
):
    own = own_ref[0]
    for q in range(QTY):
        value = state_ref[q]
        v_ref[q * MODES : (q + 1) * MODES, :] = value
        flat_ref[:, lanes(q)] = value
    dt = dt_ref[0]
    uniform_coefs(coef_ref, jnp.where(own < FINE, dt * (1.0 / SUBSTEPS), dt))
    predict_five(dense_ref, v_ref, sum_ref, coef_ref, inv_ref[...])

    def rows(q):
        return sum_ref[q * MODES : (q + 1) * MODES, :]

    def emit(q, value):
        u_ref[:, lanes(q)] = value

    mix_upwind(table_ref, rows, emit)
    put_messages(own % 2 == 0, lambda q: u_ref[:, lanes(q)], odd_ref, even_ref)
    for q in range(QTY):
        w_ref[:, lanes(q)] = rows(q)


def prep_kernel(
    own_ref, counts_ref, dense_ref, star_ref, stiff_ref, proj_ref, lift_ref, index_ref, face_ref,
    elem_ref, slot_face_ref, square_ref, star_table_ref, stiff_t_ref, proj_k_ref, lift_m_ref,
    inside_ref, outside_ref, slots_ref, factor_ref, wide_ref, k_ref, m_ref,
):
    own = own_ref[0]

    @pl.when(own < FINE)
    def _():
        whole = dense_ref[...]
        top, low = whole[:DENSE], whole[DENSE:]
        both = dot(whole, top)
        square = both[:DENSE] + (both[DENSE:] + dot(top, low))
        hi = coarse_part(square)
        wide_ref[:DENSE, :] = hi
        wide_ref[DENSE:, :] = square - hi
        square_ref[...] = wide_ref[...].astype(BF16)

    spread_star(star_ref, star_table_ref)
    k_ref[...] = jnp.zeros_like(k_ref)
    for f in range(FACES):
        put_weights_k(proj_ref[:, f, :], f * FACE_PAD, k_ref)
    proj_k_ref[...] = k_ref[: FACES * FACE_PAD, :].astype(BF16)
    k_ref[...] = jnp.zeros_like(k_ref)
    for d in range(3):
        put_weights_k(transposed(stiff_ref[d])[:, :MODES], d * MODES, k_ref)
    stiff_t_ref[...] = k_ref[...].astype(BF16)
    m_ref[...] = jnp.zeros_like(m_ref)
    for f in range(FACES):
        value = transposed(lift_ref[:, f, :])[:, :FACE_PAD]
        hi = coarse_part(value)
        for base in (f * FACE_PAD, (FACES + f) * FACE_PAD):
            m_ref[:MODES, base : base + FACE_PAD] = hi
            m_ref[MODES:, base : base + FACE_PAD] = value - hi
    lift_m_ref[...] = m_ref[...].astype(BF16)
    nb, face = index_ref[...], face_ref[...] * CELLS
    inside = (nb >= HALF) & (nb < HALF + CELLS)
    lane = jnp.where(nb < HALF, nb, nb - CELLS)
    inside_ref[...] = pick_matrix(jnp.where(inside, face + nb - HALF, -1), FACES * CELLS)
    outside_ref[...] = pick_matrix(jnp.where(inside, -1, face + lane), FACES * CELLS)
    target = four_times(slot_face_ref[...] * CELLS + elem_ref[...])
    slots = slot_matrix(as_column(target), live_slots(own, counts_ref))
    slots_ref[...] = slots.astype(BF16)
    count = jnp.sum(slots, axis=0, keepdims=True) * 0.25
    factor_ref[...] = jnp.broadcast_to(1.0 + count, factor_ref.shape)


def inner_kernel(
    section, own_ref, state_ref, w_ref, u_ref, inv_ref, inside_ref, factor_ref,
    star_table_ref, stiff_t_ref, proj_ref, lift_ref, *rest,
):
    remote_ref, slots_ref = rest[:2]
    out_ref, t_ref, y_ref = rest[0 if section == 0 else 3 if section == 1 else 2], *rest[-2:]
    own = own_ref[0]

    def work():
        apply_k(proj_ref[...], u_ref, t_ref, FACES * FACE_PAD)
        own_traces = by_quantity(t_ref)
        if section == 0:
            picked = pick_parts(own_traces, inside_ref[...])
        else:
            remote = unpack_slots(remote_ref, PACKED[0] if section != 2 else 0)
            matrix = jnp.concatenate([inside_ref[...], slots_ref[...]], axis=0)
            picked = pick_parts(jnp.concatenate([own_traces, remote], axis=1), matrix)
        rows = QTY * FACE_PAD
        jump = factor_ref[0:1, :] * own_traces - (picked[:rows] + picked[rows:])
        flux = lift(lift_ref[...], two_parts(by_face(jump)))
        apply_k(stiff_t_ref[...], w_ref, y_ref, 3 * MODES + 8)
        inv = inv_ref[...]

        def emit(q, value):
            out_ref[:, lanes(q)] = state_ref[:, lanes(q)] + inv * (value - flux[:, lanes(q)])

        mix_star(star_table_ref, y_ref, emit)

    if section == 0:
        work()
    else:
        pl.when(own < FINE)(work)


def halo_lift(
    own, odd_in, even_in, outside_ref, proj_ref, lift_w, halo_ref, t_ref, extra=None
):
    take_messages(own % 2 == 0, odd_in, even_in, halo_ref)
    apply_k(proj_ref[...], halo_ref, t_ref, FACES * FACE_PAD)
    source, matrix = by_quantity(t_ref), outside_ref[...]
    if extra is None:
        return lift_picked(lift_w, pick_parts(source, matrix))
    source = jnp.concatenate([source, extra[0]], axis=1)
    matrix = jnp.concatenate([matrix, extra[1]], axis=0)
    return lift_summed(lift_w, pick_parts(source, matrix))


def outer_kernel(
    section, own_ref, dt_ref, table_ref, state_ref, odd_in, even_in, inv_ref, outside_ref,
    proj_ref, lift_ref, dense_ref, square_ref, sum_in, *rest,
):
    flat_ref, w_ref, u_ref, odd_ref, even_ref, sum_ref, halo_ref, t_ref, coef_ref = rest[-9:]
    own = own_ref[0]

    def update():
        extra = None
        if section == 0:
            remote_ref, slots_ref = rest[:2]
            extra = (unpack_slots(remote_ref), slots_ref[...])
        gain = halo_lift(
            own, odd_in, even_in, outside_ref, proj_ref, lift_ref[...], halo_ref, t_ref, extra
        )
        inv = inv_ref[...]
        for q in range(QTY):
            flat_ref[:, lanes(q)] = state_ref[:, lanes(q)] + inv * gain[:, lanes(q)]

    if section == 0:
        update()

    @pl.when(own < FINE)
    def _():
        if section > 0:
            update()
        uniform_coefs(coef_ref, dt_ref[0] * (1.0 / SUBSTEPS))
        rows = jnp.concatenate([flat_ref[:, lanes(q)] for q in range(QTY)], axis=0)
        w = predict_three(dense_ref, square_ref, rows, coef_ref, inv_ref[...])
        for q in range(QTY):
            w_ref[:, lanes(q)] = block(w, q)

        def emit(q, value):
            u_ref[:, lanes(q)] = value
            sum_ref[:, lanes(q)] = sum_in[:, lanes(q)] + value

        mix_upwind(table_ref, lambda q: w_ref[:, lanes(q)], emit)
        put_messages(own % 2 == 0, lambda q: u_ref[:, lanes(q)], odd_ref, even_ref)


def up_kernel(
    own_ref, sum_ref, elem_ref, slot_face_ref, proj_ref, factor_in, out_ref, factor_ref, halo_ref, t_ref
):
    @pl.when(own_ref[0] < FINE)
    def _():
        tiles = slot_traces(
            lambda q: sum_ref[:, lanes(q)],
            four_times(elem_ref[...]),
            four_times(slot_face_ref[...]),
            proj_ref[...],
            halo_ref,
            t_ref,
        )
        pack_slots(tiles, None, out_ref, 0)


def last_kernel(
    own_ref, fine_ref, coarse_ref, odd_in, even_in, inv_ref, outside_ref, proj_ref,
    lift_ref, up_ref, slots_ref, out_ref, halo_ref, t_ref,
):
    own = own_ref[0]
    inv = inv_ref[...]

    @pl.when(own < FINE)
    def _():
        gain = halo_lift(
            own, odd_in, even_in, outside_ref, proj_ref, lift_ref[...], halo_ref, t_ref
        )
        for q in range(QTY):
            out_ref[q] = fine_ref[:, lanes(q)] + inv * gain[:, lanes(q)]

    @pl.when(own >= FINE)
    def _():
        picked = pick_parts(unpack_slots(up_ref), slots_ref[...])
        gain = lift_summed(lift_ref[...], picked)
        for q in range(QTY):
            out_ref[q] = coarse_ref[:, lanes(q)] + inv * gain[:, lanes(q)]


S = pl.BlockSpec(memory_space=pltpu.SMEM)
V = pl.BlockSpec(memory_space=pltpu.VMEM)
H = pl.BlockSpec(memory_space=pltpu.HBM)
FIELD = (MODES, WIDTH)
ROWS = (QTY * MODES, CELLS)
MESSAGE = (256, CELLS)


def call(kernel, inputs, outs, scratch, operands, flops, name, aliases=None, place=None, scalars=2):
    shapes = [
        jax.ShapeDtypeStruct(o, F32) if isinstance(o, tuple) else o for o in outs
    ]
    return pl.pallas_call(
        kernel,
        in_specs=[S] * scalars + [place or V] * (inputs - scalars),
        out_specs=[V] * len(outs),
        out_shape=shapes,
        scratch_shapes=[
            pltpu.VMEM(s, F32) if isinstance(s, tuple) else s for s in scratch
        ],
        input_output_aliases=aliases or {},
        compiler_params=pltpu.CompilerParams(vmem_limit_bytes=16 * 1024 * 1024),
        cost_estimate=pl.CostEstimate(
            flops=flops, bytes_accessed=2_000_000, transcendentals=0
        ),
        name=name,
    )(*operands)


def half(*shape):
    return jax.ShapeDtypeStruct(shape, BF16)


def shards(
    modal_state, inv_size, time_step, stiffness, star_matrices, projection, lifting, upwind,
    nb_index, nb_face, iface_elem, iface_face, iface_counts,
):
    own = lax.axis_index("dom").astype(jnp.int32).reshape(1)
    state = modal_state.transpose(1, 0, 2)
    star = star_matrices.transpose(1, 0, 2)
    proj = projection.transpose(1, 0, 2)
    lift_w = lifting.transpose(2, 0, 1)
    dt = time_step.reshape(1)
    inv = inv_size.reshape(1, CELLS)
    elems = iface_elem.reshape(1, SLOTS)
    faces = iface_face.reshape(1, SLOTS)
    counts = iface_counts.reshape(2, CELLS)

    count = lax.axis_size("dom")
    down = [(i + FIRST_PARTNER, i) for i in range(FINE)]
    up = [(i, i + FIRST_PARTNER) for i in range(FINE)]

    def swaps(first, last):
        pairs = [(i, i + 1) for i in range(first, last, 2)]
        pairs = [p for p in pairs if p[1] < last]
        return pairs + [(b, a) for a, b in pairs]

    odd_fine, even_fine = swaps(1, FINE), swaps(0, FINE)
    odd_all = odd_fine + swaps(FINE, count)
    even_all = even_fine + swaps(FINE + 1, count)

    coef = (8, CELLS)
    t_rows = FACES * FACE_PAD
    t_shape = (t_rows, WIDTH)
    y_rows = 3 * MODES + 8
    wide_operator = (2 * DENSE, DENSE)
    columns = FACES * CELLS

    loaded = (star, stiffness, state, inv, elems, faces, proj, lift_w, nb_index, nb_face,
              counts, upwind)
    *copies, dense_op, table, early, late = call(
        setup_kernel,
        2 + LOADED,
        [jax.ShapeDtypeStruct(x.shape, x.dtype) for x in loaded[:-1]]
        + [half(*wide_operator), (QTY * 16, CELLS)]
        + [(2 * PACKED[0], CELLS)] * 2,
        [FIELD, ROWS, ROWS, t_shape, coef, wide_operator, (t_rows, 192), (QTY, QTY),
         pltpu.SemaphoreType.DMA((LOADED,))],
        (own, dt, *(pltpu.with_memory_space_constraint(x, pltpu.HBM) for x in loaded)),
        20_000_000,
        "setup",
        place=H,
    )
    star, stiffness, state, inv, elems, faces, proj, lift_w, nb_index, nb_face, counts = copies
    early = lax.ppermute(early, "dom", down)

    flat, w, u, odd, even = call(
        first_kernel,
        6,
        [FIELD, FIELD, FIELD, MESSAGE, MESSAGE],
        [ROWS, ROWS, coef],
        (own, dt, table, state, inv, dense_op),
        2_000_000_000,
        "first",
    )
    total = u
    coarse = None
    for section in range(SUBSTEPS):
        odd_in = lax.ppermute(odd, "dom", odd_all if section == 0 else odd_fine)
        even_in = lax.ppermute(even, "dom", even_all if section == 0 else even_fine)
        if section == 0:
            (
                square_op, star_table, stiff_t, proj_k, lift_m, inside, outside, slots, factor,
            ) = call(
                prep_kernel,
                11,
                [
                    half(*wide_operator), (3 * QTY * 16, CELLS), half(y_rows, 192),
                    half(t_rows, 192), half(2 * MODES, 2 * t_rows), half(columns, columns),
                    half(columns, columns), half(CELLS, columns), (8, columns),
                ],
                [wide_operator, (y_rows, 192), (2 * MODES, 2 * t_rows)],
                (own, counts, dense_op, star, stiffness, proj, lift_w, nb_index, nb_face,
                 elems, faces),
                2_000_000_000,
                "prep",
                scalars=1,
            )
        if section == SUBSTEPS - 1:
            up_terms, factor = call(
                up_kernel,
                6,
                [PACKED, (8, columns)],
                [FIELD, t_shape],
                (own, total, elems, faces, proj_k, factor),
                2_000_000_000,
                "up",
                {5: 1},
                scalars=1,
            )
            arrived = lax.ppermute(up_terms, "dom", up)
        passed = section == 1
        extra = (() if section == 0 else (early if section == 1 else late, slots))
        results = call(
            functools.partial(inner_kernel, section),
            11 + len(extra) + passed,
            [FIELD] + [(2 * PACKED[0], CELLS)] * passed,
            [t_shape, (y_rows, WIDTH)],
            (own, flat, w, u, inv, inside, factor, star_table, stiff_t, proj_k, lift_m)
            + extra + (late,) * passed,
            2_000_000_000,
            f"inner{section}",
            {13: 1} if passed else None,
            scalars=1,
        )
        inner = results[0]
        if passed:
            late = lax.ppermute(results[1], "dom", down)
        if section == SUBSTEPS - 1:
            break
        extra = (early, slots) if section == 0 else ()
        flat, w, u, odd, even, total = call(
            functools.partial(outer_kernel, section),
            13 + len(extra),
            [FIELD, FIELD, FIELD, MESSAGE, MESSAGE, FIELD],
            [FIELD, t_shape, coef],
            (own, dt, table, inner, odd_in, even_in, inv, outside, proj_k, lift_m, dense_op,
             square_op, total) + extra,
            2_000_000_000,
            f"outer{section}",
        )
        if section == 0:
            coarse = flat
    (out,) = call(
        last_kernel,
        11,
        [(QTY, MODES, CELLS)],
        [FIELD, t_shape],
        (own, inner, coarse, odd_in, even_in, inv, outside, proj_k, lift_m, arrived, slots),
        1_000_000_000,
        "last",
        scalars=1,
    )
    return out.transpose(1, 0, 2)


def solution(mesh):
    return jax.shard_map(
        shards,
        mesh=mesh,
        in_specs=(
            P(None, None, "dom"),
            P("dom"),
            P(),
            P(),
            P(),
            P(),
            P(),
            P(),
            P(None, "dom"),
            P(None, "dom"),
            P("dom"),
            P("dom"),
            P(),
        ),
        out_specs=P(None, None, "dom"),
        check_vma=False,
    )
```

```python
import functools

import jax
import jax.numpy as jnp
from jax import lax
from jax.experimental import pallas as pl
from jax.experimental.pallas import tpu as pltpu
from jax.sharding import PartitionSpec as P

TAYLOR = 6
SUBSTEPS = 4
MODES = 56
QTY = 9
FACE_MODES = 21
FACE_PAD = 24
FACES = 4
CELLS = 128
HALF = 64
SLOTS = 32
WIDTH = QTY * CELLS
FINE = 85
FIRST_PARTNER = 256 - FINE
DENSE = 512
PACKED = (56, CELLS)
LOADED = 12

F32 = jnp.float32
BF16 = jnp.bfloat16


def lanes(q, count=1):
    return slice(q * CELLS, (q + count) * CELLS)


def lane_ids(rows):
    return lax.broadcasted_iota(jnp.int32, (rows, CELLS), 1)


def swap_halves(x):
    return pltpu.roll(x, HALF, 1)


def coarse_part(x):
    return x.astype(BF16).astype(F32)


def field_k(x):
    padded = jnp.concatenate([x, jnp.zeros((8, x.shape[1]), F32)], axis=0)
    hi = padded.astype(BF16)
    lo = (padded - hi.astype(F32)).astype(BF16)
    return jnp.concatenate([hi, lo, hi], axis=0)


def dot(a, b):
    return jnp.dot(a, b, preferred_element_type=F32)


def apply_k(weights, field_ref, out_ref, rows):
    for start in range(0, QTY, 2):
        part = lanes(start, min(2, QTY - start))
        out_ref[:rows, part] = dot(weights, field_k(field_ref[:, part]))


def spread_star(star_ref, table_ref):
    for d in range(3):
        entries = star_ref[:, d, :]
        for p in range(QTY):
            row = (d * QTY + p) * 16
            table_ref[row : row + QTY, :] = jnp.broadcast_to(
                entries[:, p : p + 1], (QTY, CELLS)
            )


def spread_upwind(upwind_ref, table_ref):
    entries = upwind_ref[...]
    for p in range(QTY):
        table_ref[p * 16 : p * 16 + QTY, :] = jnp.broadcast_to(
            entries[:, p : p + 1], (QTY, CELLS)
        )


def mix_star(table_ref, y_ref, emit):
    for base in range(0, QTY, 3):
        sums = [None] * 3
        for p in range(QTY):
            for d in range(3):
                y = y_ref[d * MODES : (d + 1) * MODES, lanes(p)]
                for j in range(3):
                    row = (d * QTY + p) * 16 + base + j
                    term = table_ref[row : row + 1, :] * y
                    sums[j] = term if sums[j] is None else sums[j] + term
        for j in range(3):
            emit(base + j, sums[j])


def mix_upwind(table_ref, w_of, emit):
    for base in range(0, QTY, 3):
        sums = [None] * 3
        for p in range(QTY):
            w = w_of(p)
            for j in range(3):
                row = p * 16 + base + j
                term = table_ref[row : row + 1, :] * w
                sums[j] = term if sums[j] is None else sums[j] + term
        for j in range(3):
            emit(base + j, sums[j])


def put_dense(value, base, out_ref):
    hi = coarse_part(value)
    out_ref[base : base + MODES, :] = hi
    out_ref[DENSE + base : DENSE + base + MODES, :] = value - hi


def build_dense(star_ref, stiff_ref, out_ref):
    tiled, scales = [], []
    wide = lax.broadcasted_iota(jnp.int32, (QTY, DENSE), 1)
    for d in range(3):
        block = jnp.concatenate(
            [stiff_ref[d], jnp.zeros((MODES, CELLS - MODES), F32)], axis=1
        )
        columns = []
        for c in range(DENSE // CELLS):
            column = lane_ids(MODES) + c * CELLS
            index = column % MODES
            columns.append(jnp.take_along_axis(block, index, axis=1))
        tiled.append(jnp.concatenate(columns, axis=1))
        entries = star_ref[:, d, :]
        scale = jnp.zeros((QTY, DENSE), F32)
        for p in range(QTY):
            here = (wide >= p * MODES) & (wide < (p + 1) * MODES)
            scale = jnp.where(here, entries[:, p : p + 1], scale)
        scales.append(scale)
    for q in range(QTY):
        value = sum(scales[d][q : q + 1, :] * tiled[d] for d in range(3))
        put_dense(value, q * MODES, out_ref)
    out_ref[QTY * MODES : DENSE, :] = jnp.zeros((8, DENSE), F32)
    out_ref[DENSE + QTY * MODES :, :] = jnp.zeros((8, DENSE), F32)


def dense(weights_ref, rows):
    padded = jnp.concatenate([rows, jnp.zeros((8, CELLS), F32)], axis=0)
    hi = padded.astype(BF16)
    lo = (padded - hi.astype(F32)).astype(BF16)
    both = dot(weights_ref[:DENSE, :], jnp.concatenate([hi, lo], axis=1))
    low = dot(weights_ref[DENSE:, :], hi)
    return ((both[:, :CELLS] + both[:, CELLS:]) + low)[: QTY * MODES]


def block(rows, q):
    return rows[q * MODES : (q + 1) * MODES]


def predict_five(dense_ref, v_ref, coef_ref, inv):
    u = coef_ref[TAYLOR - 1 : TAYLOR, :] * v_ref[...]
    for k in range(TAYLOR - 2, -1, -1):
        u = coef_ref[k : k + 1, :] * v_ref[...] - inv * dense(dense_ref, u)
    return u


def predict_three(dense_ref, square_ref, v, coef_ref, inv):
    c = [coef_ref[k : k + 1, :] for k in range(TAYLOR)]
    two = inv * inv
    u = -inv * dense(dense_ref, v)
    top = c[4] * v + c[5] * u
    mid = c[2] * v + c[3] * u + two * dense(square_ref, top)
    return c[0] * v + c[1] * u + two * dense(square_ref, mid)


def fill_coefs(coef_ref, begin, end):
    b, e, fact = begin, end, 1.0
    for k in range(TAYLOR):
        fact = fact * (k + 1)
        coef_ref[k : k + 1, :] = (e - b) * (1.0 / fact)
        b, e = b * begin, e * end


def put_messages(even, u_of, odd_ref, even_ref):
    def put(row, first, second):
        rows = first.shape[0]
        low = lane_ids(rows) < HALF
        left = jnp.where(low, first, swap_halves(second))
        right = jnp.where(low, swap_halves(first), second)
        odd_ref[row : row + rows, :] = jnp.where(even, left, right)
        even_ref[row : row + rows, :] = jnp.where(even, right, left)

    for j in range(QTY // 2):
        put(j * MODES, u_of(2 * j), u_of(2 * j + 1))
    tail = u_of(QTY - 1)
    put(QTY // 2 * MODES, tail[:32], tail[24:])


def take_messages(even, odd_ref, even_ref, halo_ref):
    def take(row, rows):
        low = lane_ids(rows) < HALF
        a, b = odd_ref[row : row + rows, :], even_ref[row : row + rows, :]
        left = jnp.where(even, a, b)
        right = jnp.where(even, b, a)
        first = jnp.where(low, left, swap_halves(right))
        second = jnp.where(low, swap_halves(left), right)
        return first, second

    for j in range(QTY // 2):
        first, second = take(j * MODES, MODES)
        halo_ref[:, lanes(2 * j)] = first
        halo_ref[:, lanes(2 * j + 1)] = second
    first, second = take(QTY // 2 * MODES, 32)
    halo_ref[:32, lanes(QTY - 1)] = first
    halo_ref[32:, lanes(QTY - 1)] = second[8:]


def pick_matrix(target, rows):
    row = lax.broadcasted_iota(jnp.int32, (rows, CELLS), 0)
    return jnp.concatenate(
        [
            jnp.where(row == target[f : f + 1, :], 1.0, 0.0).astype(BF16)
            for f in range(FACES)
        ],
        axis=1,
    )


def slot_matrix(slot_target, live):
    shape = (CELLS, FACES * CELLS)
    row = lax.broadcasted_iota(jnp.int32, shape, 0) % SLOTS
    column = lax.broadcasted_iota(jnp.int32, shape, 1)
    keep = (column == slot_target) & (row.astype(F32) < live)
    return jnp.where(keep, 1.0, 0.0)


def as_column(row):
    shape = (CELLS, CELLS)
    same = lax.broadcasted_iota(jnp.int32, shape, 0) == lax.broadcasted_iota(
        jnp.int32, shape, 1
    )
    kept = jnp.where(same, row.astype(F32), 0.0)
    return jnp.sum(kept, axis=1, keepdims=True).astype(jnp.int32)


def transposed(x):
    tall = jnp.concatenate([x, jnp.zeros((CELLS - x.shape[0], x.shape[1]), F32)], axis=0)
    full = jnp.concatenate([tall, jnp.zeros((CELLS, CELLS - x.shape[1]), F32)], axis=1)
    return full.T[: x.shape[1]]


def by_quantity(t_ref):
    return jnp.concatenate(
        [
            jnp.concatenate(
                [
                    t_ref[f * FACE_PAD : (f + 1) * FACE_PAD, lanes(q)]
                    for q in range(QTY)
                ],
                axis=0,
            )
            for f in range(FACES)
        ],
        axis=1,
    )


def by_face(g):
    return jnp.concatenate(
        [
            jnp.concatenate(
                [
                    g[q * FACE_PAD : (q + 1) * FACE_PAD, lanes(f)]
                    for f in range(FACES)
                ],
                axis=0,
            )
            for q in range(QTY)
        ],
        axis=1,
    )


def two_parts(x):
    hi = coarse_part(x)
    return jnp.concatenate([hi, x - hi], axis=0).astype(BF16)


def lift(lift_w, stacked):
    both = dot(lift_w, stacked)
    return both[:MODES] + both[MODES:]


def pick_parts(source, matrix):
    return dot(two_parts(source), matrix)


def lift_summed(lift_w, picked):
    rows = QTY * FACE_PAD
    return lift(lift_w, two_parts(by_face(picked[:rows] + picked[rows:])))


def lift_picked(lift_w, picked):
    rows = QTY * FACE_PAD
    stacked = jnp.concatenate([by_face(picked[:rows]), by_face(picked[rows:])], axis=0)
    return lift(lift_w, stacked.astype(BF16))


def slot_traces(u_of, elems, faces, proj, u_ref, t_ref):
    index = jnp.broadcast_to(elems, (MODES, CELLS))
    for q in range(QTY):
        u_ref[:, lanes(q)] = jnp.take_along_axis(u_of(q), index, axis=1)
    return slot_faces(faces, proj, u_ref, t_ref)


def pack_slots(tiles, section, out_ref, base):
    whole = jnp.concatenate(tiles + [jnp.zeros((8, CELLS), F32)], axis=0)
    group = lane_ids(8) // SLOTS
    for j in range(whole.shape[0] // 32):
        total = None
        for g in range(4):
            row = 32 * j + 8 * g
            part = whole[row : row + 8]
            if section is not None and g != section:
                part = pltpu.roll(part, SLOTS * ((g - section) % 4), 1)
            total = part if total is None else jnp.where(group == g, part, total)
        out_ref[base + 8 * j : base + 8 * j + 8, :] = total


def unpack_slots(in_ref, base=0):
    group = lane_ids(8) // SLOTS
    tiles = []
    for j in range(QTY * FACE_PAD // 8):
        row = base + 8 * (j // 4)
        tiles.append(jnp.where(group == j % 4, in_ref[row : row + 8, :], 0.0))
    return jnp.concatenate(tiles, axis=0)


def four_times(row):
    return jnp.concatenate([row] * 4, axis=1)


def slot_faces(faces, proj, u_ref, t_ref):
    apply_k(proj, u_ref, t_ref, FACES * FACE_PAD)
    tiles = []
    for q in range(QTY):
        total = jnp.zeros((FACE_PAD, CELLS), F32)
        for f in range(FACES):
            total = jnp.where(
                faces == f, t_ref[f * FACE_PAD : (f + 1) * FACE_PAD, lanes(q)], total
            )
        tiles.append(total)
    return tiles


def live_slots(own, counts_ref):
    fine = own < FINE
    partner = own >= FIRST_PARTNER
    at = jnp.where(fine, own, jnp.where(partner, own - FIRST_PARTNER, -1))
    place = lax.broadcasted_iota(jnp.int32, (2, CELLS), 0) * CELLS + lane_ids(2)
    mine = jnp.where(place == at, counts_ref[...].astype(F32), 0.0)
    return jnp.sum(jnp.sum(mine, axis=1, keepdims=True), axis=0, keepdims=True)


def put_weights_k(value, row, out_ref):
    hi = coarse_part(value)
    rows = slice(row, row + value.shape[0])
    out_ref[rows, 0:MODES] = hi
    out_ref[rows, 64 : 64 + MODES] = hi
    out_ref[rows, 128 : 128 + MODES] = value - hi


def setup_kernel(*refs):
    own_ref, dt_ref, sources, refs = *refs[:2], refs[2 : 2 + LOADED], refs[2 + LOADED :]
    copies, refs = refs[: LOADED - 1], refs[LOADED - 1 :]
    (
        dense_ref, table_ref, early_ref, late_ref,
        flat_ref, v_ref, u_ref, t_ref, coef_ref, wide_ref, proj_k_ref, upwind_ref, done,
    ) = refs
    moves = [
        pltpu.make_async_copy(source, copy, done.at[i])
        for i, (source, copy) in enumerate(zip(sources, (*copies, upwind_ref)))
    ]
    for move in moves:
        move.start()
    star_ref, stiff_ref, state_ref, inv_ref, elem_ref, face_ref, proj_ref = copies[:7]
    for move in moves[:2]:
        move.wait()
    build_dense(star_ref, stiff_ref, wide_ref)
    dense_ref[...] = wide_ref[...].astype(BF16)
    for move in moves[2:]:
        move.wait()
    spread_upwind(upwind_ref, table_ref)

    @pl.when(own_ref[0] >= FIRST_PARTNER)
    def _():
        proj_k_ref[...] = jnp.zeros_like(proj_k_ref)
        for f in range(FACES):
            put_weights_k(proj_ref[:, f, :], f * FACE_PAD, proj_k_ref)
        elems = four_times(elem_ref[...])
        faces = four_times(face_ref[...])
        index = jnp.broadcast_to(elems, (MODES, CELLS))
        for q in range(QTY):
            v_ref[q * MODES : (q + 1) * MODES, :] = jnp.take_along_axis(
                state_ref[q], index, axis=1
            )
        spread = jnp.broadcast_to(inv_ref[...], (8, CELLS))
        inv = jnp.take_along_axis(spread, index[:8], axis=1)[0:1, :]
        section = (lane_ids(1) // SLOTS).astype(F32)
        substep = jnp.full((1, CELLS), dt_ref[0], F32) * (1.0 / SUBSTEPS)
        fill_coefs(coef_ref, section * substep, (section + 1.0) * substep)
        u_ref[...] = predict_five(dense_ref, v_ref, coef_ref, inv)

        def emit(q, value):
            flat_ref[:, lanes(q)] = value

        mix_upwind(table_ref, lambda q: u_ref[q * MODES : (q + 1) * MODES, :], emit)
        tiles = slot_faces(faces, proj_k_ref[...].astype(BF16), flat_ref, t_ref)
        pack_slots(tiles, 0, early_ref, 0)
        pack_slots(tiles, 1, early_ref, PACKED[0])
        pack_slots(tiles, 2, late_ref, 0)
        pack_slots(tiles, 3, late_ref, PACKED[0])


def uniform_coefs(coef_ref, end):
    fill_coefs(coef_ref, jnp.zeros((1, CELLS), F32), jnp.full((1, CELLS), end, F32))


def first_kernel(
    own_ref, dt_ref, table_ref, state_ref, inv_ref, dense_ref,
    flat_ref, w_ref, u_ref, odd_ref, even_ref, v_ref, sum_ref, coef_ref,
):
    own = own_ref[0]
    for q in range(QTY):
        value = state_ref[q]
        v_ref[q * MODES : (q + 1) * MODES, :] = value
        flat_ref[:, lanes(q)] = value
    dt = dt_ref[0]
    uniform_coefs(coef_ref, jnp.where(own < FINE, dt * (1.0 / SUBSTEPS), dt))
    sum_ref[...] = predict_five(dense_ref, v_ref, coef_ref, inv_ref[...])

    def rows(q):
        return sum_ref[q * MODES : (q + 1) * MODES, :]

    def emit(q, value):
        u_ref[:, lanes(q)] = value

    mix_upwind(table_ref, rows, emit)
    put_messages(own % 2 == 0, lambda q: u_ref[:, lanes(q)], odd_ref, even_ref)
    for q in range(QTY):
        w_ref[:, lanes(q)] = rows(q)


def prep_kernel(
    own_ref, counts_ref, dense_ref, star_ref, stiff_ref, proj_ref, lift_ref, index_ref, face_ref,
    elem_ref, slot_face_ref, square_ref, star_table_ref, stiff_t_ref, proj_k_ref, lift_m_ref,
    inside_ref, outside_ref, slots_ref, factor_ref, wide_ref, k_ref, m_ref,
):
    own = own_ref[0]

    @pl.when(own < FINE)
    def _():
        whole = dense_ref[...]
        top, low = whole[:DENSE], whole[DENSE:]
        both = dot(whole, top)
        square = both[:DENSE] + (both[DENSE:] + dot(top, low))
        hi = coarse_part(square)
        wide_ref[:DENSE, :] = hi
        wide_ref[DENSE:, :] = square - hi
        square_ref[...] = wide_ref[...].astype(BF16)

    spread_star(star_ref, star_table_ref)
    k_ref[...] = jnp.zeros_like(k_ref)
    for f in range(FACES):
        put_weights_k(proj_ref[:, f, :], f * FACE_PAD, k_ref)
    proj_k_ref[...] = k_ref[: FACES * FACE_PAD, :].astype(BF16)
    k_ref[...] = jnp.zeros_like(k_ref)
    for d in range(3):
        put_weights_k(transposed(stiff_ref[d])[:, :MODES], d * MODES, k_ref)
    stiff_t_ref[...] = k_ref[...].astype(BF16)
    m_ref[...] = jnp.zeros_like(m_ref)
    for f in range(FACES):
        value = transposed(lift_ref[:, f, :])[:, :FACE_PAD]
        hi = coarse_part(value)
        for base in (f * FACE_PAD, (FACES + f) * FACE_PAD):
            m_ref[:MODES, base : base + FACE_PAD] = hi
            m_ref[MODES:, base : base + FACE_PAD] = value - hi
    lift_m_ref[...] = m_ref[...].astype(BF16)
    nb, face = index_ref[...], face_ref[...] * CELLS
    inside = (nb >= HALF) & (nb < HALF + CELLS)
    lane = jnp.where(nb < HALF, nb, nb - CELLS)
    inside_ref[...] = pick_matrix(jnp.where(inside, face + nb - HALF, -1), FACES * CELLS)
    outside_ref[...] = pick_matrix(jnp.where(inside, -1, face + lane), FACES * CELLS)
    target = four_times(slot_face_ref[...] * CELLS + elem_ref[...])
    slots = slot_matrix(as_column(target), live_slots(own, counts_ref))
    slots_ref[...] = slots.astype(BF16)
    count = jnp.sum(slots, axis=0, keepdims=True) * 0.25
    factor_ref[...] = jnp.broadcast_to(1.0 + count, factor_ref.shape)


def inner_kernel(
    section, own_ref, state_ref, w_ref, u_ref, inv_ref, inside_ref, factor_ref,
    star_table_ref, stiff_t_ref, proj_ref, lift_ref, *rest,
):
    remote_ref, slots_ref = rest[:2]
    out_ref, t_ref, y_ref = rest[0 if section == 0 else 3 if section == 1 else 2], *rest[-2:]
    own = own_ref[0]

    def work():
        apply_k(proj_ref[...], u_ref, t_ref, FACES * FACE_PAD)
        own_traces = by_quantity(t_ref)
        if section == 0:
            picked = pick_parts(own_traces, inside_ref[...])
        else:
            remote = unpack_slots(remote_ref, PACKED[0] if section != 2 else 0)
            matrix = jnp.concatenate([inside_ref[...], slots_ref[...]], axis=0)
            picked = pick_parts(jnp.concatenate([own_traces, remote], axis=1), matrix)
        rows = QTY * FACE_PAD
        jump = factor_ref[0:1, :] * own_traces - (picked[:rows] + picked[rows:])
        flux = lift(lift_ref[...], two_parts(by_face(jump)))
        apply_k(stiff_t_ref[...], w_ref, y_ref, 3 * MODES + 8)
        inv = inv_ref[...]

        def emit(q, value):
            out_ref[:, lanes(q)] = state_ref[:, lanes(q)] + inv * (value - flux[:, lanes(q)])

        mix_star(star_table_ref, y_ref, emit)

    if section == 0:
        work()
    else:
        pl.when(own < FINE)(work)


def halo_lift(
    own, odd_in, even_in, outside_ref, proj_ref, lift_w, halo_ref, t_ref, extra=None
):
    take_messages(own % 2 == 0, odd_in, even_in, halo_ref)
    apply_k(proj_ref[...], halo_ref, t_ref, FACES * FACE_PAD)
    source, matrix = by_quantity(t_ref), outside_ref[...]
    if extra is None:
        return lift_picked(lift_w, pick_parts(source, matrix))
    source = jnp.concatenate([source, extra[0]], axis=1)
    matrix = jnp.concatenate([matrix, extra[1]], axis=0)
    return lift_summed(lift_w, pick_parts(source, matrix))


def outer_kernel(
    section, own_ref, dt_ref, table_ref, state_ref, odd_in, even_in, inv_ref, outside_ref,
    proj_ref, lift_ref, dense_ref, square_ref, sum_in, *rest,
):
    flat_ref, w_ref, u_ref, odd_ref, even_ref, sum_ref, halo_ref, t_ref, coef_ref = rest[-9:]
    own = own_ref[0]

    def update():
        extra = None
        if section == 0:
            remote_ref, slots_ref = rest[:2]
            extra = (unpack_slots(remote_ref), slots_ref[...])
        gain = halo_lift(
            own, odd_in, even_in, outside_ref, proj_ref, lift_ref[...], halo_ref, t_ref, extra
        )
        inv = inv_ref[...]
        for q in range(QTY):
            flat_ref[:, lanes(q)] = state_ref[:, lanes(q)] + inv * gain[:, lanes(q)]

    if section == 0:
        update()

    @pl.when(own < FINE)
    def _():
        if section > 0:
            update()
        uniform_coefs(coef_ref, dt_ref[0] * (1.0 / SUBSTEPS))
        rows = jnp.concatenate([flat_ref[:, lanes(q)] for q in range(QTY)], axis=0)
        w = predict_three(dense_ref, square_ref, rows, coef_ref, inv_ref[...])
        for q in range(QTY):
            w_ref[:, lanes(q)] = block(w, q)

        def emit(q, value):
            u_ref[:, lanes(q)] = value
            sum_ref[:, lanes(q)] = sum_in[:, lanes(q)] + value

        mix_upwind(table_ref, lambda q: w_ref[:, lanes(q)], emit)
        put_messages(own % 2 == 0, lambda q: u_ref[:, lanes(q)], odd_ref, even_ref)


def up_kernel(
    own_ref, sum_ref, elem_ref, slot_face_ref, proj_ref, factor_in, out_ref, factor_ref, halo_ref, t_ref
):
    @pl.when(own_ref[0] < FINE)
    def _():
        tiles = slot_traces(
            lambda q: sum_ref[:, lanes(q)],
            four_times(elem_ref[...]),
            four_times(slot_face_ref[...]),
            proj_ref[...],
            halo_ref,
            t_ref,
        )
        pack_slots(tiles, None, out_ref, 0)


def last_kernel(
    own_ref, fine_ref, coarse_ref, odd_in, even_in, inv_ref, outside_ref, proj_ref,
    lift_ref, up_ref, slots_ref, out_ref, halo_ref, t_ref, rows_ref, done,
):
    own = own_ref[0]
    inv = inv_ref[...]

    def write(base_ref, gain):
        moves = []
        for q in range(QTY):
            rows_ref[q] = base_ref[:, lanes(q)] + inv * gain[:, lanes(q)]
            moves.append(pltpu.make_async_copy(rows_ref.at[q], out_ref.at[q], done.at[q]))
            moves[q].start()
        for move in moves:
            move.wait()

    @pl.when(own < FINE)
    def _():
        gain = halo_lift(
            own, odd_in, even_in, outside_ref, proj_ref, lift_ref[...], halo_ref, t_ref
        )
        write(fine_ref, gain)

    @pl.when(own >= FINE)
    def _():
        picked = pick_parts(unpack_slots(up_ref), slots_ref[...])
        write(coarse_ref, lift_summed(lift_ref[...], picked))


S = pl.BlockSpec(memory_space=pltpu.SMEM)
V = pl.BlockSpec(memory_space=pltpu.VMEM)
H = pl.BlockSpec(memory_space=pltpu.HBM)
FIELD = (MODES, WIDTH)
ROWS = (QTY * MODES, CELLS)
MESSAGE = (256, CELLS)


def call(kernel, inputs, outs, scratch, operands, flops, name, aliases=None, place=None, scalars=2, out_place=V):
    shapes = [
        jax.ShapeDtypeStruct(o, F32) if isinstance(o, tuple) else o for o in outs
    ]
    return pl.pallas_call(
        kernel,
        in_specs=[S] * scalars + [place or V] * (inputs - scalars),
        out_specs=[out_place] * len(outs),
        out_shape=shapes,
        scratch_shapes=[
            pltpu.VMEM(s, F32) if isinstance(s, tuple) else s for s in scratch
        ],
        input_output_aliases=aliases or {},
        compiler_params=pltpu.CompilerParams(vmem_limit_bytes=16 * 1024 * 1024),
        cost_estimate=pl.CostEstimate(
            flops=flops, bytes_accessed=2_000_000, transcendentals=0
        ),
        name=name,
    )(*operands)


def half(*shape):
    return jax.ShapeDtypeStruct(shape, BF16)


def shards(
    modal_state, inv_size, time_step, stiffness, star_matrices, projection, lifting, upwind,
    nb_index, nb_face, iface_elem, iface_face, iface_counts,
):
    own = lax.axis_index("dom").astype(jnp.int32).reshape(1)
    state = modal_state.transpose(1, 0, 2)
    star = star_matrices.transpose(1, 0, 2)
    proj = projection.transpose(1, 0, 2)
    lift_w = lifting.transpose(2, 0, 1)
    dt = time_step.reshape(1)
    inv = inv_size.reshape(1, CELLS)
    elems = iface_elem.reshape(1, SLOTS)
    faces = iface_face.reshape(1, SLOTS)
    counts = iface_counts.reshape(2, CELLS)

    count = lax.axis_size("dom")
    down = [(i + FIRST_PARTNER, i) for i in range(FINE)]
    up = [(i, i + FIRST_PARTNER) for i in range(FINE)]

    def swaps(first, last):
        pairs = [(i, i + 1) for i in range(first, last, 2)]
        pairs = [p for p in pairs if p[1] < last]
        return pairs + [(b, a) for a, b in pairs]

    odd_fine, even_fine = swaps(1, FINE), swaps(0, FINE)
    odd_all = odd_fine + swaps(FINE, count)
    even_all = even_fine + swaps(FINE + 1, count)

    coef = (8, CELLS)
    t_rows = FACES * FACE_PAD
    t_shape = (t_rows, WIDTH)
    y_rows = 3 * MODES + 8
    wide_operator = (2 * DENSE, DENSE)
    columns = FACES * CELLS

    loaded = (star, stiffness, state, inv, elems, faces, proj, lift_w, nb_index, nb_face,
              counts, upwind)
    *copies, dense_op, table, early, late = call(
        setup_kernel,
        2 + LOADED,
        [jax.ShapeDtypeStruct(x.shape, x.dtype) for x in loaded[:-1]]
        + [half(*wide_operator), (QTY * 16, CELLS)]
        + [(2 * PACKED[0], CELLS)] * 2,
        [FIELD, ROWS, ROWS, t_shape, coef, wide_operator, (t_rows, 192), (QTY, QTY),
         pltpu.SemaphoreType.DMA((LOADED,))],
        (own, dt, *(pltpu.with_memory_space_constraint(x, pltpu.HBM) for x in loaded)),
        20_000_000,
        "setup",
        place=H,
    )
    star, stiffness, state, inv, elems, faces, proj, lift_w, nb_index, nb_face, counts = copies
    early = lax.ppermute(early, "dom", down)

    flat, w, u, odd, even = call(
        first_kernel,
        6,
        [FIELD, FIELD, FIELD, MESSAGE, MESSAGE],
        [ROWS, ROWS, coef],
        (own, dt, table, state, inv, dense_op),
        2_000_000_000,
        "first",
    )
    total = u
    coarse = None
    for section in range(SUBSTEPS):
        odd_in = lax.ppermute(odd, "dom", odd_all if section == 0 else odd_fine)
        even_in = lax.ppermute(even, "dom", even_all if section == 0 else even_fine)
        if section == 0:
            (
                square_op, star_table, stiff_t, proj_k, lift_m, inside, outside, slots, factor,
            ) = call(
                prep_kernel,
                11,
                [
                    half(*wide_operator), (3 * QTY * 16, CELLS), half(y_rows, 192),
                    half(t_rows, 192), half(2 * MODES, 2 * t_rows), half(columns, columns),
                    half(columns, columns), half(CELLS, columns), (8, columns),
                ],
                [wide_operator, (y_rows, 192), (2 * MODES, 2 * t_rows)],
                (own, counts, dense_op, star, stiffness, proj, lift_w, nb_index, nb_face,
                 elems, faces),
                2_000_000_000,
                "prep",
                scalars=1,
            )
        if section == SUBSTEPS - 1:
            up_terms, factor = call(
                up_kernel,
                6,
                [PACKED, (8, columns)],
                [FIELD, t_shape],
                (own, total, elems, faces, proj_k, factor),
                2_000_000_000,
                "up",
                {5: 1},
                scalars=1,
            )
            arrived = lax.ppermute(up_terms, "dom", up)
        passed = section == 1
        extra = (() if section == 0 else (early if section == 1 else late, slots))
        results = call(
            functools.partial(inner_kernel, section),
            11 + len(extra) + passed,
            [FIELD] + [(2 * PACKED[0], CELLS)] * passed,
            [t_shape, (y_rows, WIDTH)],
            (own, flat, w, u, inv, inside, factor, star_table, stiff_t, proj_k, lift_m)
            + extra + (late,) * passed,
            2_000_000_000,
            f"inner{section}",
            {13: 1} if passed else None,
            scalars=1,
        )
        inner = results[0]
        if passed:
            late = lax.ppermute(results[1], "dom", down)
        if section == SUBSTEPS - 1:
            break
        extra = (early, slots) if section == 0 else ()
        flat, w, u, odd, even, total = call(
            functools.partial(outer_kernel, section),
            13 + len(extra),
            [FIELD, FIELD, FIELD, MESSAGE, MESSAGE, FIELD],
            [FIELD, t_shape, coef],
            (own, dt, table, inner, odd_in, even_in, inv, outside, proj_k, lift_m, dense_op,
             square_op, total) + extra,
            2_000_000_000,
            f"outer{section}",
        )
        if section == 0:
            coarse = flat
    (out,) = call(
        last_kernel,
        11,
        [pltpu.HBM((QTY, MODES, CELLS), F32)],
        [FIELD, t_shape, (QTY, MODES, CELLS), pltpu.SemaphoreType.DMA((QTY,))],
        (own, inner, coarse, odd_in, even_in, inv, outside, proj_k, lift_m, arrived, slots),
        1_000_000_000,
        "last",
        scalars=1,
        out_place=H,
    )
    return out.transpose(1, 0, 2)


def solution(mesh):
    return jax.shard_map(
        shards,
        mesh=mesh,
        in_specs=(
            P(None, None, "dom"),
            P("dom"),
            P(),
            P(),
            P(),
            P(),
            P(),
            P(),
            P(None, "dom"),
            P(None, "dom"),
            P("dom"),
            P("dom"),
            P(),
        ),
        out_specs=P(None, None, "dom"),
        check_vma=False,
    )
```

```python
import functools

import jax
import jax.numpy as jnp
from jax import lax
from jax.experimental import pallas as pl
from jax.experimental.pallas import tpu as pltpu
from jax.sharding import PartitionSpec as P

TAYLOR = 6
SUBSTEPS = 4
MODES = 56
QTY = 9
FACE_MODES = 21
FACE_PAD = 24
FACES = 4
CELLS = 128
HALF = 64
SLOTS = 32
WIDTH = QTY * CELLS
FINE = 85
FIRST_PARTNER = 256 - FINE
DENSE = 512
PACKED = (56, CELLS)
LOADED = 12

F32 = jnp.float32
BF16 = jnp.bfloat16


def lanes(q, count=1):
    return slice(q * CELLS, (q + count) * CELLS)


def lane_ids(rows):
    return lax.broadcasted_iota(jnp.int32, (rows, CELLS), 1)


def swap_halves(x):
    return pltpu.roll(x, HALF, 1)


def coarse_part(x):
    return x.astype(BF16).astype(F32)


def field_k(x):
    padded = jnp.concatenate([x, jnp.zeros((8, x.shape[1]), F32)], axis=0)
    hi = padded.astype(BF16)
    lo = (padded - hi.astype(F32)).astype(BF16)
    return jnp.concatenate([hi, lo, hi], axis=0)


def dot(a, b):
    return jnp.dot(a, b, preferred_element_type=F32)


def apply_k(weights, field_ref, out_ref, rows):
    for start in range(0, QTY, 2):
        part = lanes(start, min(2, QTY - start))
        out_ref[:rows, part] = dot(weights, field_k(field_ref[:, part]))


def spread_upwind(upwind_ref, table_ref):
    entries = upwind_ref[...]
    for p in range(QTY):
        table_ref[p * 16 : p * 16 + QTY, :] = jnp.broadcast_to(
            entries[:, p : p + 1], (QTY, CELLS)
        )


def mix_upwind(table_ref, w_of, emit):
    for base in range(0, QTY, 3):
        sums = [None] * 3
        for p in range(QTY):
            w = w_of(p)
            for j in range(3):
                row = p * 16 + base + j
                term = table_ref[row : row + 1, :] * w
                sums[j] = term if sums[j] is None else sums[j] + term
        for j in range(3):
            emit(base + j, sums[j])


def put_dense(value, base, out_ref):
    rows = value.shape[0]
    hi = value.astype(BF16)
    out_ref[base : base + rows, :] = hi
    out_ref[DENSE + base : DENSE + base + rows, :] = (value - hi.astype(F32)).astype(BF16)


def put_scales(star_ref, out_ref):
    wide = lax.broadcasted_iota(jnp.int32, (QTY, DENSE), 1)
    for d in range(3):
        entries = star_ref[:, d, :]
        scale = jnp.zeros((QTY, DENSE), F32)
        for p in range(QTY):
            here = (wide >= p * MODES) & (wide < (p + 1) * MODES)
            scale = jnp.where(here, entries[:, p : p + 1], scale)
        out_ref[16 * d : 16 * d + QTY, :] = scale


def build_dense(scales_ref, blocks, out_ref):
    tiled = []
    for d in range(3):
        columns = []
        for c in range(DENSE // CELLS):
            column = lane_ids(MODES) + c * CELLS
            columns.append(jnp.take_along_axis(blocks[d], column % MODES, axis=1))
        tiled.append(jnp.concatenate(columns, axis=1))

    def rows(q):
        return sum(scales_ref[16 * d + q : 16 * d + q + 1, :] * tiled[d] for d in range(3))

    for q in range(0, QTY - 1, 2):
        put_dense(jnp.concatenate([rows(q), rows(q + 1)], axis=0), q * MODES, out_ref)
    tail = jnp.concatenate([rows(QTY - 1), jnp.zeros((8, DENSE), F32)], axis=0)
    put_dense(tail, (QTY - 1) * MODES, out_ref)


def dense(weights_ref, rows):
    padded = jnp.concatenate([rows, jnp.zeros((8, CELLS), F32)], axis=0)
    hi = padded.astype(BF16)
    lo = (padded - hi.astype(F32)).astype(BF16)
    both = dot(weights_ref[:DENSE, :], jnp.concatenate([hi, lo], axis=1))
    low = dot(weights_ref[DENSE:, :], hi)
    return ((both[:, :CELLS] + both[:, CELLS:]) + low)[: QTY * MODES]


def block(rows, q):
    return rows[q * MODES : (q + 1) * MODES]


def predict_five(dense_ref, v_ref, coef_ref, inv):
    u = coef_ref[TAYLOR - 1 : TAYLOR, :] * v_ref[...]
    for k in range(TAYLOR - 2, -1, -1):
        u = coef_ref[k : k + 1, :] * v_ref[...] - inv * dense(dense_ref, u)
    return u


def predict_three(dense_ref, square_ref, v, coef_ref, inv):
    c = [coef_ref[k : k + 1, :] for k in range(TAYLOR)]
    two = inv * inv
    u = -inv * dense(dense_ref, v)
    top = c[4] * v + c[5] * u
    mid = c[2] * v + c[3] * u + two * dense(square_ref, top)
    return c[0] * v + c[1] * u + two * dense(square_ref, mid)


def fill_coefs(coef_ref, begin, end):
    b, e, fact = begin, end, 1.0
    for k in range(TAYLOR):
        fact = fact * (k + 1)
        coef_ref[k : k + 1, :] = (e - b) * (1.0 / fact)
        b, e = b * begin, e * end


def put_messages(even, u_of, odd_ref, even_ref):
    def put(row, first, second):
        rows = first.shape[0]
        low = lane_ids(rows) < HALF
        left = jnp.where(low, first, swap_halves(second))
        right = jnp.where(low, swap_halves(first), second)
        odd_ref[row : row + rows, :] = jnp.where(even, left, right)
        even_ref[row : row + rows, :] = jnp.where(even, right, left)

    for j in range(QTY // 2):
        put(j * MODES, u_of(2 * j), u_of(2 * j + 1))
    tail = u_of(QTY - 1)
    put(QTY // 2 * MODES, tail[:32], tail[24:])


def take_messages(even, odd_ref, even_ref, halo_ref):
    def take(row, rows):
        low = lane_ids(rows) < HALF
        a, b = odd_ref[row : row + rows, :], even_ref[row : row + rows, :]
        left = jnp.where(even, a, b)
        right = jnp.where(even, b, a)
        first = jnp.where(low, left, swap_halves(right))
        second = jnp.where(low, swap_halves(left), right)
        return first, second

    for j in range(QTY // 2):
        first, second = take(j * MODES, MODES)
        halo_ref[:, lanes(2 * j)] = first
        halo_ref[:, lanes(2 * j + 1)] = second
    first, second = take(QTY // 2 * MODES, 32)
    halo_ref[:32, lanes(QTY - 1)] = first
    halo_ref[32:, lanes(QTY - 1)] = second[8:]


def pick_matrix(target, rows):
    row = lax.broadcasted_iota(jnp.int32, (rows, CELLS), 0)
    return jnp.concatenate(
        [
            jnp.where(row == target[f : f + 1, :], 1.0, 0.0).astype(BF16)
            for f in range(FACES)
        ],
        axis=1,
    )


def slot_matrix(slot_target, live):
    shape = (CELLS, FACES * CELLS)
    row = lax.broadcasted_iota(jnp.int32, shape, 0) % SLOTS
    column = lax.broadcasted_iota(jnp.int32, shape, 1)
    keep = (column == slot_target) & (row.astype(F32) < live)
    return jnp.where(keep, 1.0, 0.0)


def as_column(row):
    shape = (CELLS, CELLS)
    same = lax.broadcasted_iota(jnp.int32, shape, 0) == lax.broadcasted_iota(
        jnp.int32, shape, 1
    )
    kept = jnp.where(same, row.astype(F32), 0.0)
    return jnp.sum(kept, axis=1, keepdims=True).astype(jnp.int32)


def by_quantity(t_ref):
    return jnp.concatenate(
        [
            jnp.concatenate(
                [
                    t_ref[f * FACE_PAD : (f + 1) * FACE_PAD, lanes(q)]
                    for q in range(QTY)
                ],
                axis=0,
            )
            for f in range(FACES)
        ],
        axis=1,
    )


def by_face(g):
    return jnp.concatenate(
        [
            jnp.concatenate(
                [
                    g[q * FACE_PAD : (q + 1) * FACE_PAD, lanes(f)]
                    for f in range(FACES)
                ],
                axis=0,
            )
            for q in range(QTY)
        ],
        axis=1,
    )


def two_parts(x):
    hi = coarse_part(x)
    return jnp.concatenate([hi, x - hi], axis=0).astype(BF16)


def lift(lift_w, stacked):
    both = dot(lift_w, stacked)
    return both[:MODES] + both[MODES:]


def pick_parts(source, matrix):
    return dot(two_parts(source), matrix)


def stack_sums(picked):
    rows = QTY * FACE_PAD
    return two_parts(by_face(picked[:rows] + picked[rows:]))


def stack_parts(picked):
    rows = QTY * FACE_PAD
    return jnp.concatenate([by_face(picked[:rows]), by_face(picked[rows:])], axis=0).astype(BF16)


def pack_slots(tiles, section, out_ref, base):
    whole = jnp.concatenate(tiles + [jnp.zeros((8, CELLS), F32)], axis=0)
    group = lane_ids(8) // SLOTS
    for j in range(whole.shape[0] // 32):
        total = None
        for g in range(4):
            row = 32 * j + 8 * g
            part = whole[row : row + 8]
            if section is not None and g != section:
                part = pltpu.roll(part, SLOTS * ((g - section) % 4), 1)
            total = part if total is None else jnp.where(group == g, part, total)
        out_ref[base + 8 * j : base + 8 * j + 8, :] = total


def unpack_slots(in_ref, base=0):
    group = lane_ids(8) // SLOTS
    tiles = []
    for j in range(QTY * FACE_PAD // 8):
        row = base + 8 * (j // 4)
        tiles.append(jnp.where(group == j % 4, in_ref[row : row + 8, :], 0.0))
    return jnp.concatenate(tiles, axis=0)


def four_times(row):
    return jnp.concatenate([row] * 4, axis=1)


def slot_faces(faces, proj, u_ref, t_ref):
    apply_k(proj, u_ref, t_ref, FACES * FACE_PAD)
    tiles = []
    for q in range(QTY):
        total = jnp.zeros((FACE_PAD, CELLS), F32)
        for f in range(FACES):
            total = jnp.where(
                faces == f, t_ref[f * FACE_PAD : (f + 1) * FACE_PAD, lanes(q)], total
            )
        tiles.append(total)
    return tiles


def live_slots(own, counts_ref):
    fine = own < FINE
    partner = own >= FIRST_PARTNER
    at = jnp.where(fine, own, jnp.where(partner, own - FIRST_PARTNER, -1))
    place = lax.broadcasted_iota(jnp.int32, (2, CELLS), 0) * CELLS + lane_ids(2)
    mine = jnp.where(place == at, counts_ref[...].astype(F32), 0.0)
    return jnp.sum(jnp.sum(mine, axis=1, keepdims=True), axis=0, keepdims=True)


def put_weights_k(value, row, out_ref):
    hi = coarse_part(value)
    rows = slice(row, row + value.shape[0])
    out_ref[rows, 0:MODES] = hi
    out_ref[rows, 64 : 64 + MODES] = hi
    out_ref[rows, 128 : 128 + MODES] = value - hi


def setup_kernel(*refs):
    own_ref, dt_ref, sources, refs = *refs[:2], refs[2 : 2 + LOADED], refs[2 + LOADED :]
    copies, refs = refs[: LOADED - 2], refs[LOADED - 2 :]
    (
        dense_ref, scales_ref, table_ref, early_ref, terms_ref,
        flat_ref, v_ref, u_ref, t_ref, coef_ref, proj_k_ref, star_ref, upwind_ref, done,
    ) = refs
    moves = [
        pltpu.make_async_copy(source, copy, done.at[i])
        for i, (source, copy) in enumerate(zip(sources, (star_ref, *copies, upwind_ref)))
    ]
    for move in moves:
        move.start()
    stiff_ref, state_ref, inv_ref, elem_ref, face_ref, proj_ref = copies[:6]
    for move in moves[:2]:
        move.wait()
    blank = jnp.zeros((MODES, CELLS - MODES), F32)
    blocks = [jnp.concatenate([stiff_ref[d], blank], axis=1) for d in range(3)]
    put_scales(star_ref, scales_ref)
    build_dense(scales_ref, blocks, dense_ref)
    for move in moves[2:]:
        move.wait()
    spread_upwind(upwind_ref, table_ref)

    @pl.when(own_ref[0] >= FIRST_PARTNER)
    def _():
        proj_k_ref[...] = jnp.zeros_like(proj_k_ref)
        for f in range(FACES):
            put_weights_k(proj_ref[:, f, :], f * FACE_PAD, proj_k_ref)
        elems = four_times(elem_ref[...])
        faces = four_times(face_ref[...])
        index = jnp.broadcast_to(elems, (MODES, CELLS))
        for q in range(QTY):
            v_ref[q * MODES : (q + 1) * MODES, :] = jnp.take_along_axis(
                state_ref[q], index, axis=1
            )
        spread = jnp.broadcast_to(inv_ref[...], (8, CELLS))
        inv = jnp.take_along_axis(spread, index[:8], axis=1)[0:1, :]
        section = (lane_ids(1) // SLOTS).astype(F32)
        substep = jnp.full((1, CELLS), dt_ref[0], F32) * (1.0 / SUBSTEPS)
        fill_coefs(coef_ref, section * substep, (section + 1.0) * substep)
        u_ref[...] = predict_five(dense_ref, v_ref, coef_ref, inv)

        def emit(q, value):
            flat_ref[:, lanes(q)] = value

        mix_upwind(table_ref, lambda q: u_ref[q * MODES : (q + 1) * MODES, :], emit)
        tiles = slot_faces(faces, proj_k_ref[...].astype(BF16), flat_ref, t_ref)
        pack_slots(tiles, 0, early_ref, 0)
        pack_slots(tiles, 1, early_ref, PACKED[0])
        for q in range(QTY):
            terms_ref[q * FACE_PAD : (q + 1) * FACE_PAD, :] = tiles[q]


def uniform_coefs(coef_ref, end):
    fill_coefs(coef_ref, jnp.zeros((1, CELLS), F32), jnp.full((1, CELLS), end, F32))


def first_kernel(
    own_ref, dt_ref, table_ref, state_ref, inv_ref, dense_ref,
    flat_ref, w_ref, u_ref, odd_ref, even_ref, v_ref, sum_ref, coef_ref,
):
    own = own_ref[0]
    for q in range(QTY):
        value = state_ref[q]
        v_ref[q * MODES : (q + 1) * MODES, :] = value
        flat_ref[:, lanes(q)] = value
    dt = dt_ref[0]
    uniform_coefs(coef_ref, jnp.where(own < FINE, dt * (1.0 / SUBSTEPS), dt))
    sum_ref[...] = predict_five(dense_ref, v_ref, coef_ref, inv_ref[...])

    def rows(q):
        return sum_ref[q * MODES : (q + 1) * MODES, :]

    def emit(q, value):
        u_ref[:, lanes(q)] = value

    mix_upwind(table_ref, rows, emit)
    put_messages(own % 2 == 0, lambda q: u_ref[:, lanes(q)], odd_ref, even_ref)
    for q in range(QTY):
        w_ref[:, lanes(q)] = rows(q)


def prep_kernel(
    own_ref, counts_ref, dense_ref, scales_ref, stiff_ref, proj_ref, lift_ref, index_ref, face_ref,
    elem_ref, slot_face_ref, terms_ref, square_ref, volume_ref, proj_k_ref, lift_m_ref,
    inside_ref, outside_ref, slots_ref, factor_ref, late_ref, k_ref, m_ref,
):
    own = own_ref[0]

    @pl.when(own < FINE)
    def _():
        whole = dense_ref[...]
        top, low = whole[:DENSE], whole[DENSE:]
        both = dot(whole, top)
        put_dense(both[:DENSE] + (both[DENSE:] + dot(top, low)), 0, square_ref)

    @pl.when(own >= FIRST_PARTNER)
    def _():
        tiles = [terms_ref[q * FACE_PAD : (q + 1) * FACE_PAD, :] for q in range(QTY)]
        pack_slots(tiles, 2, late_ref, 0)
        pack_slots(tiles, 3, late_ref, PACKED[0])

    k_ref[...] = jnp.zeros_like(k_ref)
    for f in range(FACES):
        put_weights_k(proj_ref[:, f, :], f * FACE_PAD, k_ref)
    proj_k_ref[...] = k_ref[...].astype(BF16)
    gap = jnp.zeros((MODES, 64 - MODES), F32)
    pad = jnp.zeros((FACE_PAD - FACE_MODES, MODES), F32)
    tall = jnp.zeros((CELLS - MODES, CELLS), F32)
    one = jnp.concatenate([stiff_ref[0], gap, stiff_ref[1], gap], axis=1)
    one = jnp.concatenate([one, tall], axis=0).T
    faces = [jnp.concatenate([lift_ref[:, f, :], pad], axis=0) for f in range(FACES)]
    faces = jnp.concatenate(faces + [jnp.zeros((CELLS - FACES * FACE_PAD, MODES), F32)], axis=0)
    third = jnp.concatenate([stiff_ref[2], jnp.zeros((CELLS - MODES, MODES), F32)], axis=0)
    side = jnp.zeros((CELLS, 64 - MODES), F32)
    two = jnp.concatenate([faces, side, third, side], axis=1).T
    build_dense(
        scales_ref, [one[:MODES], one[64 : 64 + MODES], two[64 : 64 + MODES]], volume_ref
    )
    value = two[:MODES, : FACES * FACE_PAD]
    hi = coarse_part(value)
    low = value - hi
    m_ref[...] = jnp.concatenate(
        [jnp.concatenate([hi, hi], axis=1), jnp.concatenate([low, low], axis=1)], axis=0
    )
    lift_m_ref[...] = m_ref[...].astype(BF16)
    nb, face = index_ref[...], face_ref[...] * CELLS
    inside = (nb >= HALF) & (nb < HALF + CELLS)
    lane = jnp.where(nb < HALF, nb, nb - CELLS)
    inside_ref[...] = pick_matrix(jnp.where(inside, face + nb - HALF, -1), FACES * CELLS)
    outside_ref[...] = pick_matrix(jnp.where(inside, -1, face + lane), FACES * CELLS)
    target = four_times(slot_face_ref[...] * CELLS + elem_ref[...])
    slots = slot_matrix(as_column(target), live_slots(own, counts_ref))
    slots_ref[...] = slots.astype(BF16)
    count = jnp.sum(slots, axis=0, keepdims=True) * 0.25
    factor_ref[...] = jnp.broadcast_to(1.0 + count, factor_ref.shape)


def inner_kernel(
    section, own_ref, state_ref, w_ref, u_ref, inv_ref, inside_ref, factor_ref,
    volume_ref, proj_ref, lift_ref, *rest,
):
    remote_ref, slots_ref = rest[:2]
    out_ref, t_ref = rest[0 if section == 0 else 3 if section == 1 else 2], rest[-1]
    own = own_ref[0]

    def work():
        apply_k(proj_ref[...], u_ref, t_ref, FACES * FACE_PAD)
        own_traces = by_quantity(t_ref)
        if section == 0:
            picked = pick_parts(own_traces, inside_ref[...])
        else:
            remote = unpack_slots(remote_ref, PACKED[0] if section != 2 else 0)
            matrix = jnp.concatenate([inside_ref[...], slots_ref[...]], axis=0)
            picked = pick_parts(jnp.concatenate([own_traces, remote], axis=1), matrix)
        rows = QTY * FACE_PAD
        jump = factor_ref[0:1, :] * own_traces - (picked[:rows] + picked[rows:])
        flux = lift(lift_ref[...], two_parts(by_face(jump)))
        rows = jnp.concatenate([w_ref[:, lanes(q)] for q in range(QTY)], axis=0)
        volume = dense(volume_ref, rows)
        inv = inv_ref[...]
        for q in range(QTY):
            change = block(volume, q) - flux[:, lanes(q)]
            out_ref[:, lanes(q)] = state_ref[:, lanes(q)] + inv * change

    if section == 0:
        work()
    else:
        pl.when(own < FINE)(work)


def halo_lift(
    own, odd_in, even_in, outside_ref, proj_ref, lift_w, halo_ref, t_ref, extra=None
):
    take_messages(own % 2 == 0, odd_in, even_in, halo_ref)
    apply_k(proj_ref[...], halo_ref, t_ref, FACES * FACE_PAD)
    source, matrix = by_quantity(t_ref), outside_ref[...]
    if extra is None:
        return lift(lift_w, stack_parts(pick_parts(source, matrix)))
    source = jnp.concatenate([source, extra[0]], axis=1)
    matrix = jnp.concatenate([matrix, extra[1]], axis=0)
    return lift(lift_w, stack_sums(pick_parts(source, matrix)))


def outer_kernel(
    section, own_ref, dt_ref, table_ref, state_ref, odd_in, even_in, inv_ref, outside_ref,
    proj_ref, lift_ref, dense_ref, square_ref, sum_in, *rest,
):
    flat_ref, w_ref, u_ref, odd_ref, even_ref, sum_ref, halo_ref, t_ref, coef_ref = rest[-9:]
    own = own_ref[0]

    def update():
        extra = None
        if section == 0:
            remote_ref, slots_ref = rest[:2]
            extra = (unpack_slots(remote_ref), slots_ref[...])
        gain = halo_lift(
            own, odd_in, even_in, outside_ref, proj_ref, lift_ref[...], halo_ref, t_ref, extra
        )
        inv = inv_ref[...]
        for q in range(QTY):
            flat_ref[:, lanes(q)] = state_ref[:, lanes(q)] + inv * gain[:, lanes(q)]

    if section == 0:
        update()

    @pl.when(own < FINE)
    def _():
        if section > 0:
            update()
        uniform_coefs(coef_ref, dt_ref[0] * (1.0 / SUBSTEPS))
        rows = jnp.concatenate([flat_ref[:, lanes(q)] for q in range(QTY)], axis=0)
        w = predict_three(dense_ref, square_ref, rows, coef_ref, inv_ref[...])
        for q in range(QTY):
            w_ref[:, lanes(q)] = block(w, q)
        if section == SUBSTEPS - 2:
            elem_ref, slot_face_ref = rest[:2]
            index = jnp.broadcast_to(four_times(elem_ref[...]), (MODES, CELLS))

        def emit(q, value):
            u_ref[:, lanes(q)] = value
            total = sum_in[:, lanes(q)] + value
            if section < SUBSTEPS - 2:
                sum_ref[:, lanes(q)] = total
            else:
                halo_ref[:, lanes(q)] = jnp.take_along_axis(total, index, axis=1)

        mix_upwind(table_ref, lambda q: w_ref[:, lanes(q)], emit)
        put_messages(own % 2 == 0, lambda q: u_ref[:, lanes(q)], odd_ref, even_ref)
        if section == SUBSTEPS - 2:
            faces = four_times(slot_face_ref[...])
            pack_slots(slot_faces(faces, proj_ref[...], halo_ref, t_ref), None, sum_ref, 0)


def last_kernel(
    own_ref, fine_ref, coarse_ref, odd_in, even_in, inv_ref, outside_ref, proj_ref,
    lift_ref, up_ref, slots_ref, out_ref, halo_ref, t_ref, rows_ref, done,
):
    own = own_ref[0]
    inv = inv_ref[...]

    def write(base_ref, stacked):
        moves = []
        for start in range(0, QTY, 2):
            count = min(2, QTY - start)
            gain = lift(lift_ref[...], stacked[:, lanes(start, count)])
            for q in range(start, start + count):
                part = gain[:, lanes(q - start)]
                rows_ref[q] = base_ref[:, lanes(q)] + inv * part
                moves.append(
                    pltpu.make_async_copy(rows_ref.at[q], out_ref.at[q], done.at[q])
                )
                moves[q].start()
        for move in moves:
            move.wait()

    @pl.when(own < FINE)
    def _():
        take_messages(own % 2 == 0, odd_in, even_in, halo_ref)
        apply_k(proj_ref[...], halo_ref, t_ref, FACES * FACE_PAD)
        picked = pick_parts(by_quantity(t_ref), outside_ref[...])
        write(fine_ref, stack_parts(picked))

    @pl.when(own >= FINE)
    def _():
        picked = pick_parts(unpack_slots(up_ref), slots_ref[...])
        write(coarse_ref, stack_sums(picked))


S = pl.BlockSpec(memory_space=pltpu.SMEM)
V = pl.BlockSpec(memory_space=pltpu.VMEM)
H = pl.BlockSpec(memory_space=pltpu.HBM)
FIELD = (MODES, WIDTH)
ROWS = (QTY * MODES, CELLS)
MESSAGE = (256, CELLS)


def call(kernel, inputs, outs, scratch, operands, flops, name, aliases=None, place=None, scalars=2, out_place=V):
    shapes = [
        jax.ShapeDtypeStruct(o, F32) if isinstance(o, tuple) else o for o in outs
    ]
    return pl.pallas_call(
        kernel,
        in_specs=[S] * scalars + [place or V] * (inputs - scalars),
        out_specs=[out_place] * len(outs),
        out_shape=shapes,
        scratch_shapes=[
            pltpu.VMEM(s, F32) if isinstance(s, tuple) else s for s in scratch
        ],
        input_output_aliases=aliases or {},
        compiler_params=pltpu.CompilerParams(vmem_limit_bytes=16 * 1024 * 1024),
        cost_estimate=pl.CostEstimate(
            flops=flops, bytes_accessed=2_000_000, transcendentals=0
        ),
        name=name,
    )(*operands)


def half(*shape):
    return jax.ShapeDtypeStruct(shape, BF16)


def shards(
    modal_state, inv_size, time_step, stiffness, star_matrices, projection, lifting, upwind,
    nb_index, nb_face, iface_elem, iface_face, iface_counts,
):
    own = lax.axis_index("dom").astype(jnp.int32).reshape(1)
    state = modal_state.transpose(1, 0, 2)
    star = star_matrices.transpose(1, 0, 2)
    proj = projection.transpose(1, 0, 2)
    lift_w = lifting.transpose(2, 0, 1)
    dt = time_step.reshape(1)
    inv = inv_size.reshape(1, CELLS)
    elems = iface_elem.reshape(1, SLOTS)
    faces = iface_face.reshape(1, SLOTS)
    counts = iface_counts.reshape(2, CELLS)

    count = lax.axis_size("dom")
    down = [(i + FIRST_PARTNER, i) for i in range(FINE)]
    up = [(i, i + FIRST_PARTNER) for i in range(FINE)]

    def swaps(first, last):
        pairs = [(i, i + 1) for i in range(first, last, 2)]
        pairs = [p for p in pairs if p[1] < last]
        return pairs + [(b, a) for a, b in pairs]

    odd_fine, even_fine = swaps(1, FINE), swaps(0, FINE)
    odd_all = odd_fine + swaps(FINE, count)
    even_all = even_fine + swaps(FINE + 1, count)

    coef = (8, CELLS)
    t_rows = FACES * FACE_PAD
    t_shape = (t_rows, WIDTH)
    wide_operator = (2 * DENSE, DENSE)
    columns = FACES * CELLS

    loaded = (star, stiffness, state, inv, elems, faces, proj, lift_w, nb_index, nb_face,
              counts, upwind)
    *copies, dense_op, scales, table, early, terms = call(
        setup_kernel,
        2 + LOADED,
        [jax.ShapeDtypeStruct(x.shape, x.dtype) for x in loaded[1:-1]]
        + [half(*wide_operator), (48, DENSE), (QTY * 16, CELLS)]
        + [(2 * PACKED[0], CELLS), (QTY * FACE_PAD, CELLS)],
        [FIELD, ROWS, ROWS, t_shape, coef, (t_rows, 192), (QTY, 3, QTY), (QTY, QTY),
         pltpu.SemaphoreType.DMA((LOADED,))],
        (own, dt, *(pltpu.with_memory_space_constraint(x, pltpu.HBM) for x in loaded)),
        20_000_000,
        "setup",
        place=H,
    )
    stiffness, state, inv, elems, faces, proj, lift_w, nb_index, nb_face, counts = copies
    early = lax.ppermute(early, "dom", down)

    flat, w, u, odd, even = call(
        first_kernel,
        6,
        [FIELD, FIELD, FIELD, MESSAGE, MESSAGE],
        [ROWS, ROWS, coef],
        (own, dt, table, state, inv, dense_op),
        2_000_000_000,
        "first",
    )
    total = u
    coarse = None
    for section in range(SUBSTEPS):
        odd_in = lax.ppermute(odd, "dom", odd_all if section == 0 else odd_fine)
        even_in = lax.ppermute(even, "dom", even_all if section == 0 else even_fine)
        if section == 0:
            (
                square_op, volume, proj_k, lift_m, inside, outside, slots, factor,
                late,
            ) = call(
                prep_kernel,
                12,
                [
                    half(*wide_operator), half(*wide_operator), half(t_rows, 192),
                    half(2 * MODES, 2 * t_rows), half(columns, columns),
                    half(columns, columns), half(CELLS, columns), (8, columns),
                    (2 * PACKED[0], CELLS),
                ],
                [(t_rows, 192), (2 * MODES, 2 * t_rows)],
                (own, counts, dense_op, scales, stiffness, proj, lift_w, nb_index, nb_face,
                 elems, faces, terms),
                2_000_000_000,
                "prep",
                scalars=1,
            )
        if section == SUBSTEPS - 1:
            arrived = lax.ppermute(total, "dom", up)
        passed = section == 1
        extra = (() if section == 0 else (early if section == 1 else late, slots))
        results = call(
            functools.partial(inner_kernel, section),
            10 + len(extra) + passed,
            [FIELD] + [(2 * PACKED[0], CELLS)] * passed,
            [t_shape],
            (own, flat, w, u, inv, inside, factor, volume, proj_k, lift_m)
            + extra + (late,) * passed,
            2_000_000_000,
            f"inner{section}",
            {12: 1} if passed else None,
            scalars=1,
        )
        inner = results[0]
        if passed:
            late = lax.ppermute(results[1], "dom", down)
        if section == SUBSTEPS - 1:
            break
        extra = ((early, slots), (), (elems, faces))[section]
        flat, w, u, odd, even, total = call(
            functools.partial(outer_kernel, section),
            13 + len(extra),
            [FIELD, FIELD, FIELD, MESSAGE, MESSAGE,
             FIELD if section < SUBSTEPS - 2 else PACKED],
            [FIELD, t_shape, coef],
            (own, dt, table, inner, odd_in, even_in, inv, outside, proj_k, lift_m, dense_op,
             square_op, total) + extra,
            2_000_000_000,
            f"outer{section}",
        )
        if section == 0:
            coarse = flat
    (out,) = call(
        last_kernel,
        11,
        [pltpu.HBM((QTY, MODES, CELLS), F32)],
        [FIELD, t_shape, (QTY, MODES, CELLS), pltpu.SemaphoreType.DMA((QTY,))],
        (own, inner, coarse, odd_in, even_in, inv, outside, proj_k, lift_m, arrived, slots),
        1_000_000_000,
        "last",
        scalars=1,
        out_place=H,
    )
    return out.transpose(1, 0, 2)


def solution(mesh):
    return jax.shard_map(
        shards,
        mesh=mesh,
        in_specs=(
            P(None, None, "dom"),
            P("dom"),
            P(),
            P(),
            P(),
            P(),
            P(),
            P(),
            P(None, "dom"),
            P(None, "dom"),
            P("dom"),
            P("dom"),
            P(),
        ),
        out_specs=P(None, None, "dom"),
        check_vma=False,
    )
```

```python
import functools

import jax
import jax.numpy as jnp
from jax import lax
from jax.experimental import pallas as pl
from jax.experimental.pallas import tpu as pltpu
from jax.sharding import PartitionSpec as P

TAYLOR = 6
SUBSTEPS = 4
MODES = 56
QTY = 9
FACE_MODES = 21
FACE_PAD = 24
FACES = 4
CELLS = 128
HALF = 64
SLOTS = 32
WIDTH = QTY * CELLS
FINE = 85
FIRST_PARTNER = 256 - FINE
DENSE = 512
PACKED = (56, CELLS)
LOADED = 12

F32 = jnp.float32
BF16 = jnp.bfloat16


def lanes(q, count=1):
    return slice(q * CELLS, (q + count) * CELLS)


def lane_ids(rows):
    return lax.broadcasted_iota(jnp.int32, (rows, CELLS), 1)


def swap_halves(x):
    return pltpu.roll(x, HALF, 1)


def coarse_part(x):
    return x.astype(BF16).astype(F32)


def field_k(x):
    padded = jnp.concatenate([x, jnp.zeros((8, x.shape[1]), F32)], axis=0)
    hi = padded.astype(BF16)
    lo = (padded - hi.astype(F32)).astype(BF16)
    return jnp.concatenate([hi, lo, hi], axis=0)


def dot(a, b):
    return jnp.dot(a, b, preferred_element_type=F32)


def apply_k(weights, field_ref, out_ref, rows):
    for start in range(0, QTY, 2):
        part = lanes(start, min(2, QTY - start))
        out_ref[:rows, part] = dot(weights, field_k(field_ref[:, part]))


def spread_upwind(upwind_ref, table_ref):
    entries = upwind_ref[...]
    for p in range(QTY):
        table_ref[p * 16 : p * 16 + QTY, :] = jnp.broadcast_to(
            entries[:, p : p + 1], (QTY, CELLS)
        )


def mix_upwind(table_ref, w_of, emit):
    for base in range(0, QTY, 3):
        sums = [None] * 3
        for p in range(QTY):
            w = w_of(p)
            for j in range(3):
                row = p * 16 + base + j
                term = table_ref[row : row + 1, :] * w
                sums[j] = term if sums[j] is None else sums[j] + term
        for j in range(3):
            emit(base + j, sums[j])


def put_dense(value, base, out_ref):
    rows = value.shape[0]
    hi = value.astype(BF16)
    out_ref[base : base + rows, :] = hi
    out_ref[DENSE + base : DENSE + base + rows, :] = (value - hi.astype(F32)).astype(BF16)


def put_scales(star_ref, out_ref):
    wide = lax.broadcasted_iota(jnp.int32, (QTY, DENSE), 1)
    for d in range(3):
        entries = star_ref[:, d, :]
        scale = jnp.zeros((QTY, DENSE), F32)
        for p in range(QTY):
            here = (wide >= p * MODES) & (wide < (p + 1) * MODES)
            scale = jnp.where(here, entries[:, p : p + 1], scale)
        out_ref[16 * d : 16 * d + QTY, :] = scale


def build_dense(scales_ref, blocks, out_ref):
    tiled = []
    for d in range(3):
        columns = []
        for c in range(DENSE // CELLS):
            column = lane_ids(MODES) + c * CELLS
            columns.append(jnp.take_along_axis(blocks[d], column % MODES, axis=1))
        tiled.append(jnp.concatenate(columns, axis=1))

    def rows(q):
        return sum(scales_ref[16 * d + q : 16 * d + q + 1, :] * tiled[d] for d in range(3))

    for q in range(0, QTY - 1, 2):
        put_dense(jnp.concatenate([rows(q), rows(q + 1)], axis=0), q * MODES, out_ref)
    tail = jnp.concatenate([rows(QTY - 1), jnp.zeros((8, DENSE), F32)], axis=0)
    put_dense(tail, (QTY - 1) * MODES, out_ref)


def dense(weights_ref, rows):
    padded = jnp.concatenate([rows, jnp.zeros((8, CELLS), F32)], axis=0)
    hi = padded.astype(BF16)
    lo = (padded - hi.astype(F32)).astype(BF16)
    both = dot(weights_ref[:DENSE, :], jnp.concatenate([hi, lo], axis=1))
    low = dot(weights_ref[DENSE:, :], hi)
    return ((both[:, :CELLS] + both[:, CELLS:]) + low)[: QTY * MODES]


def block(rows, q):
    return rows[q * MODES : (q + 1) * MODES]


def predict_five(dense_ref, v_ref, coef_ref, inv):
    u = coef_ref[TAYLOR - 1 : TAYLOR, :] * v_ref[...]
    for k in range(TAYLOR - 2, -1, -1):
        u = coef_ref[k : k + 1, :] * v_ref[...] - inv * dense(dense_ref, u)
    return u


def predict_three(dense_ref, square_ref, v, coef_ref, inv):
    c = [coef_ref[k : k + 1, :] for k in range(TAYLOR)]
    two = inv * inv
    u = -inv * dense(dense_ref, v)
    top = c[4] * v + c[5] * u
    mid = c[2] * v + c[3] * u + two * dense(square_ref, top)
    return c[0] * v + c[1] * u + two * dense(square_ref, mid)


def fill_coefs(coef_ref, begin, end):
    b, e, fact = begin, end, 1.0
    for k in range(TAYLOR):
        fact = fact * (k + 1)
        coef_ref[k : k + 1, :] = (e - b) * (1.0 / fact)
        b, e = b * begin, e * end


def put_messages(even, u_of, odd_ref, even_ref):
    def put(row, first, second):
        rows = first.shape[0]
        low = lane_ids(rows) < HALF
        turned = swap_halves(second)
        left = jnp.where(low, first, turned)
        right = jnp.where(low, turned, first)
        odd_ref[row : row + rows, :] = jnp.where(even, left, right)
        even_ref[row : row + rows, :] = jnp.where(even, right, left)

    for j in range(QTY // 2):
        put(j * MODES, u_of(2 * j), u_of(2 * j + 1))
    tail = u_of(QTY - 1)
    put(QTY // 2 * MODES, tail[:32], tail[24:])


def take_messages(even, odd_ref, even_ref, halo_ref):
    def take(row, rows):
        low = lane_ids(rows) < HALF
        a, b = odd_ref[row : row + rows, :], even_ref[row : row + rows, :]
        left = jnp.where(even, a, b)
        right = jnp.where(even, b, a)
        first = jnp.where(low, right, left)
        second = swap_halves(jnp.where(low, left, right))
        return first, second

    for j in range(QTY // 2):
        first, second = take(j * MODES, MODES)
        halo_ref[:, lanes(2 * j)] = first
        halo_ref[:, lanes(2 * j + 1)] = second
    first, second = take(QTY // 2 * MODES, 32)
    halo_ref[:32, lanes(QTY - 1)] = first
    halo_ref[32:, lanes(QTY - 1)] = second[8:]


def pick_matrix(target, rows):
    row = lax.broadcasted_iota(jnp.int32, (rows, CELLS), 0)
    return jnp.concatenate(
        [
            jnp.where(row == target[f : f + 1, :], 1.0, 0.0).astype(BF16)
            for f in range(FACES)
        ],
        axis=1,
    )


def slot_matrix(slot_target, live):
    shape = (CELLS, FACES * CELLS)
    row = lax.broadcasted_iota(jnp.int32, shape, 0) % SLOTS
    column = lax.broadcasted_iota(jnp.int32, shape, 1)
    keep = (column == slot_target) & (row.astype(F32) < live)
    return jnp.where(keep, 1.0, 0.0)


def as_column(row):
    shape = (CELLS, CELLS)
    same = lax.broadcasted_iota(jnp.int32, shape, 0) == lax.broadcasted_iota(
        jnp.int32, shape, 1
    )
    kept = jnp.where(same, row.astype(F32), 0.0)
    return jnp.sum(kept, axis=1, keepdims=True).astype(jnp.int32)


def by_quantity(t_ref):
    return jnp.concatenate(
        [
            jnp.concatenate(
                [
                    t_ref[f * FACE_PAD : (f + 1) * FACE_PAD, lanes(q)]
                    for q in range(QTY)
                ],
                axis=0,
            )
            for f in range(FACES)
        ],
        axis=1,
    )


def by_face(g):
    return jnp.concatenate(
        [
            jnp.concatenate(
                [
                    g[q * FACE_PAD : (q + 1) * FACE_PAD, lanes(f)]
                    for f in range(FACES)
                ],
                axis=0,
            )
            for q in range(QTY)
        ],
        axis=1,
    )


def two_parts(x):
    hi = coarse_part(x)
    return jnp.concatenate([hi, x - hi], axis=0).astype(BF16)


def lift(lift_w, stacked):
    both = dot(lift_w, stacked)
    return both[:MODES] + both[MODES:]


def pick_parts(source, matrix):
    return dot(two_parts(source), matrix)


def stack_sums(picked):
    rows = QTY * FACE_PAD
    return two_parts(by_face(picked[:rows] + picked[rows:]))


def stack_parts(picked):
    rows = QTY * FACE_PAD
    return jnp.concatenate([by_face(picked[:rows]), by_face(picked[rows:])], axis=0).astype(BF16)


def pack_slots(tiles, section, out_ref, base):
    whole = jnp.concatenate(tiles + [jnp.zeros((8, CELLS), F32)], axis=0)
    group = lane_ids(8) // SLOTS
    for j in range(whole.shape[0] // 32):
        total = None
        for g in range(4):
            row = 32 * j + 8 * g
            part = whole[row : row + 8]
            if section is not None and g != section:
                part = pltpu.roll(part, SLOTS * ((g - section) % 4), 1)
            total = part if total is None else jnp.where(group == g, part, total)
        out_ref[base + 8 * j : base + 8 * j + 8, :] = total


def unpack_slots(in_ref, base=0):
    group = lane_ids(8) // SLOTS
    tiles = []
    for j in range(QTY * FACE_PAD // 8):
        row = base + 8 * (j // 4)
        tiles.append(jnp.where(group == j % 4, in_ref[row : row + 8, :], 0.0))
    return jnp.concatenate(tiles, axis=0)


def four_times(row):
    return jnp.concatenate([row] * 4, axis=1)


def slot_faces(faces, proj, u_ref, t_ref):
    apply_k(proj, u_ref, t_ref, FACES * FACE_PAD)
    tiles = []
    for q in range(QTY):
        total = jnp.zeros((FACE_PAD, CELLS), F32)
        for f in range(FACES):
            total = jnp.where(
                faces == f, t_ref[f * FACE_PAD : (f + 1) * FACE_PAD, lanes(q)], total
            )
        tiles.append(total)
    return tiles


def live_slots(own, counts_ref):
    fine = own < FINE
    partner = own >= FIRST_PARTNER
    at = jnp.where(fine, own, jnp.where(partner, own - FIRST_PARTNER, -1))
    place = lax.broadcasted_iota(jnp.int32, (2, CELLS), 0) * CELLS + lane_ids(2)
    mine = jnp.where(place == at, counts_ref[...].astype(F32), 0.0)
    return jnp.sum(jnp.sum(mine, axis=1, keepdims=True), axis=0, keepdims=True)


def put_weights_k(value, row, out_ref):
    hi = coarse_part(value)
    rows = slice(row, row + value.shape[0])
    out_ref[rows, 0:MODES] = hi
    out_ref[rows, 64 : 64 + MODES] = hi
    out_ref[rows, 128 : 128 + MODES] = value - hi


def setup_kernel(*refs):
    own_ref, dt_ref, sources, refs = *refs[:2], refs[2 : 2 + LOADED], refs[2 + LOADED :]
    copies, refs = refs[: LOADED - 2], refs[LOADED - 2 :]
    (
        dense_ref, scales_ref, table_ref, early_ref, terms_ref,
        flat_ref, v_ref, u_ref, t_ref, coef_ref, proj_k_ref, star_ref, upwind_ref, done,
    ) = refs
    moves = [
        pltpu.make_async_copy(source, copy, done.at[i])
        for i, (source, copy) in enumerate(zip(sources, (star_ref, *copies, upwind_ref)))
    ]
    for move in moves:
        move.start()
    stiff_ref, state_ref, inv_ref, elem_ref, face_ref, proj_ref = copies[:6]
    for move in moves[:2]:
        move.wait()
    blank = jnp.zeros((MODES, CELLS - MODES), F32)
    blocks = [jnp.concatenate([stiff_ref[d], blank], axis=1) for d in range(3)]
    put_scales(star_ref, scales_ref)
    build_dense(scales_ref, blocks, dense_ref)
    for move in moves[2:]:
        move.wait()
    spread_upwind(upwind_ref, table_ref)

    @pl.when(own_ref[0] >= FIRST_PARTNER)
    def _():
        proj_k_ref[...] = jnp.zeros_like(proj_k_ref)
        for f in range(FACES):
            put_weights_k(proj_ref[:, f, :], f * FACE_PAD, proj_k_ref)
        elems = four_times(elem_ref[...])
        faces = four_times(face_ref[...])
        index = jnp.broadcast_to(elems, (MODES, CELLS))
        for q in range(QTY):
            v_ref[q * MODES : (q + 1) * MODES, :] = jnp.take_along_axis(
                state_ref[q], index, axis=1
            )
        spread = jnp.broadcast_to(inv_ref[...], (8, CELLS))
        inv = jnp.take_along_axis(spread, index[:8], axis=1)[0:1, :]
        section = (lane_ids(1) // SLOTS).astype(F32)
        substep = jnp.full((1, CELLS), dt_ref[0], F32) * (1.0 / SUBSTEPS)
        fill_coefs(coef_ref, section * substep, (section + 1.0) * substep)
        u_ref[...] = predict_five(dense_ref, v_ref, coef_ref, inv)

        def emit(q, value):
            flat_ref[:, lanes(q)] = value

        mix_upwind(table_ref, lambda q: u_ref[q * MODES : (q + 1) * MODES, :], emit)
        tiles = slot_faces(faces, proj_k_ref[...].astype(BF16), flat_ref, t_ref)
        pack_slots(tiles, 0, early_ref, 0)
        pack_slots(tiles, 1, early_ref, PACKED[0])
        for q in range(QTY):
            terms_ref[q * FACE_PAD : (q + 1) * FACE_PAD, :] = tiles[q]


def uniform_coefs(coef_ref, end):
    fill_coefs(coef_ref, jnp.zeros((1, CELLS), F32), jnp.full((1, CELLS), end, F32))


def first_kernel(
    own_ref, dt_ref, table_ref, state_ref, inv_ref, dense_ref,
    flat_ref, w_ref, u_ref, odd_ref, even_ref, v_ref, sum_ref, coef_ref,
):
    own = own_ref[0]
    for q in range(QTY):
        value = state_ref[q]
        v_ref[q * MODES : (q + 1) * MODES, :] = value
        flat_ref[:, lanes(q)] = value
    dt = dt_ref[0]
    uniform_coefs(coef_ref, jnp.where(own < FINE, dt * (1.0 / SUBSTEPS), dt))
    sum_ref[...] = predict_five(dense_ref, v_ref, coef_ref, inv_ref[...])

    def rows(q):
        return sum_ref[q * MODES : (q + 1) * MODES, :]

    def emit(q, value):
        u_ref[:, lanes(q)] = value

    mix_upwind(table_ref, rows, emit)
    put_messages(own % 2 == 0, lambda q: u_ref[:, lanes(q)], odd_ref, even_ref)
    for q in range(QTY):
        w_ref[:, lanes(q)] = rows(q)


def prep_kernel(
    own_ref, counts_ref, dense_ref, scales_ref, stiff_ref, proj_ref, lift_ref, index_ref, face_ref,
    elem_ref, slot_face_ref, terms_ref, square_ref, volume_ref, proj_k_ref, lift_m_ref,
    inside_ref, outside_ref, slots_ref, factor_ref, late_ref, k_ref, m_ref,
):
    own = own_ref[0]

    @pl.when(own < FINE)
    def _():
        whole = dense_ref[...]
        top, low = whole[:DENSE], whole[DENSE:]
        both = dot(whole, top)
        put_dense(both[:DENSE] + (both[DENSE:] + dot(top, low)), 0, square_ref)

    @pl.when(own >= FIRST_PARTNER)
    def _():
        tiles = [terms_ref[q * FACE_PAD : (q + 1) * FACE_PAD, :] for q in range(QTY)]
        pack_slots(tiles, 2, late_ref, 0)
        pack_slots(tiles, 3, late_ref, PACKED[0])

    k_ref[...] = jnp.zeros_like(k_ref)
    for f in range(FACES):
        put_weights_k(proj_ref[:, f, :], f * FACE_PAD, k_ref)
    proj_k_ref[...] = k_ref[...].astype(BF16)
    gap = jnp.zeros((MODES, 64 - MODES), F32)
    pad = jnp.zeros((FACE_PAD - FACE_MODES, MODES), F32)
    tall = jnp.zeros((CELLS - MODES, CELLS), F32)
    one = jnp.concatenate([stiff_ref[0], gap, stiff_ref[1], gap], axis=1)
    one = jnp.concatenate([one, tall], axis=0).T
    faces = [jnp.concatenate([lift_ref[:, f, :], pad], axis=0) for f in range(FACES)]
    faces = jnp.concatenate(faces + [jnp.zeros((CELLS - FACES * FACE_PAD, MODES), F32)], axis=0)
    third = jnp.concatenate([stiff_ref[2], jnp.zeros((CELLS - MODES, MODES), F32)], axis=0)
    side = jnp.zeros((CELLS, 64 - MODES), F32)
    two = jnp.concatenate([faces, side, third, side], axis=1).T
    build_dense(
        scales_ref, [one[:MODES], one[64 : 64 + MODES], two[64 : 64 + MODES]], volume_ref
    )
    value = two[:MODES, : FACES * FACE_PAD]
    hi = coarse_part(value)
    low = value - hi
    m_ref[...] = jnp.concatenate(
        [jnp.concatenate([hi, hi], axis=1), jnp.concatenate([low, low], axis=1)], axis=0
    )
    lift_m_ref[...] = m_ref[...].astype(BF16)
    nb, face = index_ref[...], face_ref[...] * CELLS
    inside = (nb >= HALF) & (nb < HALF + CELLS)
    lane = jnp.where(nb < HALF, nb + HALF, nb - HALF - CELLS)
    inside_ref[...] = pick_matrix(jnp.where(inside, face + nb - HALF, -1), FACES * CELLS)
    outside_ref[...] = pick_matrix(jnp.where(inside, -1, face + lane), FACES * CELLS)
    target = four_times(slot_face_ref[...] * CELLS + elem_ref[...])
    slots = slot_matrix(as_column(target), live_slots(own, counts_ref))
    slots_ref[...] = slots.astype(BF16)
    count = jnp.sum(slots, axis=0, keepdims=True) * 0.25
    factor_ref[...] = jnp.broadcast_to(1.0 + count, factor_ref.shape)


def inner_kernel(
    section, own_ref, state_ref, w_ref, u_ref, inv_ref, inside_ref, factor_ref,
    volume_ref, proj_ref, lift_ref, *rest,
):
    remote_ref, slots_ref = rest[:2]
    out_ref, t_ref = rest[0 if section == 0 else 3 if section == 1 else 2], rest[-1]
    own = own_ref[0]

    def work():
        apply_k(proj_ref[...], u_ref, t_ref, FACES * FACE_PAD)
        own_traces = by_quantity(t_ref)
        if section == 0:
            picked = pick_parts(own_traces, inside_ref[...])
        else:
            remote = unpack_slots(remote_ref, PACKED[0] if section != 2 else 0)
            matrix = jnp.concatenate([inside_ref[...], slots_ref[...]], axis=0)
            picked = pick_parts(jnp.concatenate([own_traces, remote], axis=1), matrix)
        rows = QTY * FACE_PAD
        jump = factor_ref[0:1, :] * own_traces - (picked[:rows] + picked[rows:])
        flux = lift(lift_ref[...], two_parts(by_face(jump)))
        rows = jnp.concatenate([w_ref[:, lanes(q)] for q in range(QTY)], axis=0)
        volume = dense(volume_ref, rows)
        inv = inv_ref[...]
        for q in range(QTY):
            change = block(volume, q) - flux[:, lanes(q)]
            out_ref[:, lanes(q)] = state_ref[:, lanes(q)] + inv * change

    if section == 0:
        work()
    else:
        pl.when(own < FINE)(work)


def halo_lift(
    own, odd_in, even_in, outside_ref, proj_ref, lift_w, halo_ref, t_ref, extra=None
):
    take_messages(own % 2 == 0, odd_in, even_in, halo_ref)
    apply_k(proj_ref[...], halo_ref, t_ref, FACES * FACE_PAD)
    source, matrix = by_quantity(t_ref), outside_ref[...]
    if extra is None:
        return lift(lift_w, stack_parts(pick_parts(source, matrix)))
    source = jnp.concatenate([source, extra[0]], axis=1)
    matrix = jnp.concatenate([matrix, extra[1]], axis=0)
    return lift(lift_w, stack_sums(pick_parts(source, matrix)))


def outer_kernel(
    section, own_ref, dt_ref, table_ref, state_ref, odd_in, even_in, inv_ref, outside_ref,
    proj_ref, lift_ref, dense_ref, square_ref, sum_in, *rest,
):
    flat_ref, w_ref, u_ref, odd_ref, even_ref, sum_ref, halo_ref, t_ref, coef_ref = rest[-9:]
    own = own_ref[0]

    def update():
        extra = None
        if section == 0:
            remote_ref, slots_ref = rest[:2]
            extra = (unpack_slots(remote_ref), slots_ref[...])
        gain = halo_lift(
            own, odd_in, even_in, outside_ref, proj_ref, lift_ref[...], halo_ref, t_ref, extra
        )
        inv = inv_ref[...]
        for q in range(QTY):
            flat_ref[:, lanes(q)] = state_ref[:, lanes(q)] + inv * gain[:, lanes(q)]

    if section == 0:
        update()

    @pl.when(own < FINE)
    def _():
        if section > 0:
            update()
        uniform_coefs(coef_ref, dt_ref[0] * (1.0 / SUBSTEPS))
        rows = jnp.concatenate([flat_ref[:, lanes(q)] for q in range(QTY)], axis=0)
        w = predict_three(dense_ref, square_ref, rows, coef_ref, inv_ref[...])
        for q in range(QTY):
            w_ref[:, lanes(q)] = block(w, q)
        if section == SUBSTEPS - 2:
            elem_ref, slot_face_ref = rest[:2]
            index = jnp.broadcast_to(four_times(elem_ref[...]), (MODES, CELLS))

        def emit(q, value):
            u_ref[:, lanes(q)] = value
            total = sum_in[:, lanes(q)] + value
            if section < SUBSTEPS - 2:
                sum_ref[:, lanes(q)] = total
            else:
                halo_ref[:, lanes(q)] = jnp.take_along_axis(total, index, axis=1)

        mix_upwind(table_ref, lambda q: w_ref[:, lanes(q)], emit)
        put_messages(own % 2 == 0, lambda q: u_ref[:, lanes(q)], odd_ref, even_ref)
        if section == SUBSTEPS - 2:
            faces = four_times(slot_face_ref[...])
            pack_slots(slot_faces(faces, proj_ref[...], halo_ref, t_ref), None, sum_ref, 0)


def last_kernel(
    own_ref, fine_ref, coarse_ref, odd_in, even_in, inv_ref, outside_ref, proj_ref,
    lift_ref, up_ref, slots_ref, out_ref, halo_ref, t_ref, rows_ref, done,
):
    own = own_ref[0]
    inv = inv_ref[...]

    def write(base_ref, stacked):
        moves = []
        for start in range(0, QTY, 2):
            count = min(2, QTY - start)
            gain = lift(lift_ref[...], stacked[:, lanes(start, count)])
            for q in range(start, start + count):
                part = gain[:, lanes(q - start)]
                rows_ref[q] = base_ref[:, lanes(q)] + inv * part
                moves.append(
                    pltpu.make_async_copy(rows_ref.at[q], out_ref.at[q], done.at[q])
                )
                moves[q].start()
        for move in moves:
            move.wait()

    @pl.when(own < FINE)
    def _():
        take_messages(own % 2 == 0, odd_in, even_in, halo_ref)
        apply_k(proj_ref[...], halo_ref, t_ref, FACES * FACE_PAD)
        picked = pick_parts(by_quantity(t_ref), outside_ref[...])
        write(fine_ref, stack_parts(picked))

    @pl.when(own >= FINE)
    def _():
        picked = pick_parts(unpack_slots(up_ref), slots_ref[...])
        write(coarse_ref, stack_sums(picked))


S = pl.BlockSpec(memory_space=pltpu.SMEM)
V = pl.BlockSpec(memory_space=pltpu.VMEM)
H = pl.BlockSpec(memory_space=pltpu.HBM)
FIELD = (MODES, WIDTH)
ROWS = (QTY * MODES, CELLS)
MESSAGE = (256, CELLS)


def call(kernel, inputs, outs, scratch, operands, flops, name, aliases=None, place=None, scalars=2, out_place=V):
    shapes = [
        jax.ShapeDtypeStruct(o, F32) if isinstance(o, tuple) else o for o in outs
    ]
    return pl.pallas_call(
        kernel,
        in_specs=[S] * scalars + [place or V] * (inputs - scalars),
        out_specs=[out_place] * len(outs),
        out_shape=shapes,
        scratch_shapes=[
            pltpu.VMEM(s, F32) if isinstance(s, tuple) else s for s in scratch
        ],
        input_output_aliases=aliases or {},
        compiler_params=pltpu.CompilerParams(vmem_limit_bytes=16 * 1024 * 1024),
        cost_estimate=pl.CostEstimate(
            flops=flops, bytes_accessed=2_000_000, transcendentals=0
        ),
        name=name,
    )(*operands)


def half(*shape):
    return jax.ShapeDtypeStruct(shape, BF16)


def shards(
    modal_state, inv_size, time_step, stiffness, star_matrices, projection, lifting, upwind,
    nb_index, nb_face, iface_elem, iface_face, iface_counts,
):
    own = lax.axis_index("dom").astype(jnp.int32).reshape(1)
    state = modal_state.transpose(1, 0, 2)
    star = star_matrices.transpose(1, 0, 2)
    proj = projection.transpose(1, 0, 2)
    lift_w = lifting.transpose(2, 0, 1)
    dt = time_step.reshape(1)
    inv = inv_size.reshape(1, CELLS)
    elems = iface_elem.reshape(1, SLOTS)
    faces = iface_face.reshape(1, SLOTS)
    counts = iface_counts.reshape(2, CELLS)

    count = lax.axis_size("dom")
    down = [(i + FIRST_PARTNER, i) for i in range(FINE)]
    up = [(i, i + FIRST_PARTNER) for i in range(FINE)]

    def swaps(first, last):
        pairs = [(i, i + 1) for i in range(first, last, 2)]
        pairs = [p for p in pairs if p[1] < last]
        return pairs + [(b, a) for a, b in pairs]

    odd_fine, even_fine = swaps(1, FINE), swaps(0, FINE)
    odd_all = odd_fine + swaps(FINE, count)
    even_all = even_fine + swaps(FINE + 1, count)

    coef = (8, CELLS)
    t_rows = FACES * FACE_PAD
    t_shape = (t_rows, WIDTH)
    wide_operator = (2 * DENSE, DENSE)
    columns = FACES * CELLS

    loaded = (star, stiffness, state, inv, elems, faces, proj, lift_w, nb_index, nb_face,
              counts, upwind)
    *copies, dense_op, scales, table, early, terms = call(
        setup_kernel,
        2 + LOADED,
        [jax.ShapeDtypeStruct(x.shape, x.dtype) for x in loaded[1:-1]]
        + [half(*wide_operator), (48, DENSE), (QTY * 16, CELLS)]
        + [(2 * PACKED[0], CELLS), (QTY * FACE_PAD, CELLS)],
        [FIELD, ROWS, ROWS, t_shape, coef, (t_rows, 192), (QTY, 3, QTY), (QTY, QTY),
         pltpu.SemaphoreType.DMA((LOADED,))],
        (own, dt, *(pltpu.with_memory_space_constraint(x, pltpu.HBM) for x in loaded)),
        20_000_000,
        "setup",
        place=H,
    )
    stiffness, state, inv, elems, faces, proj, lift_w, nb_index, nb_face, counts = copies
    early = lax.ppermute(early, "dom", down)

    flat, w, u, odd, even = call(
        first_kernel,
        6,
        [FIELD, FIELD, FIELD, MESSAGE, MESSAGE],
        [ROWS, ROWS, coef],
        (own, dt, table, state, inv, dense_op),
        2_000_000_000,
        "first",
    )
    total = u
    coarse = None
    for section in range(SUBSTEPS):
        odd_in = lax.ppermute(odd, "dom", odd_all if section == 0 else odd_fine)
        even_in = lax.ppermute(even, "dom", even_all if section == 0 else even_fine)
        if section == 0:
            (
                square_op, volume, proj_k, lift_m, inside, outside, slots, factor,
                late,
            ) = call(
                prep_kernel,
                12,
                [
                    half(*wide_operator), half(*wide_operator), half(t_rows, 192),
                    half(2 * MODES, 2 * t_rows), half(columns, columns),
                    half(columns, columns), half(CELLS, columns), (8, columns),
                    (2 * PACKED[0], CELLS),
                ],
                [(t_rows, 192), (2 * MODES, 2 * t_rows)],
                (own, counts, dense_op, scales, stiffness, proj, lift_w, nb_index, nb_face,
                 elems, faces, terms),
                2_000_000_000,
                "prep",
                scalars=1,
            )
        if section == SUBSTEPS - 1:
            arrived = lax.ppermute(total, "dom", up)
        passed = section == 1
        extra = (() if section == 0 else (early if section == 1 else late, slots))
        results = call(
            functools.partial(inner_kernel, section),
            10 + len(extra) + passed,
            [FIELD] + [(2 * PACKED[0], CELLS)] * passed,
            [t_shape],
            (own, flat, w, u, inv, inside, factor, volume, proj_k, lift_m)
            + extra + (late,) * passed,
            2_000_000_000,
            f"inner{section}",
            {12: 1} if passed else None,
            scalars=1,
        )
        inner = results[0]
        if passed:
            late = lax.ppermute(results[1], "dom", down)
        if section == SUBSTEPS - 1:
            break
        extra = ((early, slots), (), (elems, faces))[section]
        flat, w, u, odd, even, total = call(
            functools.partial(outer_kernel, section),
            13 + len(extra),
            [FIELD, FIELD, FIELD, MESSAGE, MESSAGE,
             FIELD if section < SUBSTEPS - 2 else PACKED],
            [FIELD, t_shape, coef],
            (own, dt, table, inner, odd_in, even_in, inv, outside, proj_k, lift_m, dense_op,
             square_op, total) + extra,
            2_000_000_000,
            f"outer{section}",
        )
        if section == 0:
            coarse = flat
    (out,) = call(
        last_kernel,
        11,
        [pltpu.HBM((QTY, MODES, CELLS), F32)],
        [FIELD, t_shape, (QTY, MODES, CELLS), pltpu.SemaphoreType.DMA((QTY,))],
        (own, inner, coarse, odd_in, even_in, inv, outside, proj_k, lift_m, arrived, slots),
        1_000_000_000,
        "last",
        scalars=1,
        out_place=H,
    )
    return out.transpose(1, 0, 2)


def solution(mesh):
    return jax.shard_map(
        shards,
        mesh=mesh,
        in_specs=(
            P(None, None, "dom"),
            P("dom"),
            P(),
            P(),
            P(),
            P(),
            P(),
            P(),
            P(None, "dom"),
            P(None, "dom"),
            P("dom"),
            P("dom"),
            P(),
        ),
        out_specs=P(None, None, "dom"),
        check_vma=False,
    )
```

```python
import functools

import jax
import jax.numpy as jnp
from jax import lax
from jax.experimental import pallas as pl
from jax.experimental.pallas import tpu as pltpu
from jax.sharding import PartitionSpec as P

TAYLOR = 6
SUBSTEPS = 4
MODES = 56
QTY = 9
FACE_MODES = 21
FACE_PAD = 24
FACES = 4
CELLS = 128
HALF = 64
SLOTS = 32
WIDTH = QTY * CELLS
FINE = 85
FIRST_PARTNER = 256 - FINE
DENSE = 512
PACKED = (56, CELLS)
LOADED = 8

F32 = jnp.float32
BF16 = jnp.bfloat16


def lanes(q, count=1):
    return slice(q * CELLS, (q + count) * CELLS)


def lane_ids(rows):
    return lax.broadcasted_iota(jnp.int32, (rows, CELLS), 1)


def swap_halves(x):
    return pltpu.roll(x, HALF, 1)


def coarse_part(x):
    return x.astype(BF16).astype(F32)


def field_k(x):
    padded = jnp.concatenate([x, jnp.zeros((8, x.shape[1]), F32)], axis=0)
    hi = padded.astype(BF16)
    lo = (padded - hi.astype(F32)).astype(BF16)
    return jnp.concatenate([hi, lo, hi], axis=0)


def dot(a, b):
    return jnp.dot(a, b, preferred_element_type=F32)


def apply_k(weights, field_ref, out_ref, rows):
    for start in range(0, QTY, 2):
        part = lanes(start, min(2, QTY - start))
        out_ref[:rows, part] = dot(weights, field_k(field_ref[:, part]))


def spread_upwind(upwind_ref, table_ref):
    entries = upwind_ref[...]
    for p in range(QTY):
        table_ref[p * 16 : p * 16 + QTY, :] = jnp.broadcast_to(
            entries[:, p : p + 1], (QTY, CELLS)
        )


def mix_upwind(table_ref, w_of, emit):
    for base in range(0, QTY, 3):
        sums = [None] * 3
        for p in range(QTY):
            w = w_of(p)
            for j in range(3):
                row = p * 16 + base + j
                term = table_ref[row : row + 1, :] * w
                sums[j] = term if sums[j] is None else sums[j] + term
        for j in range(3):
            emit(base + j, sums[j])


def put_dense(value, base, out_ref):
    rows = value.shape[0]
    hi = value.astype(BF16)
    out_ref[base : base + rows, :] = hi
    out_ref[DENSE + base : DENSE + base + rows, :] = (value - hi.astype(F32)).astype(BF16)


def put_scales(star_ref, out_ref):
    wide = lax.broadcasted_iota(jnp.int32, (QTY, DENSE), 1)
    for d in range(3):
        entries = star_ref[:, d, :]
        scale = jnp.zeros((QTY, DENSE), F32)
        for p in range(QTY):
            here = (wide >= p * MODES) & (wide < (p + 1) * MODES)
            scale = jnp.where(here, entries[:, p : p + 1], scale)
        out_ref[16 * d : 16 * d + QTY, :] = scale


def build_dense(scales_ref, blocks, out_ref):
    tiled = []
    for d in range(3):
        columns = []
        for c in range(DENSE // CELLS):
            column = lane_ids(MODES) + c * CELLS
            columns.append(jnp.take_along_axis(blocks[d], column % MODES, axis=1))
        tiled.append(jnp.concatenate(columns, axis=1))

    def rows(q):
        return sum(scales_ref[16 * d + q : 16 * d + q + 1, :] * tiled[d] for d in range(3))

    for q in range(0, QTY - 1, 2):
        put_dense(jnp.concatenate([rows(q), rows(q + 1)], axis=0), q * MODES, out_ref)
    tail = jnp.concatenate([rows(QTY - 1), jnp.zeros((8, DENSE), F32)], axis=0)
    put_dense(tail, (QTY - 1) * MODES, out_ref)


def dense(weights_ref, rows):
    padded = jnp.concatenate([rows, jnp.zeros((8, CELLS), F32)], axis=0)
    hi = padded.astype(BF16)
    lo = (padded - hi.astype(F32)).astype(BF16)
    both = dot(weights_ref[:DENSE, :], jnp.concatenate([hi, lo], axis=1))
    low = dot(weights_ref[DENSE:, :], hi)
    return ((both[:, :CELLS] + both[:, CELLS:]) + low)[: QTY * MODES]


def block(rows, q):
    return rows[q * MODES : (q + 1) * MODES]


def predict_five(dense_ref, v_ref, coef_ref, inv):
    u = coef_ref[TAYLOR - 1 : TAYLOR, :] * v_ref[...]
    for k in range(TAYLOR - 2, -1, -1):
        u = coef_ref[k : k + 1, :] * v_ref[...] - inv * dense(dense_ref, u)
    return u


def predict_three(dense_ref, square_ref, v, coef_ref, inv):
    c = [coef_ref[k : k + 1, :] for k in range(TAYLOR)]
    two = inv * inv
    u = -inv * dense(dense_ref, v)
    top = c[4] * v + c[5] * u
    mid = c[2] * v + c[3] * u + two * dense(square_ref, top)
    return c[0] * v + c[1] * u + two * dense(square_ref, mid)


def fill_coefs(coef_ref, begin, end):
    b, e, fact = begin, end, 1.0
    for k in range(TAYLOR):
        fact = fact * (k + 1)
        coef_ref[k : k + 1, :] = (e - b) * (1.0 / fact)
        b, e = b * begin, e * end


def put_messages(even, u_of, odd_ref, even_ref):
    def put(row, first, second):
        rows = first.shape[0]
        low = lane_ids(rows) < HALF
        turned = swap_halves(second)
        left = jnp.where(low, first, turned)
        right = jnp.where(low, turned, first)
        odd_ref[row : row + rows, :] = jnp.where(even, left, right)
        even_ref[row : row + rows, :] = jnp.where(even, right, left)

    for j in range(QTY // 2):
        put(j * MODES, u_of(2 * j), u_of(2 * j + 1))
    tail = u_of(QTY - 1)
    put(QTY // 2 * MODES, tail[:32], tail[24:])


def take_messages(even, odd_ref, even_ref, halo_ref):
    def take(row, rows):
        low = lane_ids(rows) < HALF
        a, b = odd_ref[row : row + rows, :], even_ref[row : row + rows, :]
        left = jnp.where(even, a, b)
        right = jnp.where(even, b, a)
        first = jnp.where(low, right, left)
        second = swap_halves(jnp.where(low, left, right))
        return first, second

    for j in range(QTY // 2):
        first, second = take(j * MODES, MODES)
        halo_ref[:, lanes(2 * j)] = first
        halo_ref[:, lanes(2 * j + 1)] = second
    first, second = take(QTY // 2 * MODES, 32)
    halo_ref[:32, lanes(QTY - 1)] = first
    halo_ref[32:, lanes(QTY - 1)] = second[8:]


def pick_matrix(target, rows):
    row = lax.broadcasted_iota(jnp.int32, (rows, CELLS), 0)
    return jnp.concatenate(
        [
            jnp.where(row == target[f : f + 1, :], 1.0, 0.0).astype(BF16)
            for f in range(FACES)
        ],
        axis=1,
    )


def slot_matrix(slot_target, live):
    shape = (CELLS, FACES * CELLS)
    row = lax.broadcasted_iota(jnp.int32, shape, 0) % SLOTS
    column = lax.broadcasted_iota(jnp.int32, shape, 1)
    keep = (column == slot_target) & (row.astype(F32) < live)
    return jnp.where(keep, 1.0, 0.0)


def as_column(row):
    shape = (CELLS, CELLS)
    same = lax.broadcasted_iota(jnp.int32, shape, 0) == lax.broadcasted_iota(
        jnp.int32, shape, 1
    )
    kept = jnp.where(same, row.astype(F32), 0.0)
    return jnp.sum(kept, axis=1, keepdims=True).astype(jnp.int32)


def by_quantity(t_ref):
    return jnp.concatenate(
        [
            jnp.concatenate(
                [
                    t_ref[f * FACE_PAD : (f + 1) * FACE_PAD, lanes(q)]
                    for q in range(QTY)
                ],
                axis=0,
            )
            for f in range(FACES)
        ],
        axis=1,
    )


def by_face(g):
    return jnp.concatenate(
        [
            jnp.concatenate(
                [
                    g[q * FACE_PAD : (q + 1) * FACE_PAD, lanes(f)]
                    for f in range(FACES)
                ],
                axis=0,
            )
            for q in range(QTY)
        ],
        axis=1,
    )


def two_parts(x):
    hi = coarse_part(x)
    return jnp.concatenate([hi, x - hi], axis=0).astype(BF16)


def lift(lift_w, stacked):
    both = dot(lift_w, stacked)
    return both[:MODES] + both[MODES:]


def pick_parts(source, matrix):
    return dot(two_parts(source), matrix)


def stack_sums(picked):
    rows = QTY * FACE_PAD
    return two_parts(by_face(picked[:rows] + picked[rows:]))


def stack_parts(picked):
    rows = QTY * FACE_PAD
    return jnp.concatenate([by_face(picked[:rows]), by_face(picked[rows:])], axis=0).astype(BF16)


def pack_slots(tiles, section, out_ref, base):
    whole = jnp.concatenate(tiles + [jnp.zeros((8, CELLS), F32)], axis=0)
    group = lane_ids(8) // SLOTS
    for j in range(whole.shape[0] // 32):
        total = None
        for g in range(4):
            row = 32 * j + 8 * g
            part = whole[row : row + 8]
            if section is not None and g != section:
                part = pltpu.roll(part, SLOTS * ((g - section) % 4), 1)
            total = part if total is None else jnp.where(group == g, part, total)
        out_ref[base + 8 * j : base + 8 * j + 8, :] = total


def unpack_slots(in_ref, base=0):
    group = lane_ids(8) // SLOTS
    tiles = []
    for j in range(QTY * FACE_PAD // 8):
        row = base + 8 * (j // 4)
        tiles.append(jnp.where(group == j % 4, in_ref[row : row + 8, :], 0.0))
    return jnp.concatenate(tiles, axis=0)


def four_times(row):
    return jnp.concatenate([row] * 4, axis=1)


def slot_faces(faces, proj, u_ref, t_ref):
    apply_k(proj, u_ref, t_ref, FACES * FACE_PAD)
    tiles = []
    for q in range(QTY):
        total = jnp.zeros((FACE_PAD, CELLS), F32)
        for f in range(FACES):
            total = jnp.where(
                faces == f, t_ref[f * FACE_PAD : (f + 1) * FACE_PAD, lanes(q)], total
            )
        tiles.append(total)
    return tiles


def live_slots(own, counts_ref):
    fine = own < FINE
    partner = own >= FIRST_PARTNER
    at = jnp.where(fine, own, jnp.where(partner, own - FIRST_PARTNER, -1))
    place = lax.broadcasted_iota(jnp.int32, (2, CELLS), 0) * CELLS + lane_ids(2)
    mine = jnp.where(place == at, counts_ref[...].astype(F32), 0.0)
    return jnp.sum(jnp.sum(mine, axis=1, keepdims=True), axis=0, keepdims=True)


def put_weights_k(value, row, out_ref):
    hi = coarse_part(value)
    rows = slice(row, row + value.shape[0])
    out_ref[rows, 0:MODES] = hi
    out_ref[rows, 64 : 64 + MODES] = hi
    out_ref[rows, 128 : 128 + MODES] = value - hi


def stiffness_blocks(stiff_ref):
    blank = jnp.zeros((MODES, CELLS - MODES), F32)
    return [jnp.concatenate([stiff_ref[d], blank], axis=1) for d in range(3)]


def setup_kernel(
    own_ref, star_ref, stiff_ref, upwind_ref, inv_ref, dense_ref, scales_ref, table_ref
):
    put_scales(star_ref, scales_ref)
    build_dense(scales_ref, stiffness_blocks(stiff_ref), dense_ref)
    spread_upwind(upwind_ref, table_ref)


def remote_kernel(own_ref, dt_ref, *refs):
    sources, (early_ref, terms_ref), refs = refs[:LOADED], refs[LOADED : LOADED + 2], refs[LOADED + 2 :]
    copies, refs = refs[:LOADED], refs[LOADED:]
    (
        dense_ref, scales_ref, table_ref,
        flat_ref, v_ref, u_ref, t_ref, coef_ref, proj_k_ref, done,
    ) = refs

    @pl.when(own_ref[0] >= FIRST_PARTNER)
    def _():
        moves = [
            pltpu.make_async_copy(source, copy, done.at[i])
            for i, (source, copy) in enumerate(zip(sources, copies))
        ]
        for move in moves:
            move.start()
        star_ref, stiff_ref, upwind_ref, state_ref, inv_ref, elem_ref, face_ref, proj_ref = copies
        for move in moves:
            move.wait()
        setup_kernel(
            own_ref, star_ref, stiff_ref, upwind_ref, inv_ref, dense_ref, scales_ref, table_ref
        )
        proj_k_ref[...] = jnp.zeros_like(proj_k_ref)
        for f in range(FACES):
            put_weights_k(proj_ref[:, f, :], f * FACE_PAD, proj_k_ref)
        elems = four_times(elem_ref[...])
        faces = four_times(face_ref[...])
        index = jnp.broadcast_to(elems, (MODES, CELLS))
        for q in range(QTY):
            v_ref[q * MODES : (q + 1) * MODES, :] = jnp.take_along_axis(
                state_ref[q], index, axis=1
            )
        spread = jnp.broadcast_to(inv_ref[...], (8, CELLS))
        inv = jnp.take_along_axis(spread, index[:8], axis=1)[0:1, :]
        section = (lane_ids(1) // SLOTS).astype(F32)
        substep = jnp.full((1, CELLS), dt_ref[0], F32) * (1.0 / SUBSTEPS)
        fill_coefs(coef_ref, section * substep, (section + 1.0) * substep)
        u_ref[...] = predict_five(dense_ref, v_ref, coef_ref, inv)

        def emit(q, value):
            flat_ref[:, lanes(q)] = value

        mix_upwind(table_ref, lambda q: u_ref[q * MODES : (q + 1) * MODES, :], emit)
        tiles = slot_faces(faces, proj_k_ref[...].astype(BF16), flat_ref, t_ref)
        pack_slots(tiles, 0, early_ref, 0)
        pack_slots(tiles, 1, early_ref, PACKED[0])
        for q in range(QTY):
            terms_ref[q * FACE_PAD : (q + 1) * FACE_PAD, :] = tiles[q]


def uniform_coefs(coef_ref, end):
    fill_coefs(coef_ref, jnp.zeros((1, CELLS), F32), jnp.full((1, CELLS), end, F32))


def first_kernel(
    own_ref, dt_ref, table_ref, state_ref, inv_ref, dense_ref,
    flat_ref, w_ref, u_ref, odd_ref, even_ref, v_ref, sum_ref, coef_ref,
):
    own = own_ref[0]
    for q in range(QTY):
        value = state_ref[q]
        v_ref[q * MODES : (q + 1) * MODES, :] = value
        flat_ref[:, lanes(q)] = value
    dt = dt_ref[0]
    uniform_coefs(coef_ref, jnp.where(own < FINE, dt * (1.0 / SUBSTEPS), dt))
    sum_ref[...] = predict_five(dense_ref, v_ref, coef_ref, inv_ref[...])

    def rows(q):
        return sum_ref[q * MODES : (q + 1) * MODES, :]

    def emit(q, value):
        u_ref[:, lanes(q)] = value

    mix_upwind(table_ref, rows, emit)
    put_messages(own % 2 == 0, lambda q: u_ref[:, lanes(q)], odd_ref, even_ref)
    for q in range(QTY):
        w_ref[:, lanes(q)] = rows(q)


def prep_kernel(
    own_ref, counts_ref, dense_ref, scales_ref, stiff_ref, proj_ref, lift_ref, index_ref, face_ref,
    elem_ref, slot_face_ref, terms_ref, square_ref, volume_ref, proj_k_ref, lift_m_ref,
    inside_ref, outside_ref, slots_ref, factor_ref, late_ref, k_ref, m_ref,
):
    own = own_ref[0]

    @pl.when(own < FINE)
    def _():
        whole = dense_ref[...]
        top, low = whole[:DENSE], whole[DENSE:]
        both = dot(whole, top)
        put_dense(both[:DENSE] + (both[DENSE:] + dot(top, low)), 0, square_ref)

    @pl.when(own >= FIRST_PARTNER)
    def _():
        tiles = [terms_ref[q * FACE_PAD : (q + 1) * FACE_PAD, :] for q in range(QTY)]
        pack_slots(tiles, 2, late_ref, 0)
        pack_slots(tiles, 3, late_ref, PACKED[0])

    k_ref[...] = jnp.zeros_like(k_ref)
    for f in range(FACES):
        put_weights_k(proj_ref[:, f, :], f * FACE_PAD, k_ref)
    proj_k_ref[...] = k_ref[...].astype(BF16)
    gap = jnp.zeros((MODES, 64 - MODES), F32)
    pad = jnp.zeros((FACE_PAD - FACE_MODES, MODES), F32)
    tall = jnp.zeros((CELLS - MODES, CELLS), F32)
    one = jnp.concatenate([stiff_ref[0], gap, stiff_ref[1], gap], axis=1)
    one = jnp.concatenate([one, tall], axis=0).T
    faces = [jnp.concatenate([lift_ref[:, f, :], pad], axis=0) for f in range(FACES)]
    faces = jnp.concatenate(faces + [jnp.zeros((CELLS - FACES * FACE_PAD, MODES), F32)], axis=0)
    third = jnp.concatenate([stiff_ref[2], jnp.zeros((CELLS - MODES, MODES), F32)], axis=0)
    side = jnp.zeros((CELLS, 64 - MODES), F32)
    two = jnp.concatenate([faces, side, third, side], axis=1).T
    build_dense(
        scales_ref, [one[:MODES], one[64 : 64 + MODES], two[64 : 64 + MODES]], volume_ref
    )
    value = two[:MODES, : FACES * FACE_PAD]
    hi = coarse_part(value)
    low = value - hi
    m_ref[...] = jnp.concatenate(
        [jnp.concatenate([hi, hi], axis=1), jnp.concatenate([low, low], axis=1)], axis=0
    )
    lift_m_ref[...] = m_ref[...].astype(BF16)
    nb, face = index_ref[...], face_ref[...] * CELLS
    inside = (nb >= HALF) & (nb < HALF + CELLS)
    lane = jnp.where(nb < HALF, nb + HALF, nb - HALF - CELLS)
    inside_ref[...] = pick_matrix(jnp.where(inside, face + nb - HALF, -1), FACES * CELLS)
    outside_ref[...] = pick_matrix(jnp.where(inside, -1, face + lane), FACES * CELLS)
    target = four_times(slot_face_ref[...] * CELLS + elem_ref[...])
    slots = slot_matrix(as_column(target), live_slots(own, counts_ref))
    slots_ref[...] = slots.astype(BF16)
    count = jnp.sum(slots, axis=0, keepdims=True) * 0.25
    factor_ref[...] = jnp.broadcast_to(1.0 + count, factor_ref.shape)


def inner_kernel(
    section, own_ref, state_ref, w_ref, u_ref, inv_ref, inside_ref, factor_ref,
    volume_ref, proj_ref, lift_ref, *rest,
):
    remote_ref, slots_ref = rest[:2]
    out_ref, t_ref = rest[0 if section == 0 else 3 if section == 1 else 2], rest[-1]
    own = own_ref[0]

    def work():
        apply_k(proj_ref[...], u_ref, t_ref, FACES * FACE_PAD)
        own_traces = by_quantity(t_ref)
        if section == 0:
            picked = pick_parts(own_traces, inside_ref[...])
        else:
            remote = unpack_slots(remote_ref, PACKED[0] if section != 2 else 0)
            matrix = jnp.concatenate([inside_ref[...], slots_ref[...]], axis=0)
            picked = pick_parts(jnp.concatenate([own_traces, remote], axis=1), matrix)
        rows = QTY * FACE_PAD
        jump = factor_ref[0:1, :] * own_traces - (picked[:rows] + picked[rows:])
        flux = lift(lift_ref[...], two_parts(by_face(jump)))
        rows = jnp.concatenate([w_ref[:, lanes(q)] for q in range(QTY)], axis=0)
        volume = dense(volume_ref, rows)
        inv = inv_ref[...]
        for q in range(QTY):
            change = block(volume, q) - flux[:, lanes(q)]
            out_ref[:, lanes(q)] = state_ref[:, lanes(q)] + inv * change

    if section == 0:
        work()
    else:
        pl.when(own < FINE)(work)


def halo_lift(
    own, odd_in, even_in, outside_ref, proj_ref, lift_w, halo_ref, t_ref, extra=None
):
    take_messages(own % 2 == 0, odd_in, even_in, halo_ref)
    apply_k(proj_ref[...], halo_ref, t_ref, FACES * FACE_PAD)
    source, matrix = by_quantity(t_ref), outside_ref[...]
    if extra is None:
        return lift(lift_w, stack_parts(pick_parts(source, matrix)))
    source = jnp.concatenate([source, extra[0]], axis=1)
    matrix = jnp.concatenate([matrix, extra[1]], axis=0)
    return lift(lift_w, stack_sums(pick_parts(source, matrix)))


def outer_kernel(
    section, own_ref, dt_ref, table_ref, state_ref, odd_in, even_in, inv_ref, outside_ref,
    proj_ref, lift_ref, dense_ref, square_ref, sum_in, *rest,
):
    flat_ref, w_ref, u_ref, odd_ref, even_ref, sum_ref, halo_ref, t_ref, coef_ref = rest[-9:]
    own = own_ref[0]

    def update():
        extra = None
        if section == 0:
            remote_ref, slots_ref = rest[:2]
            extra = (unpack_slots(remote_ref), slots_ref[...])
        gain = halo_lift(
            own, odd_in, even_in, outside_ref, proj_ref, lift_ref[...], halo_ref, t_ref, extra
        )
        inv = inv_ref[...]
        for q in range(QTY):
            flat_ref[:, lanes(q)] = state_ref[:, lanes(q)] + inv * gain[:, lanes(q)]

    if section == 0:
        update()

    @pl.when(own < FINE)
    def _():
        if section > 0:
            update()
        uniform_coefs(coef_ref, dt_ref[0] * (1.0 / SUBSTEPS))
        rows = jnp.concatenate([flat_ref[:, lanes(q)] for q in range(QTY)], axis=0)
        w = predict_three(dense_ref, square_ref, rows, coef_ref, inv_ref[...])
        for q in range(QTY):
            w_ref[:, lanes(q)] = block(w, q)
        if section == SUBSTEPS - 2:
            elem_ref, slot_face_ref = rest[:2]
            index = jnp.broadcast_to(four_times(elem_ref[...]), (MODES, CELLS))

        def emit(q, value):
            u_ref[:, lanes(q)] = value
            total = sum_in[:, lanes(q)] + value
            if section < SUBSTEPS - 2:
                sum_ref[:, lanes(q)] = total
            else:
                halo_ref[:, lanes(q)] = jnp.take_along_axis(total, index, axis=1)

        mix_upwind(table_ref, lambda q: w_ref[:, lanes(q)], emit)
        put_messages(own % 2 == 0, lambda q: u_ref[:, lanes(q)], odd_ref, even_ref)
        if section == SUBSTEPS - 2:
            faces = four_times(slot_face_ref[...])
            pack_slots(slot_faces(faces, proj_ref[...], halo_ref, t_ref), None, sum_ref, 0)


def last_kernel(
    own_ref, fine_ref, coarse_ref, odd_in, even_in, inv_ref, outside_ref, proj_ref,
    lift_ref, up_ref, slots_ref, out_ref, halo_ref, t_ref, rows_ref, done,
):
    own = own_ref[0]
    inv = inv_ref[...]

    def write(base_ref, stacked):
        moves = []
        for start in range(0, QTY, 2):
            count = min(2, QTY - start)
            gain = lift(lift_ref[...], stacked[:, lanes(start, count)])
            for q in range(start, start + count):
                part = gain[:, lanes(q - start)]
                rows_ref[q] = base_ref[:, lanes(q)] + inv * part
                moves.append(
                    pltpu.make_async_copy(rows_ref.at[q], out_ref.at[q], done.at[q])
                )
                moves[q].start()
        for move in moves:
            move.wait()

    @pl.when(own < FINE)
    def _():
        take_messages(own % 2 == 0, odd_in, even_in, halo_ref)
        apply_k(proj_ref[...], halo_ref, t_ref, FACES * FACE_PAD)
        picked = pick_parts(by_quantity(t_ref), outside_ref[...])
        write(fine_ref, stack_parts(picked))

    @pl.when(own >= FINE)
    def _():
        picked = pick_parts(unpack_slots(up_ref), slots_ref[...])
        write(coarse_ref, stack_sums(picked))


S = pl.BlockSpec(memory_space=pltpu.SMEM)
V = pl.BlockSpec(memory_space=pltpu.VMEM)
H = pl.BlockSpec(memory_space=pltpu.HBM)
FIELD = (MODES, WIDTH)
ROWS = (QTY * MODES, CELLS)
MESSAGE = (256, CELLS)


def call(kernel, inputs, outs, scratch, operands, flops, name, aliases=None, place=None, scalars=2, out_place=V):
    shapes = [
        jax.ShapeDtypeStruct(o, F32) if isinstance(o, tuple) else o for o in outs
    ]
    return pl.pallas_call(
        kernel,
        in_specs=[S] * scalars + [place or V] * (inputs - scalars),
        out_specs=[out_place] * len(outs),
        out_shape=shapes,
        scratch_shapes=[
            pltpu.VMEM(s, F32) if isinstance(s, tuple) else s for s in scratch
        ],
        input_output_aliases=aliases or {},
        compiler_params=pltpu.CompilerParams(vmem_limit_bytes=16 * 1024 * 1024),
        cost_estimate=pl.CostEstimate(
            flops=flops, bytes_accessed=2_000_000, transcendentals=0
        ),
        name=name,
    )(*operands)


def half(*shape):
    return jax.ShapeDtypeStruct(shape, BF16)


def shards(
    modal_state, inv_size, time_step, stiffness, star_matrices, projection, lifting, upwind,
    nb_index, nb_face, iface_elem, iface_face, iface_counts,
):
    own = lax.axis_index("dom").astype(jnp.int32).reshape(1)
    state = modal_state.transpose(1, 0, 2)
    star = star_matrices.transpose(1, 0, 2)
    proj = projection.transpose(1, 0, 2)
    lift_w = lifting.transpose(2, 0, 1)
    dt = time_step.reshape(1)
    inv = inv_size.reshape(1, CELLS)
    elems = iface_elem.reshape(1, SLOTS)
    faces = iface_face.reshape(1, SLOTS)
    counts = iface_counts.reshape(2, CELLS)

    count = lax.axis_size("dom")
    down = [(i + FIRST_PARTNER, i) for i in range(FINE)]
    up = [(i, i + FIRST_PARTNER) for i in range(FINE)]

    def swaps(first, last):
        pairs = [(i, i + 1) for i in range(first, last, 2)]
        pairs = [p for p in pairs if p[1] < last]
        return pairs + [(b, a) for a, b in pairs]

    odd_fine, even_fine = swaps(1, FINE), swaps(0, FINE)
    odd_all = odd_fine + swaps(FINE, count)
    even_all = even_fine + swaps(FINE + 1, count)

    coef = (8, CELLS)
    t_rows = FACES * FACE_PAD
    t_shape = (t_rows, WIDTH)
    wide_operator = (2 * DENSE, DENSE)
    columns = FACES * CELLS

    loaded = (star, stiffness, upwind, state, inv, elems, faces, proj)
    tables = [half(*wide_operator), (48, DENSE), (QTY * 16, CELLS)]
    early, terms = call(
        remote_kernel,
        2 + LOADED,
        [(2 * PACKED[0], CELLS), (QTY * FACE_PAD, CELLS)],
        [pltpu.VMEM(x.shape, x.dtype) for x in loaded]
        + [pltpu.VMEM(wide_operator, BF16), (48, DENSE), (QTY * 16, CELLS)]
        + [FIELD, ROWS, ROWS, t_shape, coef, (t_rows, 192),
           pltpu.SemaphoreType.DMA((LOADED,))],
        (own, dt, *(pltpu.with_memory_space_constraint(x, pltpu.HBM) for x in loaded)),
        20_000_000,
        "remote",
        place=H,
    )
    early = lax.ppermute(early, "dom", down)
    dense_op, scales, table = call(
        setup_kernel, 5, tables, [], (own, star, stiffness, upwind, inv), 20_000_000, "setup",
        scalars=1,
    )

    flat, w, u, odd, even = call(
        first_kernel,
        6,
        [FIELD, FIELD, FIELD, MESSAGE, MESSAGE],
        [ROWS, ROWS, coef],
        (own, dt, table, state, inv, dense_op),
        2_000_000_000,
        "first",
    )
    total = u
    coarse = None
    for section in range(SUBSTEPS):
        odd_in = lax.ppermute(odd, "dom", odd_all if section == 0 else odd_fine)
        even_in = lax.ppermute(even, "dom", even_all if section == 0 else even_fine)
        if section == 0:
            (
                square_op, volume, proj_k, lift_m, inside, outside, slots, factor,
                late,
            ) = call(
                prep_kernel,
                12,
                [
                    half(*wide_operator), half(*wide_operator), half(t_rows, 192),
                    half(2 * MODES, 2 * t_rows), half(columns, columns),
                    half(columns, columns), half(CELLS, columns), (8, columns),
                    (2 * PACKED[0], CELLS),
                ],
                [(t_rows, 192), (2 * MODES, 2 * t_rows)],
                (own, counts, dense_op, scales, stiffness, proj, lift_w, nb_index, nb_face,
                 elems, faces, terms),
                2_000_000_000,
                "prep",
                scalars=1,
            )
        if section == SUBSTEPS - 1:
            arrived = lax.ppermute(total, "dom", up)
        passed = section == 1
        extra = (() if section == 0 else (early if section == 1 else late, slots))
        results = call(
            functools.partial(inner_kernel, section),
            10 + len(extra) + passed,
            [FIELD] + [(2 * PACKED[0], CELLS)] * passed,
            [t_shape],
            (own, flat, w, u, inv, inside, factor, volume, proj_k, lift_m)
            + extra + (late,) * passed,
            2_000_000_000,
            f"inner{section}",
            {12: 1} if passed else None,
            scalars=1,
        )
        inner = results[0]
        if passed:
            late = lax.ppermute(results[1], "dom", down)
        if section == SUBSTEPS - 1:
            break
        extra = ((early, slots), (), (elems, faces))[section]
        flat, w, u, odd, even, total = call(
            functools.partial(outer_kernel, section),
            13 + len(extra),
            [FIELD, FIELD, FIELD, MESSAGE, MESSAGE,
             FIELD if section < SUBSTEPS - 2 else PACKED],
            [FIELD, t_shape, coef],
            (own, dt, table, inner, odd_in, even_in, inv, outside, proj_k, lift_m, dense_op,
             square_op, total) + extra,
            2_000_000_000,
            f"outer{section}",
        )
        if section == 0:
            coarse = flat
    (out,) = call(
        last_kernel,
        11,
        [pltpu.HBM((QTY, MODES, CELLS), F32)],
        [FIELD, t_shape, (QTY, MODES, CELLS), pltpu.SemaphoreType.DMA((QTY,))],
        (own, inner, coarse, odd_in, even_in, inv, outside, proj_k, lift_m, arrived, slots),
        1_000_000_000,
        "last",
        scalars=1,
        out_place=H,
    )
    return out.transpose(1, 0, 2)


def solution(mesh):
    return jax.shard_map(
        shards,
        mesh=mesh,
        in_specs=(
            P(None, None, "dom"),
            P("dom"),
            P(),
            P(),
            P(),
            P(),
            P(),
            P(),
            P(None, "dom"),
            P(None, "dom"),
            P("dom"),
            P("dom"),
            P(),
        ),
        out_specs=P(None, None, "dom"),
        check_vma=False,
    )
```
